32 devices in a mesh: seq: 4 (over y, x), batch: 8 (over z, core).
Axes of the slice: x: 2, y: 2, z: 4, core: 2. Of those that a mesh axis runs over, the one named last changes fastest.
Arguments:
- inputs: bfloat16 [24, 896, 768], P('batch', 'seq'), may hold values from -6 to 6
- lengths: int32 [24], P('batch'), may hold values from 672 to 896, as said below
- gain_one: bfloat16 [768], replicated, may hold values from 0.5 to 1.5
- shift_one: bfloat16 [768], replicated, may hold values from -1.5 to 1.5
- w_query: bfloat16 [768, 768], replicated, may hold values from -0.4375 to 0.4375
- b_query: bfloat16 [768], replicated, may hold values from -1.5 to 1.5
- w_key: bfloat16 [768, 768], replicated, may hold values from -0.21875 to 0.21875
- w_value: bfloat16 [768, 768], replicated, may hold values from -0.21875 to 0.21875
- b_value: bfloat16 [768], replicated, may hold values from -1.5 to 1.5
- w_out: bfloat16 [768, 768], replicated, may hold values from -0.875 to 0.875
- b_out: bfloat16 [768], replicated, may hold values from -1.5 to 1.5
- gain_two: bfloat16 [768], replicated, may hold values from 0.5 to 1.5
- shift_two: bfloat16 [768], replicated, may hold values from -1.5 to 1.5
- w_up: bfloat16 [768, 3072], replicated, may hold values from -0.21875 to 0.21875
- b_up: bfloat16 [3072], replicated, may hold values from -1.5 to 1.5
- w_down: bfloat16 [3072, 768], replicated, may hold values from -0.109375 to 0.109375
- b_down: bfloat16 [768], replicated, may hold values from -1.5 to 1.5
- cotangent: bfloat16 [24, 896, 768], P('batch', 'seq'), may hold values from -6 to 6
Outputs:
- outputs: bfloat16 [24, 896, 768], P('batch', 'seq')
- input_grad: bfloat16 [24, 896, 768], P('batch', 'seq')
- grad_gain_one: float32 [768], P('batch')
- grad_shift_one: float32 [768], P('batch')
- grad_w_query: float32 [768, 768], P('batch')
- grad_b_query: float32 [768], P('batch')
- grad_w_key: float32 [768, 768], P('batch')
- grad_w_value: float32 [768, 768], P('batch')
- grad_b_value: float32 [768], P('batch')
- grad_w_out: float32 [768, 768], P('batch')
- grad_b_out: float32 [768], P('batch')
- grad_gain_two: float32 [768], P('batch')
- grad_shift_two: float32 [768], P('batch')
- grad_w_up: float32 [768, 3072], P('batch')
- grad_b_up: float32 [3072], P('batch')
- grad_w_down: float32 [3072, 768], P('batch')
- grad_b_down: float32 [768], P('batch')
The draws below stay inside these ranges and needn't reach their ends.
Inputs may be any that keep to these rules, and one draw needn't show every extreme that they name: Rows 0 to lengths - 1 of a sequence are valid keys; in each aligned block of 3 sequences one has length 896.
All inputs are finite; a program needn't handle non-finite values.
Results may differ from the reference program's by a relative error of at most 0.022.
Values may be sent and summed in bfloat16 or wider, within the bound.
A program may use at most 256 MiB of HBM per device.

```python
from functools import partial
import jax
import jax.numpy as jnp
from jax import lax

D = 768
FF = 3072
HEADS = 12
HEAD_DIM = 64
SEQ_LEN = 896
SEQS_DEV = 3
SEQS = 24


def draw_lengths(key, part):
    key = jax.random.fold_in(key, 7)
    base_key, pick_key = jax.random.split(key)
    drawn_lengths = jax.random.randint(base_key, (SEQS,), SEQ_LEN * 3 // 4, SEQ_LEN + 1, dtype=jnp.int32)
    chosen_slot = jax.random.randint(pick_key, (SEQS // SEQS_DEV, 1), 0, SEQS_DEV, dtype=jnp.int32)
    slot_index = jnp.arange(SEQS, dtype=jnp.int32).reshape(SEQS // SEQS_DEV, SEQS_DEV) % SEQS_DEV
    full_slot = (slot_index == chosen_slot).reshape(SEQS)
    return jnp.where(full_slot, SEQ_LEN, drawn_lengths).astype(jnp.int32)


def block_levels(rng, shape, cuts, least, top_value):
    def one(position, blocks):
        steps = jax.random.uniform(jax.random.fold_in(jax.random.fold_in(rng, 6), position), (blocks,), jnp.float32, least / len(cuts), top_value / len(cuts))
        return jnp.repeat(jnp.exp(steps), shape[position] // blocks).reshape((-1,) + (1,) * (len(shape) - position - 1))

    loudness = one(*cuts[0])
    for cut in cuts[1:]:
        loudness = loudness * one(*cut)
    return loudness


def bell_draw(rng, dims, deviation, most, cuts=(), kind=jnp.bfloat16):
    array = deviation * jax.random.normal(rng, dims, jnp.float32)
    if cuts:
        array = array * block_levels(rng, dims, cuts, -0.22, 0.18)
    return jnp.clip(array, -most, most).astype(kind)


def setup_inputs(seed: int = 0) -> dict:
    key_of = jax.random.split(jax.random.key(seed), 19)
    inputs = bell_draw(key_of[0], (SEQS, SEQ_LEN, D), 1.0, 6.0, ((0, 8), (1, 4)))
    lengths = draw_lengths(jax.random.fold_in(key_of[18], 71), 0)
    gain_one = jnp.clip(1.0 + 0.1 * jax.random.normal(key_of[2], (D,), jnp.float32), 0.5, 1.5).astype(jnp.bfloat16)
    shift_one = bell_draw(key_of[3], (D,), 0.3, 1.5)
    w_query = bell_draw(key_of[4], (D, D), (D // 4) ** -0.5, 0.4375)
    b_query = bell_draw(key_of[5], (D,), 0.3, 1.5)
    w_key = bell_draw(key_of[6], (D, D), D ** -0.5, 0.21875)
    w_value = bell_draw(key_of[7], (D, D), D ** -0.5, 0.21875)
    b_value = bell_draw(key_of[8], (D,), 0.3, 1.5)
    w_out = bell_draw(key_of[9], (D, D), (D // 16) ** -0.5, 0.875)
    b_out = bell_draw(key_of[10], (D,), 0.3, 1.5)
    gain_two = jnp.clip(1.0 + 0.1 * jax.random.normal(key_of[11], (D,), jnp.float32), 0.5, 1.5).astype(jnp.bfloat16)
    shift_two = bell_draw(key_of[12], (D,), 0.3, 1.5)
    w_up = bell_draw(key_of[13], (D, FF), D ** -0.5, 0.21875)
    b_up = bell_draw(key_of[14], (FF,), 0.3, 1.5)
    w_down = bell_draw(key_of[15], (FF, D), FF ** -0.5, 0.109375)
    b_down = bell_draw(key_of[16], (D,), 0.3, 1.5)
    cotangent = bell_draw(key_of[17], (SEQS, SEQ_LEN, D), 1.0, 6.0, ((0, 8), (1, 4)))
    return {"inputs": inputs, "lengths": lengths, "gain_one": gain_one, "shift_one": shift_one, "w_query": w_query, "b_query": b_query, "w_key": w_key, "w_value": w_value, "b_value": b_value, "w_out": w_out, "b_out": b_out, "gain_two": gain_two, "shift_two": shift_two, "w_up": w_up, "b_up": b_up, "w_down": w_down, "b_down": b_down, "cotangent": cotangent}


@jax.custom_vjp
def low(v):
    return lax.optimization_barrier(v.astype(jnp.bfloat16)).astype(jnp.float32)

@jax.custom_vjp
def low_back(v):
    return v

def low_keep(v):
    return (low(v), None)

def low_pass(kept, grad):
    return (grad,)

def back_keep(v):
    return (v, None)

def back_low(kept, grad):
    return (low(grad),)
low.defvjp(low_keep, low_pass)
low_back.defvjp(back_keep, back_low)
norm_eps = 1e-05
masked_score = -1e+30

def product(left, right):
    return jnp.dot(left, right, precision=lax.Precision.HIGHEST)

def normed(values, gain, offset):
    average = lax.optimization_barrier(jnp.mean(values, axis=-1, keepdims=True))
    centred = values - average
    spread = lax.optimization_barrier(jnp.mean(centred * centred, axis=-1, keepdims=True))
    return centred * lax.rsqrt(spread + norm_eps) * gain + offset

def layer_one(params, pieces):
    seq_rows, seq_length = pieces
    gain_one, shift_one, w_query, b_query, w_key, w_value, b_value, w_out, b_out, gain_two, shift_two, w_up, b_up, w_down, b_down = params
    first = low(normed(seq_rows, gain_one, shift_one))
    queries = low_back(low(product(first, w_query) + b_query)).reshape(SEQ_LEN, HEADS, HEAD_DIM)
    key_rows = low_back(low(product(first, w_key))).reshape(SEQ_LEN, HEADS, HEAD_DIM)
    value_rows = low_back(low(product(first, w_value) + b_value)).reshape(SEQ_LEN, HEADS, HEAD_DIM)
    scores = low_back(jnp.einsum('qhd,khd->hqk', queries, key_rows, precision=lax.Precision.HIGHEST) * HEAD_DIM ** (-0.5))
    valid = (jnp.arange(SEQ_LEN, dtype=jnp.int32) < seq_length)[None, None, :]
    scores = jnp.where(valid, scores, masked_score)
    row_max = lax.optimization_barrier(jnp.max(scores, axis=-1, keepdims=True))
    weights_exp = jnp.exp(scores - row_max)
    row_total = lax.optimization_barrier(jnp.sum(weights_exp, axis=-1, keepdims=True))
    attended = jnp.einsum('hqk,khd->hqd', low(weights_exp), value_rows, precision=lax.Precision.HIGHEST) / row_total
    attended = low_back(low(jnp.transpose(attended, (1, 0, 2)).reshape(SEQ_LEN, D)))
    middle = seq_rows + low_back(product(attended, w_out) + b_out)
    second = low(normed(middle, gain_two, shift_two))
    hidden = low_back(product(second, w_up) + b_up)
    active = low(jax.nn.gelu(hidden))
    return middle + low_back(product(active, w_down) + b_down)

def reference(inputs, lengths, gain_one, shift_one, w_query, b_query, w_key, w_value, b_value, w_out, b_out, gain_two, shift_two, w_up, b_up, w_down, b_down, cotangent):
    params = tuple((item.astype(jnp.float32) for item in (gain_one, shift_one, w_query, b_query, w_key, w_value, b_value, w_out, b_out, gain_two, shift_two, w_up, b_up, w_down, b_down)))
    rows_in = inputs.astype(jnp.float32)

    def forward(rows_all, weights_all):
        return lax.map(jax.checkpoint(partial(layer_one, weights_all)), (rows_all, lengths))
    outputs, pullback = jax.vjp(forward, rows_in, params)
    input_grad, grads = pullback(cotangent.astype(jnp.float32))
    return (outputs.astype(jnp.bfloat16), input_grad.astype(jnp.bfloat16), grads[0], grads[1], grads[2], grads[3], grads[4], grads[5], grads[6], grads[7], grads[8], grads[9], grads[10], grads[11], grads[12], grads[13], grads[14])
```

```python
import functools
import math

import jax
import jax.numpy as jnp
from jax import lax
from jax.experimental import pallas as pl
from jax.experimental.pallas import tpu as pltpu
from jax.sharding import PartitionSpec as P

HEAD_DIM = 64
norm_eps = 1e-05
masked_score = -1e30

bf16 = jnp.bfloat16
f32 = jnp.float32
MESH = pl.DeviceIdType.MESH
ANY = pl.BlockSpec(memory_space=pl.ANY)
VM = pl.BlockSpec(memory_space=pltpu.VMEM)
SM = pl.BlockSpec(memory_space=pltpu.SMEM)
NN = (((1,), (0,)), ((), ()))
NT = (((1,), (1,)), ((), ()))
TN = (((0,), (0,)), ((), ()))
LOG2E = math.log2(math.e)
GC0 = math.sqrt(2.0 / math.pi)
GC1 = GC0 * 0.044715


def dg(a, b, dims):
    return lax.dot_general(a, b, dims, preferred_element_type=f32)


def al(i, m=16):
    return pl.multiple_of(i, m)


def places():
    s = lax.axis_index("seq")
    b = lax.axis_index("batch")
    y, x = s // 2, s % 2
    return s, b, y * 2 + (1 - x), (1 - y) * 2 + x, (1 - y) * 2 + (1 - x)


def row_norm(x):
    mean = jnp.mean(x, axis=-1, keepdims=True)
    c = x - mean
    r = lax.rsqrt(jnp.mean(c * c, axis=-1, keepdims=True) + norm_eps)
    return c * r, r


def attend_kernel(
    C, R, D, S,
    x_h, len_s, vec, wq_h, wk_h, wv_h,
    n1_h, q_h, k_h, v_h, a_h, li_h, e_h,
    x_v, n1, wq, wk, wv, q_v, k_v, v_v, a_v, li_v, e_v, s_v,
    lsem, osem, esem, sx, sy, rx, ry, sdx, sdy, rdx, rdy,
):
    T = R * S
    HR = R // 2
    pairs = D // 128
    s, b, px, py, pd = places()
    bar = pltpu.get_barrier_semaphore()
    for o in (px, py):
        pl.semaphore_signal(bar, 1, device_id=(o, b), device_id_type=MESH)
    xc = [
        pltpu.make_async_copy(
            x_h.at[pl.ds(i * R, R)], x_v.at[pl.ds(i * R, R)], lsem.at[i]
        )
        for i in range(C)
    ]
    for c in xc:
        c.start()
    wc = [
        pltpu.make_async_copy(h, v, lsem.at[C + i])
        for i, (h, v) in enumerate(((wk_h, wk), (wv_h, wv), (wq_h, wq)))
    ]
    for c in wc:
        c.start()

    def rows(q, blk, off, n):
        return pl.ds(al((q * S + blk) * R + off), n)

    def own_copy(q, peer, ss, rs):
        ref = n1.at[rows(q, s, 0, R)]
        return pltpu.make_async_remote_copy(
            ref, ref, ss.at[q], rs.at[q], device_id=(peer, b), device_id_type=MESH
        )

    def relay_copy(q, peer, blk, off, ss, rs):
        ref = n1.at[rows(q, blk, off, HR)]
        return pltpu.make_async_remote_copy(
            ref, ref, ss.at[q], rs.at[q], device_id=(peer, b), device_id_type=MESH
        )

    own = [(own_copy(q, px, sx, rx), own_copy(q, py, sy, ry)) for q in range(C)]
    rel = [
        (relay_copy(q, py, px, 0, sdy, rdy), relay_copy(q, px, py, HR, sdx, rdx))
        for q in range(C)
    ]

    gain, shift = vec[0:1, :], vec[1:2, :]
    bq, bv = vec[2:3, :], vec[3:4, :]
    for q in range(C):
        xc[q].wait()
        z, _ = row_norm(x_v[q * R : (q + 1) * R, :].astype(f32))
        n1[rows(q, s, 0, R), :] = (z * gain + shift).astype(bf16)
        if q == 0:
            pl.semaphore_wait(bar, 2)
        if q < 2:
            for c in own[q]:
                c.start()
    for c in wc:
        c.wait()

    def kv(q, blk):
        rs = rows(q, blk, 0, R)
        v = n1[rs, :]
        k_v[rs, :] = dg(v, wk[...], NN).astype(bf16)
        v_v[rs, :] = (dg(v, wv[...], NN) + bv).astype(bf16)

    def own_rows(q, _):
        v = n1[rows(q, s, 0, R), :]
        q_v[pl.ds(al(q * R), R), :] = (
            (dg(v, wq[...], NN) + bq) * (HEAD_DIM ** (-0.5) * LOG2E)
        ).astype(bf16)
        kv(q, s)
        return 0

    lax.fori_loop(0, C, own_rows, 0)
    qc = pltpu.make_async_copy(q_v, q_h, osem.at[0])
    qc.start()

    def arrived(q):
        for c in own[q]:
            c.wait_recv()
        for c in rel[q]:
            c.start()

    def near(q):
        lax.fori_loop(0, 2, lambda i, c: (kv(q, jnp.where(i == 0, px, py)), c)[1], 0)

    def far(q):
        for c in rel[q]:
            c.wait_recv()
        kv(q, pd)
        for i, (v, h) in enumerate(((n1, n1_h), (k_v, k_h), (v_v, v_h))):
            pltpu.make_async_copy(
                v.at[pl.ds(q * T, T)], h.at[pl.ds(q * T, T)], osem.at[3 + 3 * q + i]
            ).start()

    arrived(0)
    for c in own[2]:
        c.start()
    near(0)
    arrived(1)
    near(1)
    far(0)

    lane = lax.broadcasted_iota(jnp.int32, (1, 128), 1)
    lo = lane < 64
    col = lax.broadcasted_iota(jnp.int32, (1, T), 1)

    def e_copy(t):
        return pltpu.make_async_copy(e_v.at[t % 2], e_h.at[t], esem.at[t % 2])

    def pair(t, _):
        q, p = t // pairs, t % pairs

        @pl.when(t == pairs // 2)
        def _():
            arrived(2)
            near(2)

        for i in range(1, C):

            @pl.when(t == i * pairs)
            def _():
                far(i)

        off = al(p * 128, 128)
        rq = pl.ds(al(q * R), R)
        rk = pl.ds(al(q * T), T)
        qp = q_v[rq, pl.ds(off, 128)]
        zero = jnp.zeros_like(qp)
        qs = jnp.concatenate([jnp.where(lo, qp, zero), jnp.where(lo, zero, qp)], 0)
        bias = jnp.where(col < len_s[q], 0.0, masked_score).astype(f32)
        s_v[...] = dg(qs, k_v[rk, pl.ds(off, 128)], NT) + bias
        m = jnp.max(s_v[...], axis=1, keepdims=True)
        e = jnp.exp2(s_v[...] - m)
        eb = e.astype(bf16)
        tot = jnp.sum(e, axis=1, keepdims=True)

        @pl.when(t >= 2)
        def _():
            e_copy(t - 2).wait()

        e_v[t % 2] = eb
        e_copy(t).start()
        ol = dg(eb, v_v[rk, pl.ds(off, 128)], NN)
        inv = 1.0 / tot
        inv = jnp.where(lo, inv[:R], inv[R:])
        li_v[rq, pl.ds(off, 128)] = inv
        a_v[rq, pl.ds(off, 128)] = (jnp.where(lo, ol[:R], ol[R:]) * inv).astype(bf16)
        return 0

    lax.fori_loop(0, C * pairs, pair, 0)
    ac = pltpu.make_async_copy(a_v, a_h, osem.at[1])
    lc = pltpu.make_async_copy(li_v, li_h, osem.at[2])
    ac.start()
    lc.start()
    e_copy(C * pairs - 2).wait()
    e_copy(C * pairs - 1).wait()
    for q in range(C):
        for i, (v, h) in enumerate(((n1, n1_h), (k_v, k_h), (v_v, v_h))):
            pltpu.make_async_copy(
                v.at[pl.ds(q * T, T)], h.at[pl.ds(q * T, T)], osem.at[3 + 3 * q + i]
            ).wait()
        for c in own[q] + rel[q]:
            c.wait_send()
    qc.wait()
    ac.wait()
    lc.wait()


def attend(C, R, D, S, x, lengths, vec, wq, wk, wv):
    N, T, pairs = C * R, R * S, D // 128
    sd = jax.ShapeDtypeStruct
    dma = pltpu.SemaphoreType.DMA
    return pl.pallas_call(
        functools.partial(attend_kernel, C, R, D, S),
        out_shape=(
            sd((C * T, D), bf16),
            sd((N, D), bf16),
            sd((C * T, D), bf16),
            sd((C * T, D), bf16),
            sd((N, D), bf16),
            sd((N, D), f32),
            sd((C * pairs, 2 * R, T), bf16),
        ),
        in_specs=[ANY, SM, VM, ANY, ANY, ANY],
        out_specs=(ANY,) * 7,
        scratch_shapes=[
            pltpu.VMEM((N, D), bf16),
            pltpu.VMEM((C * T, D), bf16),
            pltpu.VMEM((D, D), bf16),
            pltpu.VMEM((D, D), bf16),
            pltpu.VMEM((D, D), bf16),
            pltpu.VMEM((N, D), bf16),
            pltpu.VMEM((C * T, D), bf16),
            pltpu.VMEM((C * T, D), bf16),
            pltpu.VMEM((N, D), bf16),
            pltpu.VMEM((N, D), f32),
            pltpu.VMEM((2, 2 * R, T), bf16),
            pltpu.VMEM((2 * R, T), f32),
            dma((C + 3,)),
            dma((3 + 3 * C,)),
            dma((2,)),
        ]
        + [dma((C,))] * 8,
        compiler_params=pltpu.CompilerParams(
            collective_id=1, has_side_effects=True, vmem_limit_bytes=60 * 2**20
        ),
        cost_estimate=pl.CostEstimate(
            flops=20 * 10**9, bytes_accessed=40 * 10**6, transcendentals=0
        ),
    )(x, lengths, vec, wq, wk, wv)


def backward_kernel(
    C, R, D, S, FF,
    x_h, cot_h, a_h, li_h, q_h, k_h, v_h, n1_h, e_h, vec, bup, wo_h, wu_h, wd_h, wq_h, wk_h, wv_h,
    out_h, dh_h, g_h, dn_h, sm_h,
    x_v, cot, a_v, q_v, n2, pb, du, h_v, acc, dn2, kk, vv, n1, wq, wk, wv, wo, gb, dn, e_v, sm, lsem, esem, osem,
):
    T, N = R * S, C * R
    pairs = D // 128
    J = FF // D
    B = 8
    CH = D // B
    s, b, px, py, pd = places()
    t_rows = C * T

    def load(i, h, v):
        c = pltpu.make_async_copy(h, v, lsem.at[i])
        c.start()
        return c

    c_a = load(0, a_h, a_v)
    c_wo = load(1, wo_h, wo)
    c_x = load(2, x_h, x_v)
    c_cot = load(3, cot_h, cot)
    c_w = [
        (
            load(4 + 2 * j, wu_h.at[:, pl.ds(j * D, D)], vv.at[pl.ds(j * D, D)]),
            load(5 + 2 * j, wd_h.at[pl.ds(j * D, D)], kk.at[pl.ds(j * D, D)]),
        )
        for j in range(J)
    ]
    n0 = 4 + 2 * J
    c_q = load(n0, q_h, q_v)
    c_n1 = load(n0 + 1, n1_h, n1)
    c_wk = load(n0 + 2, wk_h, wk)
    c_wv = load(n0 + 3, wv_h, wv)
    c_wq = load(n0 + 4, wq_h, wq)

    def e_copy(t, slot):
        return pltpu.make_async_copy(e_h.at[t], e_v.at[slot], esem.at[slot])

    e_copy(0, 0).start()
    e_copy(1, 1).start()

    gain1, shift1 = vec[0:1, :], vec[1:2, :]
    b_out, gain2, shift2, b_down = vec[4:5, :], vec[5:6, :], vec[6:7, :], vec[7:8, :]
    sm[...] = jnp.zeros_like(sm)
    for c in (c_a, c_wo, c_x, c_cot):
        c.wait()

    def first(i, _):
        r = pl.ds(al(i * R), R)
        h = x_v[r, :].astype(f32) + dg(a_v[r, :], wo[...], NN) + b_out
        h_v[r, :] = h
        z, _r = row_norm(h)
        n2[r, :] = (z * gain2 + shift2).astype(bf16)
        acc[r, :] = h + b_down
        dn2[r, :] = jnp.zeros((R, D), f32)
        sm[7:8, :] += jnp.sum(cot[r, :].astype(f32), axis=0, keepdims=True)
        return 0

    lax.fori_loop(0, C, first, 0)

    def ffn(j, _):
        jr = pl.ds(al(j * D), D)
        for jj in range(J):

            @pl.when(j == jj)
            def _():
                c_w[jj][0].wait()
                c_w[jj][1].wait()

        bias = bup[pl.ds(j, 1), :]

        def chunk(i, sums):
            r = pl.ds(al(i * R), R)
            u = dg(n2[r, :], vv[jr, :], NN) + bias
            g = dg(cot[r, :], kk[jr, :], NT)
            u2 = u * u
            t = jnp.tanh(u * (GC0 + GC1 * u2))
            hu = 0.5 * u
            half = 0.5 + 0.5 * t
            p = (u * half).astype(bf16)
            d = (g * (half + hu * (1.0 - t * t) * (GC0 + 3.0 * GC1 * u2))).astype(bf16)
            pb[r, :] = p
            du[r, :] = d
            acc[r, :] += dg(p, kk[jr, :], NN)
            dn2[r, :] += dg(d, vv[jr, :], NT)
            return sums + jnp.sum(d.astype(f32), axis=0, keepdims=True)

        sm[pl.ds(8 + j, 1), :] = lax.fori_loop(0, C, chunk, jnp.zeros((1, D), f32))
        gb[j] = dg(n2[...], du[...], TN).astype(bf16).reshape(B // 2, 2, CH, D)
        gw = dg(pb[...], cot[...], TN).astype(bf16)
        per = FF // B
        for bb in range(D // per):
            for i in range(per // CH):
                o = bb * per + i * CH
                gb[J + i, j, bb] = gw[o : o + CH, :]
        return 0

    lax.fori_loop(0, J, ffn, 0)

    c_k = load(0, k_h, kk.at[pl.ds(0, t_rows)])
    c_v = load(1, v_h, vv.at[pl.ds(0, t_rows)])

    def second(i, _):
        r = pl.ds(al(i * R), R)
        pb[r, :] = acc[r, :].astype(bf16)
        z, rr = row_norm(h_v[r, :])
        dn = dn2[r, :]
        g = dn * gain2
        sm[5:6, :] += jnp.sum(dn * z, axis=0, keepdims=True)
        sm[6:7, :] += jnp.sum(dn, axis=0, keepdims=True)
        dh = cot[r, :].astype(f32) + rr * (
            g
            - jnp.mean(g, axis=-1, keepdims=True)
            - z * jnp.mean(g * z, axis=-1, keepdims=True)
        )
        h_v[r, :] = dh
        db = dh.astype(bf16)
        n2[r, :] = db
        sm[4:5, :] += jnp.sum(db.astype(f32), axis=0, keepdims=True)
        du[r, :] = dg(db, wo[...], NT).astype(bf16)
        return 0

    lax.fori_loop(0, C, second, 0)
    c_li = load(2, li_h, acc)
    c_o = pltpu.make_async_copy(pb, out_h, osem.at[0])
    c_o.start()
    c_dh = pltpu.make_async_copy(h_v, dh_h, osem.at[1])
    c_dh.start()
    gb[2 * J] = dg(a_v[...], n2[...], TN).astype(bf16).reshape(B // 2, 2, CH, D)

    for c in (c_k, c_v, c_li, c_q, c_wk, c_wv, c_wq, c_n1):
        c.wait()
    dq_v, do_v = cot, du
    lane = lax.broadcasted_iota(jnp.int32, (1, 128), 1)
    lo = lane < 64

    def stack(v):
        zero = jnp.zeros_like(v)
        return jnp.concatenate([jnp.where(lo, v, zero), jnp.where(lo, zero, v)], 0)

    def pair(t, _):
        q, p = t // pairs, t % pairs
        slot = t % 2
        lanes = pl.ds(al(p * 128, 128), 128)
        rq = pl.ds(al(q * R), R)
        rk = pl.ds(al(q * T), T)
        qs = stack(q_v[rq, lanes])
        dof = do_v[rq, lanes].astype(f32) * acc[rq, lanes]
        dos = stack(dof.astype(bf16))
        dl = jnp.sum(stack(dof * a_v[rq, lanes].astype(f32)), axis=1, keepdims=True)
        e_copy(t, slot).wait()
        dp = dg(dos, vv[rk, lanes], NT)
        ds = (e_v[slot].astype(f32) * (dp - dl)).astype(bf16)
        dqs = dg(ds, kk[rk, lanes], NN)
        dq_v[rq, lanes] = (jnp.where(lo, dqs[:R], dqs[R:]) * (HEAD_DIM ** (-0.5))).astype(
            bf16
        )
        kk[rk, lanes] = (dg(qs, ds, TN) * (1.0 / LOG2E)).astype(bf16).T
        vv[rk, lanes] = dg(dos, e_v[slot], TN).astype(bf16).T

        @pl.when(t + 2 < C * pairs)
        def _():
            e_copy(t + 2, slot).start()

        @pl.when(p == pairs - 1)
        def _():
            def block(i, _):
                blk = (s + 1 + i) % S
                rr = pl.ds(al((q * S + blk) * R), R)
                f = dg(kk[rr, :], wk[...], NT) + dg(vv[rr, :], wv[...], NT)
                f += jnp.where(blk == s, 1.0, 0.0) * dg(dq_v[rq, :], wq[...], NT)
                n = n1[rr, :].astype(f32)
                sm[0:1, :] += jnp.sum(f * n, axis=0, keepdims=True)
                sm[1:2, :] += jnp.sum(f, axis=0, keepdims=True)
                dn[rr, :] = f.astype(bf16)
                return 0

            lax.fori_loop(0, S, block, 0)

        return 0

    lax.fori_loop(0, C * pairs, pair, 0)
    c_dn = pltpu.make_async_copy(dn, dn_h, osem.at[2])
    c_dn.start()
    sm[0:1, :] = (sm[0:1, :] - shift1 * sm[1:2, :]) / gain1
    sm[2:3, :] = jnp.sum(dq_v[...].astype(f32), axis=0, keepdims=True)
    sm[3:4, :] = jnp.sum(vv[0:t_rows, :].astype(f32), axis=0, keepdims=True)
    for i in range(C):
        r = pl.ds(i * R, R)
        x_v[r, :] = n1[pl.ds(al((i * S + s) * R), R), :]
    gb[2 * J + 1] = dg(x_v[...], dq_v[...], TN).astype(bf16).reshape(B // 2, 2, CH, D)
    gb[2 * J + 2] = dg(n1[...], kk[0:t_rows, :], TN).astype(bf16).reshape(B // 2, 2, CH, D)
    gb[2 * J + 3] = dg(n1[...], vv[0:t_rows, :], TN).astype(bf16).reshape(B // 2, 2, CH, D)
    c_g = pltpu.make_async_copy(gb, g_h, osem.at[3])
    c_g.start()
    c_s = pltpu.make_async_copy(sm, sm_h, osem.at[4])
    c_s.start()
    for c in (c_o, c_dh, c_dn, c_g, c_s):
        c.wait()


def backward(C, R, D, S, FF, x, cot, a, li, q, k, v, n1, e, vec, bup, wo, wu, wd, wq, wk, wv):
    N, T = C * R, R * S
    J = FF // D
    U = 2 * J + 4
    sd = jax.ShapeDtypeStruct
    dma = pltpu.SemaphoreType.DMA
    vm = pltpu.VMEM
    return pl.pallas_call(
        functools.partial(backward_kernel, C, R, D, S, FF),
        out_shape=(
            sd((N, D), bf16),
            sd((N, D), f32),
            sd((U, 4, 2, D // 8, D), bf16),
            sd((C * T, D), bf16),
            sd((16, D), f32),
        ),
        in_specs=[ANY] * 9 + [VM, VM] + [ANY] * 6,
        out_specs=(ANY,) * 5,
        scratch_shapes=[
            vm((N, D), bf16), vm((N, D), bf16), vm((N, D), bf16), vm((N, D), bf16),
            vm((N, D), bf16), vm((N, D), bf16), vm((N, D), bf16),
            vm((N, D), f32), vm((N, D), f32), vm((N, D), f32),
            vm((FF, D), bf16), vm((FF, D), bf16), vm((C * T, D), bf16),
            vm((D, D), bf16), vm((D, D), bf16), vm((D, D), bf16), vm((D, D), bf16),
            vm((U, 4, 2, D // 8, D), bf16), vm((C * T, D), bf16),
            vm((2, 2 * R, T), bf16), vm((16, D), f32),
            dma((4 + 2 * J + 5,)), dma((2,)), dma((5,)),
        ],
        compiler_params=pltpu.CompilerParams(vmem_limit_bytes=62 * 2**20),
        cost_estimate=pl.CostEstimate(
            flops=40 * 10**9, bytes_accessed=60 * 10**6, transcendentals=0
        ),
    )(x, cot, a, li, q, k, v, n1, e, vec, bup, wo, wu, wd, wq, wk, wv)


def fast_body(
    inputs, lengths, gain_one, shift_one, w_query, b_query, w_key, w_value, b_value, w_out, b_out,
    gain_two, shift_two, w_up, b_up, w_down, b_down, cotangent,
):
    C, R, D = inputs.shape
    S = lax.axis_size("seq")
    FF = w_up.shape[1]
    N = C * R
    x = inputs.reshape(N, D)
    cot = cotangent.reshape(N, D)
    vec = jnp.stack(
        (gain_one, shift_one, b_query, b_value, b_out, gain_two, shift_two, b_down)
    ).astype(f32)
    bup = b_up.reshape(FF // D, D).astype(f32)
    n1, q, k, v, a, li, e = attend(C, R, D, S, x, lengths, vec, w_query, w_key, w_value)
    out, dh, g, dn, sm = backward(
        C, R, D, S, FF, x, cot, a, li, q, k, v, n1, e, vec, bup, w_out, w_up, w_down,
        w_query, w_key, w_value,
    )
    dn = lax.psum_scatter(
        dn.reshape(C, S, R, D), "seq", scatter_dimension=1, tiled=True
    ).reshape(N, D).astype(f32)
    z, r = row_norm(x.astype(f32))
    gg = dn * gain_one.astype(f32)
    dx = r * (
        gg - jnp.mean(gg, axis=-1, keepdims=True) - z * jnp.mean(gg * z, axis=-1, keepdims=True)
    )
    input_grad = (dh + dx).astype(bf16)
    sm = lax.psum(sm, ("seq", "batch"))
    b = lax.axis_index("batch")
    U = g.shape[0]
    g = lax.psum_scatter(g.reshape(U, 8, D // 8, D), "batch", scatter_dimension=1, tiled=True)
    g = lax.psum(g, "seq").reshape(U, D // 8, D).astype(f32)
    J = FF // D
    part = D // 8
    small = lax.dynamic_slice(sm, (0, b * part), (8, part))
    up = jnp.concatenate([g[i] for i in range(J)], axis=1)
    down = g[J : 2 * J].reshape(FF // 8, D)
    gbup = lax.dynamic_slice(sm[8 : 8 + J].reshape(FF), (b * (FF // 8),), (FF // 8,))
    return (
        out.reshape(inputs.shape), input_grad.reshape(inputs.shape),
        small[0], small[1], g[2 * J + 1], small[2], g[2 * J + 2], g[2 * J + 3], small[3],
        g[2 * J], small[4], small[5], small[6], up, gbup, down, small[7],
    )


def from_behind(x, axis, by):
    length = lax.axis_size(axis)
    return lax.ppermute(x, axis, [(i, (i + by) % length) for i in range(length)])


def normed(values, gain, offset):
    average = jnp.mean(values, axis=-1, keepdims=True)
    centred = values - average
    spread = jnp.mean(centred * centred, axis=-1, keepdims=True)
    return centred * lax.rsqrt(spread + norm_eps) * gain + offset


def outer_sum(left, right):
    return lax.dot_general(
        left, right, (((0,), (0,)), ((), ())), preferred_element_type=jnp.float32
    )


def back_dot(grad_rows, weight):
    return lax.dot_general(
        grad_rows, weight, (((1,), (1,)), ((), ())), preferred_element_type=jnp.float32
    )


def front_dot(rows_low, weight, bias):
    return jnp.dot(rows_low, weight, preferred_element_type=jnp.float32) + bias.astype(jnp.float32)


def column_sums(values):
    return jnp.sum(values.astype(jnp.float32), axis=0)


def key_valid(lengths, source, block_rows):
    positions = source * block_rows + jnp.arange(block_rows, dtype=jnp.int32)
    return (positions[None, :] < lengths[:, None])[:, None, None, :]


def block_scores(queries, key_block, valid):
    scores = jnp.einsum(
        "srhd,sthd->srht", queries, key_block, preferred_element_type=jnp.float32
    ) * HEAD_DIM ** (-0.5)
    return jnp.where(valid, scores, masked_score)


def ring_body(
    inputs,
    lengths,
    gain_one,
    shift_one,
    w_query,
    b_query,
    w_key,
    w_value,
    b_value,
    w_out,
    b_out,
    gain_two,
    shift_two,
    w_up,
    b_up,
    w_down,
    b_down,
    cotangent,
):
    cycle_size = lax.axis_size("seq")
    position = lax.axis_index("seq")
    count, block_rows, width = inputs.shape
    heads = width // HEAD_DIM
    total_rows = count * block_rows
    split_shape = (count, block_rows, heads, HEAD_DIM)
    scale = HEAD_DIM ** (-0.5)
    rows_in = inputs.astype(jnp.float32).reshape(total_rows, width)
    first_full, norm_one_pull = jax.vjp(
        normed, rows_in, gain_one.astype(jnp.float32), shift_one.astype(jnp.float32)
    )
    first = first_full.astype(jnp.bfloat16)
    queries = front_dot(first, w_query, b_query).astype(jnp.bfloat16).reshape(split_shape)
    key_rows = jnp.dot(first, w_key, preferred_element_type=jnp.float32).astype(jnp.bfloat16)
    value_rows = front_dot(first, w_value, b_value).astype(jnp.bfloat16)
    own_block = jnp.stack((key_rows, value_rows)).reshape((2,) + split_shape)
    running_max = jnp.full((count, block_rows, heads), masked_score, jnp.float32)
    running_total = jnp.zeros((count, block_rows, heads), jnp.float32)
    running_sum = jnp.zeros(split_shape, jnp.float32)
    moving = own_block
    for rotation in range(cycle_size):
        source = (position - rotation) % cycle_size
        valid = key_valid(lengths, source, block_rows)
        scores = block_scores(queries, moving[0], valid)
        new_max = jnp.maximum(running_max, jnp.max(scores, axis=-1))
        decay = jnp.exp(running_max - new_max)
        weights_exp = jnp.where(valid, jnp.exp(scores - new_max[..., None]), 0.0)
        running_total = running_total * decay + jnp.sum(weights_exp, axis=-1)
        running_sum = running_sum * decay[..., None] + jnp.einsum(
            "srht,sthd->srhd",
            weights_exp.astype(jnp.bfloat16),
            moving[1],
            preferred_element_type=jnp.float32,
        )
        running_max = new_max
        if rotation + 1 < cycle_size:
            moving = from_behind(moving, "seq", 1)
    attended = running_sum / running_total[..., None]
    log_total = running_max + jnp.log(running_total)
    attended_low = attended.reshape(total_rows, width).astype(jnp.bfloat16)
    middle = rows_in + front_dot(attended_low, w_out, b_out)
    second_full, norm_two_pull = jax.vjp(
        normed, middle, gain_two.astype(jnp.float32), shift_two.astype(jnp.float32)
    )
    second = second_full.astype(jnp.bfloat16)
    hidden = front_dot(second, w_up, b_up)
    gelu_value, gelu_pull = jax.vjp(jax.nn.gelu, hidden)
    active = gelu_value.astype(jnp.bfloat16)
    outputs = middle + front_dot(active, w_down, b_down)
    grad_rows_out = cotangent.astype(jnp.float32).reshape(total_rows, width)
    grad_ffn = cotangent.reshape(total_rows, width)
    grad_w_down = outer_sum(active, grad_ffn)
    grad_b_down = column_sums(grad_ffn)
    grad_hidden = gelu_pull(back_dot(grad_ffn, w_down))[0].astype(jnp.bfloat16)
    grad_w_up = outer_sum(second, grad_hidden)
    grad_b_up = column_sums(grad_hidden)
    grad_middle_part, grad_gain_two, grad_shift_two = norm_two_pull(back_dot(grad_hidden, w_up))
    grad_middle = grad_rows_out + grad_middle_part
    grad_branch = grad_middle.astype(jnp.bfloat16)
    grad_w_out = outer_sum(attended_low, grad_branch)
    grad_b_out = column_sums(grad_branch)
    grad_attended = back_dot(grad_branch, w_out).astype(jnp.bfloat16).reshape(split_shape)
    row_delta = jnp.sum(grad_attended.astype(jnp.float32) * attended, axis=-1)
    grad_queries = jnp.zeros(split_shape, jnp.float32)
    carried = jnp.zeros((2,) + split_shape, jnp.float32)
    moving = own_block
    for rotation in range(cycle_size):
        source = (position - rotation) % cycle_size
        valid = key_valid(lengths, source, block_rows)
        scores = block_scores(queries, moving[0], valid)
        probs = jnp.where(valid, jnp.exp(scores - log_total[..., None]), 0.0)
        grad_probs = jnp.einsum(
            "srhd,sthd->srht", grad_attended, moving[1], preferred_element_type=jnp.float32
        )
        grad_scores = (probs * (grad_probs - row_delta[..., None])).astype(jnp.bfloat16)
        grad_queries = (
            grad_queries
            + jnp.einsum(
                "srht,sthd->srhd", grad_scores, moving[0], preferred_element_type=jnp.float32
            )
            * scale
        )
        grad_keys_part = (
            jnp.einsum("srht,srhd->sthd", grad_scores, queries, preferred_element_type=jnp.float32)
            * scale
        )
        grad_values_part = jnp.einsum(
            "srht,srhd->sthd",
            probs.astype(jnp.bfloat16),
            grad_attended,
            preferred_element_type=jnp.float32,
        )
        carried = from_behind(
            (carried + jnp.stack((grad_keys_part, grad_values_part))).astype(jnp.bfloat16), "seq", 1
        ).astype(jnp.float32)
        if rotation + 1 < cycle_size:
            moving = from_behind(moving, "seq", 1)
    grad_keys = carried[0].reshape(total_rows, width).astype(jnp.bfloat16)
    grad_values = carried[1].reshape(total_rows, width).astype(jnp.bfloat16)
    grad_query_rows = grad_queries.reshape(total_rows, width).astype(jnp.bfloat16)
    grad_w_query = outer_sum(first, grad_query_rows)
    grad_b_query = column_sums(grad_query_rows)
    grad_w_key = outer_sum(first, grad_keys)
    grad_w_value = outer_sum(first, grad_values)
    grad_b_value = column_sums(grad_values)
    grad_first = (
        back_dot(grad_query_rows, w_query)
        + back_dot(grad_keys, w_key)
        + back_dot(grad_values, w_value)
    )
    grad_rows_part, grad_gain_one, grad_shift_one = norm_one_pull(grad_first)
    input_grad = grad_middle + grad_rows_part
    scattered = (
        lax.psum_scatter(
            grad_gain_one.astype(jnp.bfloat16), "batch", scatter_dimension=0, tiled=True
        ).astype(jnp.float32),
        lax.psum_scatter(
            grad_shift_one.astype(jnp.bfloat16), "batch", scatter_dimension=0, tiled=True
        ).astype(jnp.float32),
        lax.psum_scatter(
            grad_w_query.astype(jnp.bfloat16), "batch", scatter_dimension=0, tiled=True
        ).astype(jnp.float32),
        lax.psum_scatter(
            grad_b_query.astype(jnp.bfloat16), "batch", scatter_dimension=0, tiled=True
        ).astype(jnp.float32),
        lax.psum_scatter(
            grad_w_key.astype(jnp.bfloat16), "batch", scatter_dimension=0, tiled=True
        ).astype(jnp.float32),
        lax.psum_scatter(
            grad_w_value.astype(jnp.bfloat16), "batch", scatter_dimension=0, tiled=True
        ).astype(jnp.float32),
        lax.psum_scatter(
            grad_b_value.astype(jnp.bfloat16), "batch", scatter_dimension=0, tiled=True
        ).astype(jnp.float32),
        lax.psum_scatter(
            grad_w_out.astype(jnp.bfloat16), "batch", scatter_dimension=0, tiled=True
        ).astype(jnp.float32),
        lax.psum_scatter(
            grad_b_out.astype(jnp.bfloat16), "batch", scatter_dimension=0, tiled=True
        ).astype(jnp.float32),
        lax.psum_scatter(
            grad_gain_two.astype(jnp.bfloat16), "batch", scatter_dimension=0, tiled=True
        ).astype(jnp.float32),
        lax.psum_scatter(
            grad_shift_two.astype(jnp.bfloat16), "batch", scatter_dimension=0, tiled=True
        ).astype(jnp.float32),
        lax.psum_scatter(
            grad_w_up.astype(jnp.bfloat16), "batch", scatter_dimension=0, tiled=True
        ).astype(jnp.float32),
        lax.psum_scatter(
            grad_b_up.astype(jnp.bfloat16), "batch", scatter_dimension=0, tiled=True
        ).astype(jnp.float32),
        lax.psum_scatter(
            grad_w_down.astype(jnp.bfloat16), "batch", scatter_dimension=0, tiled=True
        ).astype(jnp.float32),
        lax.psum_scatter(
            grad_b_down.astype(jnp.bfloat16), "batch", scatter_dimension=0, tiled=True
        ).astype(jnp.float32),
    )
    summed = (
        lax.psum(scattered[0].astype(jnp.bfloat16), "seq").astype(jnp.float32),
        lax.psum(scattered[1].astype(jnp.bfloat16), "seq").astype(jnp.float32),
        lax.psum(scattered[2].astype(jnp.bfloat16), "seq").astype(jnp.float32),
        lax.psum(scattered[3].astype(jnp.bfloat16), "seq").astype(jnp.float32),
        lax.psum(scattered[4].astype(jnp.bfloat16), "seq").astype(jnp.float32),
        lax.psum(scattered[5].astype(jnp.bfloat16), "seq").astype(jnp.float32),
        lax.psum(scattered[6].astype(jnp.bfloat16), "seq").astype(jnp.float32),
        lax.psum(scattered[7].astype(jnp.bfloat16), "seq").astype(jnp.float32),
        lax.psum(scattered[8].astype(jnp.bfloat16), "seq").astype(jnp.float32),
        lax.psum(scattered[9].astype(jnp.bfloat16), "seq").astype(jnp.float32),
        lax.psum(scattered[10].astype(jnp.bfloat16), "seq").astype(jnp.float32),
        lax.psum(scattered[11].astype(jnp.bfloat16), "seq").astype(jnp.float32),
        lax.psum(scattered[12].astype(jnp.bfloat16), "seq").astype(jnp.float32),
        lax.psum(scattered[13].astype(jnp.bfloat16), "seq").astype(jnp.float32),
        lax.psum(scattered[14].astype(jnp.bfloat16), "seq").astype(jnp.float32),
    )
    return (
        outputs.astype(jnp.bfloat16).reshape(inputs.shape),
        input_grad.astype(jnp.bfloat16).reshape(inputs.shape),
        summed[0],
        summed[1],
        summed[2],
        summed[3],
        summed[4],
        summed[5],
        summed[6],
        summed[7],
        summed[8],
        summed[9],
        summed[10],
        summed[11],
        summed[12],
        summed[13],
        summed[14],
    )


def solution(mesh):
    placed = (
        P("batch", "seq", None),
        P("batch"),
        P(),
        P(),
        P(),
        P(),
        P(),
        P(),
        P(),
        P(),
        P(),
        P(),
        P(),
        P(),
        P(),
        P(),
        P(),
        P("batch", "seq", None),
    )
    small = mesh.shape["seq"] == 4 and mesh.shape["batch"] == 8
    body = fast_body if small else ring_body
    return jax.shard_map(
        body,
        mesh=mesh,
        in_specs=placed,
        out_specs=(
            P("batch", "seq", None),
            P("batch", "seq", None),
            P("batch"),
            P("batch"),
            P("batch", None),
            P("batch"),
            P("batch", None),
            P("batch", None),
            P("batch"),
            P("batch", None),
            P("batch"),
            P("batch"),
            P("batch"),
            P("batch", None),
            P("batch"),
            P("batch", None),
            P("batch"),
        ),
        check_vma=False,
    )
```

```python
import functools
import math

import jax
import jax.numpy as jnp
from jax import lax
from jax.experimental import pallas as pl
from jax.experimental.pallas import tpu as pltpu
from jax.sharding import PartitionSpec as P

HEAD_DIM = 64
norm_eps = 1e-05
masked_score = -1e30

bf16 = jnp.bfloat16
f32 = jnp.float32
MESH = pl.DeviceIdType.MESH
ANY = pl.BlockSpec(memory_space=pl.ANY)
VM = pl.BlockSpec(memory_space=pltpu.VMEM)
SM = pl.BlockSpec(memory_space=pltpu.SMEM)
NN = (((1,), (0,)), ((), ()))
NT = (((1,), (1,)), ((), ()))
TN = (((0,), (0,)), ((), ()))
LOG2E = math.log2(math.e)
GC0 = math.sqrt(2.0 / math.pi)
GC1 = GC0 * 0.044715


def dg(a, b, dims):
    return lax.dot_general(a, b, dims, preferred_element_type=f32)


def al(i, m=16):
    return pl.multiple_of(i, m)


def places():
    s = lax.axis_index("seq")
    b = lax.axis_index("batch")
    y, x = s // 2, s % 2
    return s, b, y * 2 + (1 - x), (1 - y) * 2 + x, (1 - y) * 2 + (1 - x)


def row_norm(x):
    mean = jnp.mean(x, axis=-1, keepdims=True)
    c = x - mean
    r = lax.rsqrt(jnp.mean(c * c, axis=-1, keepdims=True) + norm_eps)
    return c * r, r


def attend_kernel(
    C, R, D, S,
    x_h, len_s, vec, wq_h, wk_h, wv_h,
    n1_h, q_h, k_h, v_h, a_h, li_h, e_h,
    x_v, n1, wq, wk, wv, q_v, k_v, v_v, a_v, li_v, e_v, s_v,
    lsem, osem, esem, sx, sy, rx, ry, sdx, sdy, rdx, rdy,
):
    T = R * S
    HR = R // 2
    pairs = D // 128
    s, b, px, py, pd = places()
    bar = pltpu.get_barrier_semaphore()
    for o in (px, py):
        pl.semaphore_signal(bar, 1, device_id=(o, b), device_id_type=MESH)
    xc = [
        pltpu.make_async_copy(
            x_h.at[pl.ds(i * R, R)], x_v.at[pl.ds(i * R, R)], lsem.at[i]
        )
        for i in range(C)
    ]
    for c in xc:
        c.start()
    wc = [
        pltpu.make_async_copy(h, v, lsem.at[C + i])
        for i, (h, v) in enumerate(((wk_h, wk), (wv_h, wv), (wq_h, wq)))
    ]
    for c in wc:
        c.start()

    def rows(q, blk, off, n):
        return pl.ds(al((q * S + blk) * R + off), n)

    def own_copy(q, peer, ss, rs):
        ref = n1.at[rows(q, s, 0, R)]
        return pltpu.make_async_remote_copy(
            ref, ref, ss.at[q], rs.at[q], device_id=(peer, b), device_id_type=MESH
        )

    def relay_copy(q, peer, blk, off, ss, rs):
        ref = n1.at[rows(q, blk, off, HR)]
        return pltpu.make_async_remote_copy(
            ref, ref, ss.at[q], rs.at[q], device_id=(peer, b), device_id_type=MESH
        )

    own = [(own_copy(q, px, sx, rx), own_copy(q, py, sy, ry)) for q in range(C)]
    rel = [
        (relay_copy(q, py, px, 0, sdy, rdy), relay_copy(q, px, py, HR, sdx, rdx))
        for q in range(C)
    ]

    gain, shift = vec[0:1, :], vec[1:2, :]
    bq, bv = vec[2:3, :], vec[3:4, :]
    for q in range(C):
        xc[q].wait()
        z, _ = row_norm(x_v[q * R : (q + 1) * R, :].astype(f32))
        n1[rows(q, s, 0, R), :] = (z * gain + shift).astype(bf16)
        if q == 0:
            pl.semaphore_wait(bar, 2)
        if q < 2:
            for c in own[q]:
                c.start()
    for c in wc:
        c.wait()

    def kv(q, blk):
        rs = rows(q, blk, 0, R)
        v = n1[rs, :]
        k_v[rs, :] = dg(v, wk[...], NN).astype(bf16)
        v_v[rs, :] = (dg(v, wv[...], NN) + bv).astype(bf16)

    def own_rows(q, _):
        v = n1[rows(q, s, 0, R), :]
        q_v[pl.ds(al(q * R), R), :] = (
            (dg(v, wq[...], NN) + bq) * (HEAD_DIM ** (-0.5) * LOG2E)
        ).astype(bf16)
        kv(q, s)
        return 0

    lax.fori_loop(0, C, own_rows, 0)
    qc = pltpu.make_async_copy(q_v, q_h, osem.at[0])
    qc.start()

    def arrived(q):
        for c in own[q]:
            c.wait_recv()
        for c in rel[q]:
            c.start()

    def near(q):
        lax.fori_loop(0, 2, lambda i, c: (kv(q, jnp.where(i == 0, px, py)), c)[1], 0)

    def far(q):
        for c in rel[q]:
            c.wait_recv()
        kv(q, pd)
        for i, (v, h) in enumerate(((n1, n1_h), (k_v, k_h), (v_v, v_h))):
            pltpu.make_async_copy(
                v.at[pl.ds(q * T, T)], h.at[pl.ds(q * T, T)], osem.at[3 + 3 * q + i]
            ).start()

    arrived(0)
    for c in own[2]:
        c.start()
    near(0)
    arrived(1)
    near(1)
    far(0)

    lane = lax.broadcasted_iota(jnp.int32, (1, 128), 1)
    lo = lane < 64
    col = lax.broadcasted_iota(jnp.int32, (1, T), 1)

    def e_copy(t):
        return pltpu.make_async_copy(e_v.at[t % 2], e_h.at[t], esem.at[t % 2])

    def pair(t, _):
        q, p = t // pairs, t % pairs

        @pl.when(t == pairs // 2)
        def _():
            arrived(2)
            near(2)

        for i in range(1, C):

            @pl.when(t == i * pairs)
            def _():
                far(i)

        off = al(p * 128, 128)
        rq = pl.ds(al(q * R), R)
        rk = pl.ds(al(q * T), T)
        qp = q_v[rq, pl.ds(off, 128)]
        zero = jnp.zeros_like(qp)
        qs = jnp.concatenate([jnp.where(lo, qp, zero), jnp.where(lo, zero, qp)], 0)
        bias = jnp.where(col < len_s[q], 0.0, masked_score).astype(f32)
        s_v[...] = dg(qs, k_v[rk, pl.ds(off, 128)], NT) + bias
        m = jnp.max(s_v[...], axis=1, keepdims=True)
        e = jnp.exp2(s_v[...] - m)
        eb = e.astype(bf16)
        tot = jnp.sum(e, axis=1, keepdims=True)

        @pl.when(t >= 2)
        def _():
            e_copy(t - 2).wait()

        e_v[t % 2] = eb
        e_copy(t).start()
        ol = dg(eb, v_v[rk, pl.ds(off, 128)], NN)
        inv = 1.0 / tot
        inv = jnp.where(lo, inv[:R], inv[R:])
        li_v[rq, pl.ds(off, 128)] = inv
        a_v[rq, pl.ds(off, 128)] = (jnp.where(lo, ol[:R], ol[R:]) * inv).astype(bf16)
        return 0

    lax.fori_loop(0, C * pairs, pair, 0)
    ac = pltpu.make_async_copy(a_v, a_h, osem.at[1])
    lc = pltpu.make_async_copy(li_v, li_h, osem.at[2])
    ac.start()
    lc.start()
    e_copy(C * pairs - 2).wait()
    e_copy(C * pairs - 1).wait()
    for q in range(C):
        for i, (v, h) in enumerate(((n1, n1_h), (k_v, k_h), (v_v, v_h))):
            pltpu.make_async_copy(
                v.at[pl.ds(q * T, T)], h.at[pl.ds(q * T, T)], osem.at[3 + 3 * q + i]
            ).wait()
        for c in own[q] + rel[q]:
            c.wait_send()
    qc.wait()
    ac.wait()
    lc.wait()


def attend(C, R, D, S, x, lengths, vec, wq, wk, wv):
    N, T, pairs = C * R, R * S, D // 128
    sd = jax.ShapeDtypeStruct
    dma = pltpu.SemaphoreType.DMA
    return pl.pallas_call(
        functools.partial(attend_kernel, C, R, D, S),
        out_shape=(
            sd((C * T, D), bf16),
            sd((N, D), bf16),
            sd((C * T, D), bf16),
            sd((C * T, D), bf16),
            sd((N, D), bf16),
            sd((N, D), f32),
            sd((C * pairs, 2 * R, T), bf16),
        ),
        in_specs=[ANY, SM, VM, ANY, ANY, ANY],
        out_specs=(ANY,) * 7,
        scratch_shapes=[
            pltpu.VMEM((N, D), bf16),
            pltpu.VMEM((C * T, D), bf16),
            pltpu.VMEM((D, D), bf16),
            pltpu.VMEM((D, D), bf16),
            pltpu.VMEM((D, D), bf16),
            pltpu.VMEM((N, D), bf16),
            pltpu.VMEM((C * T, D), bf16),
            pltpu.VMEM((C * T, D), bf16),
            pltpu.VMEM((N, D), bf16),
            pltpu.VMEM((N, D), f32),
            pltpu.VMEM((2, 2 * R, T), bf16),
            pltpu.VMEM((2 * R, T), f32),
            dma((C + 3,)),
            dma((3 + 3 * C,)),
            dma((2,)),
        ]
        + [dma((C,))] * 8,
        compiler_params=pltpu.CompilerParams(
            collective_id=1, has_side_effects=True, vmem_limit_bytes=60 * 2**20
        ),
        cost_estimate=pl.CostEstimate(
            flops=20 * 10**9, bytes_accessed=40 * 10**6, transcendentals=0
        ),
    )(x, lengths, vec, wq, wk, wv)


def backward_kernel(
    C, R, D, S, FF,
    x_h, cot_h, a_h, li_h, q_h, k_h, v_h, n1_h, e_h, vec, bup, wo_h, wu_h, wd_h, wq_h, wk_h, wv_h,
    out_h, ig_h, f_h, sm_h,
    cot, a_v, q_v, n2, pb, du, h_v, acc, dn2, kk, vv, n1, wk, wv, wo, gb, dn, e_v, sm,
    rc, r2, r3, s3, r4, f, d1, d2, mc, mz, mx,
    lsem, esem, osem, sems, rems, zs, zr, ds_s, ds_r, ms, mr, cr,
):
    T, N = R * S, C * R
    pairs = D // 128
    J = FF // D
    B = 8
    CH = D // B
    s, b, px, py, pd = places()
    y, x = s // 2, s % 2
    z, c = b // 2, b % 2
    sib = z * 2 + 1 - c
    t_rows = C * T
    HC, HR = CH // 2, R // 2
    U = 2 * J + 4
    bar = pltpu.get_barrier_semaphore()
    beside = [(px, b), (py, b), (s, sib)] + [(s, (z + k) % 4 * 2 + c) for k in (1, 2, 3)]
    for o in beside:
        pl.semaphore_signal(bar, 1, device_id=o, device_id_type=MESH)

    def remote(src, dst, ss, rs, dev):
        return pltpu.make_async_remote_copy(
            src, dst, ss, rs, device_id=dev, device_id_type=MESH
        )

    def slot(u):
        return u - 2 * J * (u // (2 * J))

    def mine(u):
        return x + (u % 2) * (y - x)

    def first_peer(u):
        return px + (u % 2) * (py - px)

    def last_peer(u):
        return py + (u % 2) * (px - py)

    def half(h):
        return pl.ds(al(h * HC), HC)

    def cp1(u):
        return remote(gb.at[slot(u), :, 1 - c], rc.at[u % 4], sems.at[0, u], rems.at[0, u], (s, sib))

    def cp2(u):
        return remote(
            gb.at[slot(u), :, c, half(1 - mine(u))], r2.at[slot(u)], sems.at[1, u], rems.at[1, u],
            (first_peer(u), b),
        )

    def cp3(u, k):
        zz = (z + k) % 4
        return remote(
            gb.at[slot(u), zz, c, half(mine(u))], r3.at[u, k - 1], zs.at[k - 1, u], zr.at[k - 1, u],
            (s, zz * 2 + c),
        )

    def cp4(u):
        return remote(s3.at[u % 4], r4.at[u], sems.at[2, u], rems.at[2, u], (last_peer(u), b))

    def cp5(u):
        ref = f.at[u, half(mine(u))]
        return remote(ref, ref, sems.at[3, u], rems.at[3, u], (first_peer(u), b))

    def sent(u):
        cp1(u).wait_send()
        cp2(u).wait_send()
        for k in (1, 2, 3):
            cp3(u, k).wait_send()

    def step1(u, again):
        if again:
            pl.semaphore_wait(cr.at[u % 4], 1)
        cp1(u).start()

    def step2(u, more):
        cp1(u).wait_recv()
        gb[slot(u), :, c] += rc[u % 4]
        if more:
            pl.semaphore_signal(cr.at[u % 4], 1, device_id=(s, sib), device_id_type=MESH)
        cp2(u).start()

    def step3(u):
        cp2(u).wait_recv()
        gb[slot(u), :, c, half(mine(u))] += r2[slot(u)]
        for k in (1, 2, 3):
            cp3(u, k).start()

    def step4(u):
        for k in (1, 2, 3):
            cp3(u, k).wait_recv()
        if isinstance(u, int):
            if u >= 4:
                cp4(u - 4).wait_send()
        else:

            @pl.when(u >= 4)
            def _():
                cp4(u - 4).wait_send()

        v = gb[slot(u), z, c, half(mine(u))].astype(f32)
        for k in range(3):
            v += r3[u, k].astype(f32)
        s3[u % 4] = v.astype(bf16)
        cp4(u).start()

    def step5(u):
        cp4(u).wait_recv()
        f[u, half(mine(u))] = s3[u % 4] + r4[u]
        cp5(u).start()

    def dcp(q, i):
        sl = q % 2
        if i == 0:
            a, o, dev = dn.at[sl, :, 1 - x, pl.ds(0, HR)], d1.at[sl, 0], px
        elif i == 1:
            a, o, dev = dn.at[sl, 1 - y, :, pl.ds(HR, HR)], d1.at[sl, 1], py
        elif i == 2:
            a, o, dev = dn.at[sl, 1 - y, x, pl.ds(0, HR)], d2.at[q, 0], py
        else:
            a, o, dev = dn.at[sl, y, 1 - x, pl.ds(HR, HR)], d2.at[q, 1], px
        return remote(a, o, ds_s.at[i, q], ds_r.at[i, q], (dev, b))

    def rows1(q):
        dcp(q, 0).start()
        dcp(q, 1).start()

    def rows2(q):
        sl = q % 2
        dcp(q, 0).wait_recv()
        dcp(q, 1).wait_recv()
        dn[sl, :, x, 0:HR] += d1[sl, 0]
        dn[sl, y, :, HR:R] += d1[sl, 1]
        dcp(q, 2).start()
        dcp(q, 3).start()

    def rows3(q):
        sl = q % 2
        dcp(q, 2).wait_recv()
        dcp(q, 3).wait_recv()
        for i in range(2):
            d = dn[sl, y, x, i * HR : (i + 1) * HR].astype(f32) + d2[q, i].astype(f32)
            r = pl.ds(al(q * R + i * HR), HR)
            zz, rr = row_norm(n2[r, :].astype(f32))
            g = d * gain1
            pb[r, :] = (
                h_v[r, :]
                + rr
                * (
                    g
                    - jnp.mean(g, axis=-1, keepdims=True)
                    - zz * jnp.mean(g * zz, axis=-1, keepdims=True)
                )
            ).astype(bf16)


    def load(i, h, v):
        cp = pltpu.make_async_copy(h, v, lsem.at[i])
        cp.start()
        return cp

    c_a = load(0, a_h, a_v)
    c_wo = load(1, wo_h, wo)
    c_x = load(2, x_h, du)
    c_cot = load(3, cot_h, cot)
    c_w = [
        (
            load(4 + 2 * j, wu_h.at[:, pl.ds(j * D, D)], vv.at[pl.ds(j * D, D)]),
            load(5 + 2 * j, wd_h.at[pl.ds(j * D, D)], kk.at[pl.ds(j * D, D)]),
        )
        for j in range(J)
    ]
    n0 = 4 + 2 * J
    c_q = load(n0, q_h, q_v)
    c_n1 = load(n0 + 1, n1_h, n1)
    c_wk = load(n0 + 2, wk_h, wk)
    c_wv = load(n0 + 3, wv_h, wv)

    def e_copy(t, slot):
        return pltpu.make_async_copy(e_h.at[t], e_v.at[slot], esem.at[slot])

    e_copy(0, 0).start()
    e_copy(1, 1).start()

    gain1, shift1 = vec[0:1, :], vec[1:2, :]
    b_out, gain2, shift2, b_down = vec[4:5, :], vec[5:6, :], vec[6:7, :], vec[7:8, :]
    sm[...] = jnp.zeros_like(sm)
    for w in (c_a, c_wo, c_x, c_cot):
        w.wait()

    def first(i, _):
        r = pl.ds(al(i * R), R)
        h = du[r, :].astype(f32) + dg(a_v[r, :], wo[...], NN) + b_out
        h_v[r, :] = h
        zn, _r = row_norm(h)
        n2[r, :] = (zn * gain2 + shift2).astype(bf16)
        acc[r, :] = h + b_down
        dn2[r, :] = jnp.zeros((R, D), f32)
        sm[7:8, :] += jnp.sum(cot[r, :].astype(f32), axis=0, keepdims=True)
        return 0

    lax.fori_loop(0, C, first, 0)
    pl.semaphore_wait(bar, len(beside))

    def ffn(j, _):
        jr = pl.ds(al(j * D), D)
        for jj in range(J):

            @pl.when(j == jj)
            def _():
                c_w[jj][0].wait()
                c_w[jj][1].wait()

        bias = bup[pl.ds(j, 1), :]

        def chunk(i, sums):
            r = pl.ds(al(i * R), R)
            u = dg(n2[r, :], vv[jr, :], NN) + bias
            g = dg(cot[r, :], kk[jr, :], NT)
            u2 = u * u
            t = jnp.tanh(u * (GC0 + GC1 * u2))
            hu = 0.5 * u
            half = 0.5 + 0.5 * t
            p = (u * half).astype(bf16)
            d = (g * (half + hu * (1.0 - t * t) * (GC0 + 3.0 * GC1 * u2))).astype(bf16)
            pb[r, :] = p
            du[r, :] = d
            acc[r, :] += dg(p, kk[jr, :], NN)
            dn2[r, :] += dg(d, vv[jr, :], NT)
            return sums + jnp.sum(d.astype(f32), axis=0, keepdims=True)

        dj = lax.fori_loop(0, C, chunk, jnp.zeros((1, D), f32))
        sm[pl.ds(8 + j, 1), :] = dj

        @pl.when(j >= 3)
        def _():
            step4(j - 3)

        @pl.when(j >= 2)
        def _():
            step3(j - 2)

        @pl.when(j >= 1)
        def _():
            step2(j - 1, True)

        gb[j] = dg(n2[...], du[...], TN).astype(bf16).reshape(B // 2, 2, CH, D)
        step1(j, False)
        gw = dg(pb[...], cot[...], TN).astype(bf16)
        per = FF // B
        for bb in range(D // per):
            for i in range(per // CH):
                o = bb * per + i * CH
                gb[J + i, j, bb] = gw[o : o + CH, :]
        return 0

    lax.fori_loop(0, J, ffn, 0)
    for u in (J, J + 1, J + 2):
        step1(u, True)

    c_k = load(0, k_h, kk.at[pl.ds(0, t_rows)])
    c_v = load(1, v_h, vv.at[pl.ds(0, t_rows)])

    def second(i, _):
        r = pl.ds(al(i * R), R)
        pb[r, :] = acc[r, :].astype(bf16)
        zn, rr = row_norm(h_v[r, :])
        dnn = dn2[r, :]
        g = dnn * gain2
        sm[5:6, :] += jnp.sum(dnn * zn, axis=0, keepdims=True)
        sm[6:7, :] += jnp.sum(dnn, axis=0, keepdims=True)
        dh = cot[r, :].astype(f32) + rr * (
            g
            - jnp.mean(g, axis=-1, keepdims=True)
            - zn * jnp.mean(g * zn, axis=-1, keepdims=True)
        )
        h_v[r, :] = dh
        db = dh.astype(bf16)
        n2[r, :] = db
        sm[4:5, :] += jnp.sum(db.astype(f32), axis=0, keepdims=True)
        du[r, :] = dg(db, wo[...], NT).astype(bf16)
        return 0

    lax.fori_loop(0, C, second, 0)
    c_li = load(2, li_h, acc)
    c_o = pltpu.make_async_copy(pb, out_h, osem.at[0])
    c_o.start()
    step5(0)
    step4(1)
    step3(2)
    step2(3, True)
    step1(J + 3, True)
    sent(0)
    c_wq = load(3, wq_h, wo)
    gb[slot(2 * J)] = dg(a_v[...], n2[...], TN).astype(bf16).reshape(B // 2, 2, CH, D)

    c_x = load(4, x_h, n2)
    for w in (c_o, c_x, c_k, c_v, c_li, c_q, c_wk, c_wv, c_wq, c_n1):
        w.wait()
    dq_v, do_v = cot, du
    lane = lax.broadcasted_iota(jnp.int32, (1, 128), 1)
    lo = lane < 64

    def stack(v):
        zero = jnp.zeros_like(v)
        return jnp.concatenate([jnp.where(lo, v, zero), jnp.where(lo, zero, v)], 0)

    def pair(t, _):
        q, p = t // pairs, t % pairs
        slot = t % 2
        lanes = pl.ds(al(p * 128, 128), 128)
        rq = pl.ds(al(q * R), R)
        rk = pl.ds(al(q * T), T)
        qs = stack(q_v[rq, lanes])
        dof = do_v[rq, lanes].astype(f32) * acc[rq, lanes]
        dos = stack(dof.astype(bf16))
        dl = jnp.sum(stack(dof * a_v[rq, lanes].astype(f32)), axis=1, keepdims=True)
        e_copy(t, slot).wait()
        dp = dg(dos, vv[rk, lanes], NT)
        ds = (e_v[slot].astype(f32) * (dp - dl)).astype(bf16)
        dqs = dg(ds, kk[rk, lanes], NN)
        dq_v[rq, lanes] = (jnp.where(lo, dqs[:R], dqs[R:]) * (HEAD_DIM ** (-0.5))).astype(
            bf16
        )
        kk[rk, lanes] = (dg(qs, ds, TN) * (1.0 / LOG2E)).astype(bf16).T
        vv[rk, lanes] = dg(dos, e_v[slot], TN).astype(bf16).T

        third = t // 3
        hit = t % 3 == 0

        @pl.when(t == 1)
        def _():
            step3(3)
            step4(2)
            step5(1)
            step1(2 * J, True)

        @pl.when(t == 4)
        def _():
            step4(3)
            step5(2)

        @pl.when(t == 7)
        def _():
            step5(3)

        @pl.when(hit & (t >= 6))
        def _():
            step4(J + third - 2)

        @pl.when(hit & (t >= 3))
        def _():
            step3(J + third - 1)

        @pl.when(hit & (t <= 9))
        def _():
            step2(J + third, True)

        @pl.when(t == 12)
        def _():
            cp5(0).wait_recv()
            step2(2 * J, False)

        @pl.when((t % 3 == 2) & (t >= 8))
        def _():
            step5(J + third - 2)

        for i in range(C - 1):

            @pl.when(t == (i + 1) * pairs + 3)
            def _():
                rows2(i)

        @pl.when(t == pairs + 8)
        def _():
            rows3(0)

        @pl.when(t + 2 < C * pairs)
        def _():
            e_copy(t + 2, slot).start()

        @pl.when(p == pairs - 1)
        def _():
            @pl.when(q == 2)
            def _():
                for i in range(4):
                    dcp(0, i).wait_send()

            def block(i, _):
                blk = (s + 1 + i) % S
                rr = pl.ds(al((q * S + blk) * R), R)
                f = dg(kk[rr, :], wk[...], NT) + dg(vv[rr, :], wv[...], NT)
                f += jnp.where(blk == s, 1.0, 0.0) * dg(dq_v[rq, :], wo[...], NT)
                n = n1[rr, :].astype(f32)
                sm[0:1, :] += jnp.sum(f * n, axis=0, keepdims=True)
                sm[1:2, :] += jnp.sum(f, axis=0, keepdims=True)
                dn[q % 2, blk // 2, blk % 2] = f.astype(bf16)
                return 0

            lax.fori_loop(0, S, block, 0)
            rows1(q)

        return 0

    lax.fori_loop(0, C * pairs, pair, 0)
    step4(2 * J)
    for u in (1, 2, 3):
        sent(u)
        cp5(u).wait_recv()
    sm[2:3, :] = jnp.sum(dq_v[...].astype(f32), axis=0, keepdims=True)
    sm[3:4, :] = jnp.sum(vv[0:t_rows, :].astype(f32), axis=0, keepdims=True)
    sm[0:1, :] = (sm[0:1, :] - shift1 * sm[1:2, :]) / gain1

    def mcp(i, src, dst, dev):
        return remote(src, dst, ms.at[i], mr.at[i], dev)

    m1 = mcp(0, sm, mc.at[0], (s, sib))
    m1.start()
    for i in range(C):
        r = pl.ds(i * R, R)
        a_v[r, :] = n1[pl.ds(al((i * S + s) * R), R), :]
    gb[slot(2 * J + 1)] = dg(a_v[...], dq_v[...], TN).astype(bf16).reshape(B // 2, 2, CH, D)
    step1(2 * J + 1, True)
    rows2(2)
    gb[slot(2 * J + 2)] = dg(n1[...], kk[0:t_rows, :], TN).astype(bf16).reshape(B // 2, 2, CH, D)
    step1(2 * J + 2, True)
    step2(2 * J + 1, False)
    step5(2 * J)
    m1.wait()
    mz[0] = sm[...] + mc[0]
    m2 = [mcp(k, mz.at[0], mz.at[k], (s, (z + k) % 4 * 2 + c)) for k in (1, 2, 3)]
    for m in m2:
        m.start()
    rows3(1)
    gb[slot(2 * J + 3)] = dg(n1[...], vv[0:t_rows, :], TN).astype(bf16).reshape(B // 2, 2, CH, D)
    step1(2 * J + 3, True)
    step3(2 * J + 1)
    step2(2 * J + 2, False)
    for m in m2:
        m.wait()
    mx[0] = (mz[0] + mz[1]) + (mz[2] + mz[3])
    m3 = mcp(4, mx.at[0], mx.at[1], (px, b))
    m3.start()
    rows3(2)
    c_i = pltpu.make_async_copy(pb, ig_h, osem.at[1])
    c_i.start()
    step2(2 * J + 3, False)
    m3.wait()
    mx[2] = mx[0] + mx[1]
    m4 = mcp(5, mx.at[2], mx.at[3], (py, b))
    m4.start()
    step3(2 * J + 2)
    step4(2 * J + 1)
    step3(2 * J + 3)
    step4(2 * J + 2)
    step5(2 * J + 1)
    m4.wait()
    sm[...] = mx[2] + mx[3]
    c_s = pltpu.make_async_copy(sm, sm_h, osem.at[2])
    c_s.start()
    step4(2 * J + 3)
    step5(2 * J + 2)
    step5(2 * J + 3)
    for u in range(U):
        if u > 3:
            cp5(u).wait_recv()
    c_f = pltpu.make_async_copy(f, f_h, osem.at[3])
    c_f.start()
    for u in range(U):
        if u > 3:
            sent(u)
        if u >= 2 * J:
            cp4(u).wait_send()
        cp5(u).wait_send()
    for q in (1, 2):
        for i in range(4):
            dcp(q, i).wait_send()
    for o in (c_i, c_s, c_f):
        o.wait()


def backward(C, R, D, S, FF, x, cot, a, li, q, k, v, n1, e, vec, bup, wo, wu, wd, wq, wk, wv):
    N, T = C * R, R * S
    J = FF // D
    U, CH = 2 * J + 4, D // 8
    sd = jax.ShapeDtypeStruct
    dma = pltpu.SemaphoreType.DMA
    vm = pltpu.VMEM
    return pl.pallas_call(
        functools.partial(backward_kernel, C, R, D, S, FF),
        out_shape=(
            sd((N, D), bf16),
            sd((N, D), bf16),
            sd((U, D // 8, D), bf16),
            sd((16, D), f32),
        ),
        in_specs=[ANY] * 9 + [VM, VM] + [ANY] * 6,
        out_specs=(ANY,) * 4,
        scratch_shapes=[
            vm((N, D), bf16), vm((N, D), bf16), vm((N, D), bf16),
            vm((N, D), bf16), vm((N, D), bf16), vm((N, D), bf16),
            vm((N, D), f32), vm((N, D), f32), vm((N, D), f32),
            vm((FF, D), bf16), vm((FF, D), bf16), vm((C * T, D), bf16),
            vm((D, D), bf16), vm((D, D), bf16), vm((D, D), bf16),
            vm((2 * J, 4, 2, CH, D), bf16), vm((2, 2, 2, R, D), bf16),
            vm((2, 2 * R, T), bf16), vm((16, D), f32),
            vm((4, 4, CH, D), bf16), vm((2 * J, 4, CH // 2, D), bf16), vm((U, 3, CH // 2, D), bf16),
            vm((4, CH // 2, D), bf16), vm((U, CH // 2, D), bf16), vm((U, CH, D), bf16),
            vm((2, 2, 2, R // 2, D), bf16), vm((C, 2, R // 2, D), bf16),
            vm((1, 16, D), f32), vm((4, 16, D), f32), vm((4, 16, D), f32),
            dma((4 + 2 * J + 4,)), dma((2,)), dma((4,)),
            dma((4, U)), dma((4, U)), dma((3, U)), dma((3, U)),
            dma((4, C)), dma((4, C)), dma((6,)), dma((6,)),
            pltpu.SemaphoreType.REGULAR((4,)),
        ],
        compiler_params=pltpu.CompilerParams(
            collective_id=2, has_side_effects=True, vmem_limit_bytes=(64 * 2**20) - 2**17
        ),
        cost_estimate=pl.CostEstimate(
            flops=40 * 10**9, bytes_accessed=60 * 10**6, transcendentals=0
        ),
    )(x, cot, a, li, q, k, v, n1, e, vec, bup, wo, wu, wd, wq, wk, wv)


def fast_body(
    inputs, lengths, gain_one, shift_one, w_query, b_query, w_key, w_value, b_value, w_out, b_out,
    gain_two, shift_two, w_up, b_up, w_down, b_down, cotangent,
):
    C, R, D = inputs.shape
    S = lax.axis_size("seq")
    FF = w_up.shape[1]
    N = C * R
    x = inputs.reshape(N, D)
    cot = cotangent.reshape(N, D)
    vec = jnp.stack(
        (gain_one, shift_one, b_query, b_value, b_out, gain_two, shift_two, b_down)
    ).astype(f32)
    bup = b_up.reshape(FF // D, D).astype(f32)
    n1, q, k, v, a, li, e = attend(C, R, D, S, x, lengths, vec, w_query, w_key, w_value)
    out, input_grad, g, sm = backward(
        C, R, D, S, FF, x, cot, a, li, q, k, v, n1, e, vec, bup, w_out, w_up, w_down,
        w_query, w_key, w_value,
    )
    b = lax.axis_index("batch")
    J = FF // D
    part = D // 8
    g = g.astype(f32)
    small = lax.dynamic_slice(sm, (0, b * part), (8, part))
    up = jnp.concatenate([g[i] for i in range(J)], axis=1)
    down = g[J : 2 * J].reshape(FF // 8, D)
    gbup = lax.dynamic_slice(sm[8 : 8 + J].reshape(FF), (b * (FF // 8),), (FF // 8,))
    return (
        out.reshape(inputs.shape), input_grad.reshape(inputs.shape),
        small[0], small[1], g[2 * J + 1], small[2], g[2 * J + 2], g[2 * J + 3], small[3],
        g[2 * J], small[4], small[5], small[6], up, gbup, down, small[7],
    )


def from_behind(x, axis, by):
    length = lax.axis_size(axis)
    return lax.ppermute(x, axis, [(i, (i + by) % length) for i in range(length)])


def normed(values, gain, offset):
    average = jnp.mean(values, axis=-1, keepdims=True)
    centred = values - average
    spread = jnp.mean(centred * centred, axis=-1, keepdims=True)
    return centred * lax.rsqrt(spread + norm_eps) * gain + offset


def outer_sum(left, right):
    return lax.dot_general(
        left, right, (((0,), (0,)), ((), ())), preferred_element_type=jnp.float32
    )


def back_dot(grad_rows, weight):
    return lax.dot_general(
        grad_rows, weight, (((1,), (1,)), ((), ())), preferred_element_type=jnp.float32
    )


def front_dot(rows_low, weight, bias):
    return jnp.dot(rows_low, weight, preferred_element_type=jnp.float32) + bias.astype(jnp.float32)


def column_sums(values):
    return jnp.sum(values.astype(jnp.float32), axis=0)


def key_valid(lengths, source, block_rows):
    positions = source * block_rows + jnp.arange(block_rows, dtype=jnp.int32)
    return (positions[None, :] < lengths[:, None])[:, None, None, :]


def block_scores(queries, key_block, valid):
    scores = jnp.einsum(
        "srhd,sthd->srht", queries, key_block, preferred_element_type=jnp.float32
    ) * HEAD_DIM ** (-0.5)
    return jnp.where(valid, scores, masked_score)


def ring_body(
    inputs,
    lengths,
    gain_one,
    shift_one,
    w_query,
    b_query,
    w_key,
    w_value,
    b_value,
    w_out,
    b_out,
    gain_two,
    shift_two,
    w_up,
    b_up,
    w_down,
    b_down,
    cotangent,
):
    cycle_size = lax.axis_size("seq")
    position = lax.axis_index("seq")
    count, block_rows, width = inputs.shape
    heads = width // HEAD_DIM
    total_rows = count * block_rows
    split_shape = (count, block_rows, heads, HEAD_DIM)
    scale = HEAD_DIM ** (-0.5)
    rows_in = inputs.astype(jnp.float32).reshape(total_rows, width)
    first_full, norm_one_pull = jax.vjp(
        normed, rows_in, gain_one.astype(jnp.float32), shift_one.astype(jnp.float32)
    )
    first = first_full.astype(jnp.bfloat16)
    queries = front_dot(first, w_query, b_query).astype(jnp.bfloat16).reshape(split_shape)
    key_rows = jnp.dot(first, w_key, preferred_element_type=jnp.float32).astype(jnp.bfloat16)
    value_rows = front_dot(first, w_value, b_value).astype(jnp.bfloat16)
    own_block = jnp.stack((key_rows, value_rows)).reshape((2,) + split_shape)
    running_max = jnp.full((count, block_rows, heads), masked_score, jnp.float32)
    running_total = jnp.zeros((count, block_rows, heads), jnp.float32)
    running_sum = jnp.zeros(split_shape, jnp.float32)
    moving = own_block
    for rotation in range(cycle_size):
        source = (position - rotation) % cycle_size
        valid = key_valid(lengths, source, block_rows)
        scores = block_scores(queries, moving[0], valid)
        new_max = jnp.maximum(running_max, jnp.max(scores, axis=-1))
        decay = jnp.exp(running_max - new_max)
        weights_exp = jnp.where(valid, jnp.exp(scores - new_max[..., None]), 0.0)
        running_total = running_total * decay + jnp.sum(weights_exp, axis=-1)
        running_sum = running_sum * decay[..., None] + jnp.einsum(
            "srht,sthd->srhd",
            weights_exp.astype(jnp.bfloat16),
            moving[1],
            preferred_element_type=jnp.float32,
        )
        running_max = new_max
        if rotation + 1 < cycle_size:
            moving = from_behind(moving, "seq", 1)
    attended = running_sum / running_total[..., None]
    log_total = running_max + jnp.log(running_total)
    attended_low = attended.reshape(total_rows, width).astype(jnp.bfloat16)
    middle = rows_in + front_dot(attended_low, w_out, b_out)
    second_full, norm_two_pull = jax.vjp(
        normed, middle, gain_two.astype(jnp.float32), shift_two.astype(jnp.float32)
    )
    second = second_full.astype(jnp.bfloat16)
    hidden = front_dot(second, w_up, b_up)
    gelu_value, gelu_pull = jax.vjp(jax.nn.gelu, hidden)
    active = gelu_value.astype(jnp.bfloat16)
    outputs = middle + front_dot(active, w_down, b_down)
    grad_rows_out = cotangent.astype(jnp.float32).reshape(total_rows, width)
    grad_ffn = cotangent.reshape(total_rows, width)
    grad_w_down = outer_sum(active, grad_ffn)
    grad_b_down = column_sums(grad_ffn)
    grad_hidden = gelu_pull(back_dot(grad_ffn, w_down))[0].astype(jnp.bfloat16)
    grad_w_up = outer_sum(second, grad_hidden)
    grad_b_up = column_sums(grad_hidden)
    grad_middle_part, grad_gain_two, grad_shift_two = norm_two_pull(back_dot(grad_hidden, w_up))
    grad_middle = grad_rows_out + grad_middle_part
    grad_branch = grad_middle.astype(jnp.bfloat16)
    grad_w_out = outer_sum(attended_low, grad_branch)
    grad_b_out = column_sums(grad_branch)
    grad_attended = back_dot(grad_branch, w_out).astype(jnp.bfloat16).reshape(split_shape)
    row_delta = jnp.sum(grad_attended.astype(jnp.float32) * attended, axis=-1)
    grad_queries = jnp.zeros(split_shape, jnp.float32)
    carried = jnp.zeros((2,) + split_shape, jnp.float32)
    moving = own_block
    for rotation in range(cycle_size):
        source = (position - rotation) % cycle_size
        valid = key_valid(lengths, source, block_rows)
        scores = block_scores(queries, moving[0], valid)
        probs = jnp.where(valid, jnp.exp(scores - log_total[..., None]), 0.0)
        grad_probs = jnp.einsum(
            "srhd,sthd->srht", grad_attended, moving[1], preferred_element_type=jnp.float32
        )
        grad_scores = (probs * (grad_probs - row_delta[..., None])).astype(jnp.bfloat16)
        grad_queries = (
            grad_queries
            + jnp.einsum(
                "srht,sthd->srhd", grad_scores, moving[0], preferred_element_type=jnp.float32
            )
            * scale
        )
        grad_keys_part = (
            jnp.einsum("srht,srhd->sthd", grad_scores, queries, preferred_element_type=jnp.float32)
            * scale
        )
        grad_values_part = jnp.einsum(
            "srht,srhd->sthd",
            probs.astype(jnp.bfloat16),
            grad_attended,
            preferred_element_type=jnp.float32,
        )
        carried = from_behind(
            (carried + jnp.stack((grad_keys_part, grad_values_part))).astype(jnp.bfloat16), "seq", 1
        ).astype(jnp.float32)
        if rotation + 1 < cycle_size:
            moving = from_behind(moving, "seq", 1)
    grad_keys = carried[0].reshape(total_rows, width).astype(jnp.bfloat16)
    grad_values = carried[1].reshape(total_rows, width).astype(jnp.bfloat16)
    grad_query_rows = grad_queries.reshape(total_rows, width).astype(jnp.bfloat16)
    grad_w_query = outer_sum(first, grad_query_rows)
    grad_b_query = column_sums(grad_query_rows)
    grad_w_key = outer_sum(first, grad_keys)
    grad_w_value = outer_sum(first, grad_values)
    grad_b_value = column_sums(grad_values)
    grad_first = (
        back_dot(grad_query_rows, w_query)
        + back_dot(grad_keys, w_key)
        + back_dot(grad_values, w_value)
    )
    grad_rows_part, grad_gain_one, grad_shift_one = norm_one_pull(grad_first)
    input_grad = grad_middle + grad_rows_part
    scattered = (
        lax.psum_scatter(
            grad_gain_one.astype(jnp.bfloat16), "batch", scatter_dimension=0, tiled=True
        ).astype(jnp.float32),
        lax.psum_scatter(
            grad_shift_one.astype(jnp.bfloat16), "batch", scatter_dimension=0, tiled=True
        ).astype(jnp.float32),
        lax.psum_scatter(
            grad_w_query.astype(jnp.bfloat16), "batch", scatter_dimension=0, tiled=True
        ).astype(jnp.float32),
        lax.psum_scatter(
            grad_b_query.astype(jnp.bfloat16), "batch", scatter_dimension=0, tiled=True
        ).astype(jnp.float32),
        lax.psum_scatter(
            grad_w_key.astype(jnp.bfloat16), "batch", scatter_dimension=0, tiled=True
        ).astype(jnp.float32),
        lax.psum_scatter(
            grad_w_value.astype(jnp.bfloat16), "batch", scatter_dimension=0, tiled=True
        ).astype(jnp.float32),
        lax.psum_scatter(
            grad_b_value.astype(jnp.bfloat16), "batch", scatter_dimension=0, tiled=True
        ).astype(jnp.float32),
        lax.psum_scatter(
            grad_w_out.astype(jnp.bfloat16), "batch", scatter_dimension=0, tiled=True
        ).astype(jnp.float32),
        lax.psum_scatter(
            grad_b_out.astype(jnp.bfloat16), "batch", scatter_dimension=0, tiled=True
        ).astype(jnp.float32),
        lax.psum_scatter(
            grad_gain_two.astype(jnp.bfloat16), "batch", scatter_dimension=0, tiled=True
        ).astype(jnp.float32),
        lax.psum_scatter(
            grad_shift_two.astype(jnp.bfloat16), "batch", scatter_dimension=0, tiled=True
        ).astype(jnp.float32),
        lax.psum_scatter(
            grad_w_up.astype(jnp.bfloat16), "batch", scatter_dimension=0, tiled=True
        ).astype(jnp.float32),
        lax.psum_scatter(
            grad_b_up.astype(jnp.bfloat16), "batch", scatter_dimension=0, tiled=True
        ).astype(jnp.float32),
        lax.psum_scatter(
            grad_w_down.astype(jnp.bfloat16), "batch", scatter_dimension=0, tiled=True
        ).astype(jnp.float32),
        lax.psum_scatter(
            grad_b_down.astype(jnp.bfloat16), "batch", scatter_dimension=0, tiled=True
        ).astype(jnp.float32),
    )
    summed = (
        lax.psum(scattered[0].astype(jnp.bfloat16), "seq").astype(jnp.float32),
        lax.psum(scattered[1].astype(jnp.bfloat16), "seq").astype(jnp.float32),
        lax.psum(scattered[2].astype(jnp.bfloat16), "seq").astype(jnp.float32),
        lax.psum(scattered[3].astype(jnp.bfloat16), "seq").astype(jnp.float32),
        lax.psum(scattered[4].astype(jnp.bfloat16), "seq").astype(jnp.float32),
        lax.psum(scattered[5].astype(jnp.bfloat16), "seq").astype(jnp.float32),
        lax.psum(scattered[6].astype(jnp.bfloat16), "seq").astype(jnp.float32),
        lax.psum(scattered[7].astype(jnp.bfloat16), "seq").astype(jnp.float32),
        lax.psum(scattered[8].astype(jnp.bfloat16), "seq").astype(jnp.float32),
        lax.psum(scattered[9].astype(jnp.bfloat16), "seq").astype(jnp.float32),
        lax.psum(scattered[10].astype(jnp.bfloat16), "seq").astype(jnp.float32),
        lax.psum(scattered[11].astype(jnp.bfloat16), "seq").astype(jnp.float32),
        lax.psum(scattered[12].astype(jnp.bfloat16), "seq").astype(jnp.float32),
        lax.psum(scattered[13].astype(jnp.bfloat16), "seq").astype(jnp.float32),
        lax.psum(scattered[14].astype(jnp.bfloat16), "seq").astype(jnp.float32),
    )
    return (
        outputs.astype(jnp.bfloat16).reshape(inputs.shape),
        input_grad.astype(jnp.bfloat16).reshape(inputs.shape),
        summed[0],
        summed[1],
        summed[2],
        summed[3],
        summed[4],
        summed[5],
        summed[6],
        summed[7],
        summed[8],
        summed[9],
        summed[10],
        summed[11],
        summed[12],
        summed[13],
        summed[14],
    )


def solution(mesh):
    placed = (
        P("batch", "seq", None),
        P("batch"),
        P(),
        P(),
        P(),
        P(),
        P(),
        P(),
        P(),
        P(),
        P(),
        P(),
        P(),
        P(),
        P(),
        P(),
        P(),
        P("batch", "seq", None),
    )
    small = mesh.shape["seq"] == 4 and mesh.shape["batch"] == 8
    body = fast_body if small else ring_body
    return jax.shard_map(
        body,
        mesh=mesh,
        in_specs=placed,
        out_specs=(
            P("batch", "seq", None),
            P("batch", "seq", None),
            P("batch"),
            P("batch"),
            P("batch", None),
            P("batch"),
            P("batch", None),
            P("batch", None),
            P("batch"),
            P("batch", None),
            P("batch"),
            P("batch"),
            P("batch"),
            P("batch", None),
            P("batch"),
            P("batch", None),
            P("batch"),
        ),
        check_vma=False,
    )
```

```python
import functools
import math

import jax
import jax.numpy as jnp
from jax import lax
from jax.experimental import pallas as pl
from jax.experimental.pallas import tpu as pltpu
from jax.sharding import PartitionSpec as P

HEAD_DIM = 64
norm_eps = 1e-05
masked_score = -1e30

bf16 = jnp.bfloat16
f32 = jnp.float32
MESH = pl.DeviceIdType.MESH
ANY = pl.BlockSpec(memory_space=pl.ANY)
VM = pl.BlockSpec(memory_space=pltpu.VMEM)
SM = pl.BlockSpec(memory_space=pltpu.SMEM)
NN = (((1,), (0,)), ((), ()))
NT = (((1,), (1,)), ((), ()))
TN = (((0,), (0,)), ((), ()))
LOG2E = math.log2(math.e)
GC0 = math.sqrt(2.0 / math.pi)
GC1 = GC0 * 0.044715


def dg(a, b, dims):
    return lax.dot_general(a, b, dims, preferred_element_type=f32)


def row(ref):
    return ref[...].astype(f32).reshape(1, ref.shape[0])


def al(i, m=16):
    return pl.multiple_of(i, m)


def places():
    s = lax.axis_index("seq")
    b = lax.axis_index("batch")
    y, x = s // 2, s % 2
    return s, b, y * 2 + (1 - x), (1 - y) * 2 + x, (1 - y) * 2 + (1 - x)


def row_norm(x):
    mean = jnp.mean(x, axis=-1, keepdims=True)
    c = x - mean
    r = lax.rsqrt(jnp.mean(c * c, axis=-1, keepdims=True) + norm_eps)
    return c * r, r


def attend_kernel(
    C, R, D, S,
    x_h, cot_h, len_s, g_r, s_r, bq_r, bv_r, wq_h, wk_h, wv_h, wd_h,
    n1_h, q_h, k_h, v_h, a_h, li_h, e_h, gu_h,
    x_v, n1, wq, wk, wv, q_v, k_v, v_v, a_v, li_v, e_v, s_v, cot, wd, gu,
    lsem, osem, esem, gsem, os, orr, rs, rr,
):
    T = R * S
    HR = R // 2
    pairs = D // 128
    s, b, px, py, pd = places()
    bar = pltpu.get_barrier_semaphore()
    for o in (px, py):
        pl.semaphore_signal(bar, 1, device_id=(o, b), device_id_type=MESH)
    xc = [
        pltpu.make_async_copy(
            x_h.at[pl.ds(i * R, R)], x_v.at[pl.ds(i * R, R)], lsem.at[i]
        )
        for i in range(C)
    ]
    for c in xc:
        c.start()
    wc = [
        pltpu.make_async_copy(h, v, lsem.at[C + i])
        for i, (h, v) in enumerate(((wk_h, wk), (wv_h, wv), (wq_h, wq), (cot_h, cot), (wd_h, wd)))
    ]
    for c in wc:
        c.start()

    def rows(q, blk, off, n):
        return pl.ds(al((q * S + blk) * R + off), n)

    def copy(q, peer, blk, off, ss, rs):
        ref = n1.at[rows(q, blk, off, HR)]
        return pltpu.make_async_remote_copy(
            ref, ref, ss, rs, device_id=(peer, b), device_id_type=MESH
        )

    own = [
        [
            copy(q, peer, s, off, os.at[i, q], orr.at[i, q])
            for i, (peer, off) in enumerate(((px, 0), (py, HR), (px, HR), (py, 0)))
        ]
        for q in range(C)
    ]
    rel = [
        [
            copy(q, peer, blk, off, rs.at[i, q], rr.at[i, q])
            for i, (peer, blk, off) in enumerate(((py, px, 0), (px, py, HR)))
        ]
        for q in range(C)
    ]

    gain, shift, bq, bv = (row(r) for r in (g_r, s_r, bq_r, bv_r))
    for q in range(C):
        xc[q].wait()
        z, _ = row_norm(x_v[q * R : (q + 1) * R, :].astype(f32))
        n1[rows(q, s, 0, R), :] = (z * gain + shift).astype(bf16)
        if q == 0:
            pl.semaphore_wait(bar, 2)
        if q < 2:
            for c in own[q]:
                c.start()
    for c in wc[:3]:
        c.wait()

    def kv(q, blk):
        rs = rows(q, blk, 0, R)
        v = n1[rs, :]
        k_v[rs, :] = dg(v, wk[...], NN).astype(bf16)
        v_v[rs, :] = (dg(v, wv[...], NN) + bv).astype(bf16)

    def own_rows(q, _):
        v = n1[rows(q, s, 0, R), :]
        q_v[pl.ds(al(q * R), R), :] = (
            (dg(v, wq[...], NN) + bq) * (HEAD_DIM ** (-0.5) * LOG2E)
        ).astype(bf16)
        kv(q, s)
        return 0

    lax.fori_loop(0, C, own_rows, 0)
    qc = pltpu.make_async_copy(q_v, q_h, osem.at[0])
    qc.start()

    def onward(q):
        for c in own[q][:2]:
            c.wait_recv()
        for c in rel[q]:
            c.start()

    def near(q):
        for c in own[q][2:]:
            c.wait_recv()
        lax.fori_loop(0, 2, lambda i, c: (kv(q, jnp.where(i == 0, px, py)), c)[1], 0)

    def gu_copy(j):
        return pltpu.make_async_copy(
            gu.at[pl.ds(al(j * C * R), C * R)], gu_h.at[pl.ds(al(j * C * R), C * R)], gsem.at[j]
        )

    def hidden(j, _):
        gu[pl.ds(al(j * C * R), C * R), :] = dg(
            cot[...], wd[pl.ds(al(j * D), D), :], NT
        ).astype(bf16)
        gu_copy(j).start()
        return 0

    J = wd.shape[0] // D

    def far(q):
        for c in rel[q]:
            c.wait_recv()
        kv(q, pd)
        for i, (v, h) in enumerate(((n1, n1_h), (k_v, k_h), (v_v, v_h))):
            pltpu.make_async_copy(
                v.at[pl.ds(q * T, T)], h.at[pl.ds(q * T, T)], osem.at[3 + 3 * q + i]
            ).start()

    onward(0)
    for c in wc[3:]:
        c.wait()
    lax.fori_loop(0, J // 2, hidden, 0)
    near(0)
    lax.fori_loop(J // 2, J, hidden, 0)
    onward(1)
    for c in own[2]:
        c.start()
    near(1)
    far(0)

    lane = lax.broadcasted_iota(jnp.int32, (1, 128), 1)
    lo = lane < 64
    col = lax.broadcasted_iota(jnp.int32, (1, T), 1)

    def e_copy(t):
        return pltpu.make_async_copy(e_v.at[t % 2], e_h.at[t], esem.at[t % 2])

    def pair(t, _):
        q, p = t // pairs, t % pairs

        @pl.when(t == pairs)
        def _():
            far(1)
            onward(2)

        @pl.when(t == 2 * pairs)
        def _():
            near(2)
            far(2)

        off = al(p * 128, 128)
        rq = pl.ds(al(q * R), R)
        rk = pl.ds(al(q * T), T)
        qp = q_v[rq, pl.ds(off, 128)]
        zero = jnp.zeros_like(qp)
        qs = jnp.concatenate([jnp.where(lo, qp, zero), jnp.where(lo, zero, qp)], 0)
        bias = jnp.where(col < len_s[q], 0.0, masked_score).astype(f32)
        s_v[...] = dg(qs, k_v[rk, pl.ds(off, 128)], NT) + bias
        m = jnp.max(s_v[...], axis=1, keepdims=True)
        e = jnp.exp2(s_v[...] - m)
        eb = e.astype(bf16)
        tot = jnp.sum(e, axis=1, keepdims=True)

        @pl.when(t >= 2)
        def _():
            e_copy(t - 2).wait()

        e_v[t % 2] = eb
        e_copy(t).start()
        ol = dg(eb, v_v[rk, pl.ds(off, 128)], NN)
        inv = 1.0 / tot
        inv = jnp.where(lo, inv[:R], inv[R:])
        li_v[rq, pl.ds(off, 128)] = inv
        a_v[rq, pl.ds(off, 128)] = (jnp.where(lo, ol[:R], ol[R:]) * inv).astype(bf16)
        return 0

    lax.fori_loop(0, C * pairs, pair, 0)
    ac = pltpu.make_async_copy(a_v, a_h, osem.at[1])
    lc = pltpu.make_async_copy(li_v, li_h, osem.at[2])
    ac.start()
    lc.start()
    e_copy(C * pairs - 2).wait()
    e_copy(C * pairs - 1).wait()
    for q in range(C):
        for i, (v, h) in enumerate(((n1, n1_h), (k_v, k_h), (v_v, v_h))):
            pltpu.make_async_copy(
                v.at[pl.ds(q * T, T)], h.at[pl.ds(q * T, T)], osem.at[3 + 3 * q + i]
            ).wait()
        for c in own[q] + rel[q]:
            c.wait_send()
    for j in range(J):
        gu_copy(j).wait()
    qc.wait()
    ac.wait()
    lc.wait()


def attend(C, R, D, S, FF, x, cot, lengths, vecs, wq, wk, wv, wd):
    N, T, pairs = C * R, R * S, D // 128
    sd = jax.ShapeDtypeStruct
    dma = pltpu.SemaphoreType.DMA
    return pl.pallas_call(
        functools.partial(attend_kernel, C, R, D, S),
        out_shape=(
            sd((C * T, D), bf16),
            sd((N, D), bf16),
            sd((C * T, D), bf16),
            sd((C * T, D), bf16),
            sd((N, D), bf16),
            sd((N, D), f32),
            sd((C * pairs, 2 * R, T), bf16),
            sd((FF // D * N, D), bf16),
        ),
        in_specs=[ANY, ANY, SM] + [VM] * 4 + [ANY] * 4,
        out_specs=(ANY,) * 8,
        scratch_shapes=[
            pltpu.VMEM((N, D), bf16),
            pltpu.VMEM((C * T, D), bf16),
            pltpu.VMEM((D, D), bf16),
            pltpu.VMEM((D, D), bf16),
            pltpu.VMEM((D, D), bf16),
            pltpu.VMEM((N, D), bf16),
            pltpu.VMEM((C * T, D), bf16),
            pltpu.VMEM((C * T, D), bf16),
            pltpu.VMEM((N, D), bf16),
            pltpu.VMEM((N, D), f32),
            pltpu.VMEM((2, 2 * R, T), bf16),
            pltpu.VMEM((2 * R, T), f32),
            pltpu.VMEM((N, D), bf16),
            pltpu.VMEM((FF, D), bf16),
            pltpu.VMEM((FF // D * N, D), bf16),
            dma((C + 5,)),
            dma((3 + 3 * C,)),
            dma((2,)),
            dma((FF // D,)),
            dma((4, C)),
            dma((4, C)),
            dma((2, C)),
            dma((2, C)),
        ],
        compiler_params=pltpu.CompilerParams(
            collective_id=1, has_side_effects=True, vmem_limit_bytes=60 * 2**20
        ),
        cost_estimate=pl.CostEstimate(
            flops=20 * 10**9, bytes_accessed=40 * 10**6, transcendentals=0
        ),
    )(x, cot, lengths, *vecs, wq, wk, wv, wd)


SCHEDULE = {
    "w1": ((2, 0),),
    "f30": ((2, 1),),
    "u3": ((3, 0),),
    "w3": ((2, 2),),
    "s0": ((2, 3),),
    "s1": ((1, 4),),
    "s2": ((3, 1), (1, 7),),
    "wo": ((1, 6), (2, 4), (1, 5), (4, 0),),
    "t0": ((2, 7), (3, 2),),
    "t1": ((1, 8),),
    "t3": ((5, 0), (2, 5), (3, 3), (4, 1), (2, 8),),
    "t6": ((3, 7), (6, 0), (5, 1),),
    "t9": ((3, 4),),
    "t11": ((4, 3),),
    "d12": ((4, 2), (3, 5),),
    "d13": ((7, 0),),
    "t12": ((6, 1), (2, 6),),
    "t16": ((4, 4), (8, 0),),
    "t17": ((5, 2),),
    "d21": ((5, 3),),
    "k": ((1, 9), (3, 8), (4, 5), (7, 1), (2, 9),),
    "v": ((1, 10), (3, 6),),
    "o0": ((5, 5), (1, 11), (2, 10), (2, 11), (3, 9), (6, 2),),
    "o1": ((5, 4), (4, 6), (4, 7), (4, 8), (3, 10), (4, 9), (3, 11), (7, 2), (5, 6),),
    "o2": ((4, 10), (5, 7), (4, 11),),
    "end0": ((5, 8), (5, 9),),
    "end1": ((5, 10), (5, 11), (8, 2), (8, 1),),
}


def backward_kernel(
    C, R, D, S, FF,
    x_h, cot_h, a_h, li_h, q_h, k_h, v_h, n1_h, e_h, gu_h,
    g1_r, s1_r, bo_r, g2_r, s2_r, bd_r, bu_r, wo_h, wu_h, wd_h, wq_h, wk_h, wv_h,
    out_h, ig_h, f_h, sm_h, p_h,
    cot, a_v, q_v, n2, pb, du, h_v, acc, dn2, kk, vv, n1, wk, wv, wo, gb, dn, e_v, sm,
    rc, r2, r3, s3, r4, f, d1, d2, mc, mz, mx, bup,
    lsem, esem, osem, psem, sems, rems, zs, zr, ds_s, ds_r, ms, mr, cr,
):
    T, N = R * S, C * R
    pairs = D // 128
    J = FF // D
    B = 8
    CH = D // B
    s, b, px, py, pd = places()
    y, x = s // 2, s % 2
    z, c = b // 2, b % 2
    sib = z * 2 + 1 - c
    t_rows = C * T
    HC, HR = CH // 2, R // 2
    U = 2 * J + 4
    bar = pltpu.get_barrier_semaphore()
    beside = [(px, b), (py, b), (s, sib)] + [(s, (z + k) % 4 * 2 + c) for k in (1, 2, 3)]
    for o in beside:
        pl.semaphore_signal(bar, 1, device_id=o, device_id_type=MESH)

    def remote(src, dst, ss, rs, dev):
        return pltpu.make_async_remote_copy(
            src, dst, ss, rs, device_id=dev, device_id_type=MESH
        )

    def slot(u):
        return u - 2 * J * (u // (2 * J))

    def mine(u):
        return x + (u % 2) * (y - x)

    def first_peer(u):
        return px + (u % 2) * (py - px)

    def last_peer(u):
        return py + (u % 2) * (px - py)

    def half(h):
        return pl.ds(al(h * HC), HC)

    def cp1(u):
        return remote(gb.at[slot(u), :, 1 - c], rc.at[u % 4], sems.at[0, u], rems.at[0, u], (s, sib))

    def cp2(u):
        return remote(
            gb.at[slot(u), :, c, half(1 - mine(u))], r2.at[slot(u)], sems.at[1, u], rems.at[1, u],
            (first_peer(u), b),
        )

    def cp3(u, k):
        zz = (z + k) % 4
        return remote(
            gb.at[slot(u), zz, c, half(mine(u))], r3.at[u, k - 1], zs.at[k - 1, u], zr.at[k - 1, u],
            (s, zz * 2 + c),
        )

    def cp4(u):
        return remote(s3.at[u % 4], r4.at[u], sems.at[2, u], rems.at[2, u], (last_peer(u), b))

    def cp5(u):
        ref = f.at[u, half(mine(u))]
        return remote(ref, ref, sems.at[3, u], rems.at[3, u], (first_peer(u), b))

    def sent(u):
        cp1(u).wait_send()
        cp2(u).wait_send()
        for k in (1, 2, 3):
            cp3(u, k).wait_send()

    def step1(u, again):
        if again:
            pl.semaphore_wait(cr.at[u % 4], 1)
        cp1(u).start()

    def step2(u, more):
        cp1(u).wait_recv()
        gb[slot(u), :, c] += rc[u % 4]
        if more:
            pl.semaphore_signal(cr.at[u % 4], 1, device_id=(s, sib), device_id_type=MESH)
        cp2(u).start()

    def step3(u):
        cp2(u).wait_recv()
        gb[slot(u), :, c, half(mine(u))] += r2[slot(u)]
        for k in (1, 2, 3):
            cp3(u, k).start()

    def step4(u):
        for k in (1, 2, 3):
            cp3(u, k).wait_recv()
        if isinstance(u, int):
            if u >= 4:
                cp4(u - 4).wait_send()
        else:

            @pl.when(u >= 4)
            def _():
                cp4(u - 4).wait_send()

        v = gb[slot(u), z, c, half(mine(u))].astype(f32)
        for k in range(3):
            v += r3[u, k].astype(f32)
        s3[u % 4] = v.astype(bf16)
        cp4(u).start()

    def step5(u):
        cp4(u).wait_recv()
        f[u, half(mine(u))] = s3[u % 4] + r4[u]
        cp5(u).start()

    def dcp(q, i):
        sl = q % 2
        if i == 0:
            a, o, dev = dn.at[sl, :, 1 - x, pl.ds(0, HR)], d1.at[sl, 0], px
        elif i == 1:
            a, o, dev = dn.at[sl, 1 - y, :, pl.ds(HR, HR)], d1.at[sl, 1], py
        elif i == 2:
            a, o, dev = dn.at[sl, 1 - y, x, pl.ds(0, HR)], d2.at[q, 0], py
        else:
            a, o, dev = dn.at[sl, y, 1 - x, pl.ds(HR, HR)], d2.at[q, 1], px
        return remote(a, o, ds_s.at[i, q], ds_r.at[i, q], (dev, b))

    def rows1(q):
        dcp(q, 0).start()
        dcp(q, 1).start()

    def rows2(q):
        sl = q % 2
        dcp(q, 0).wait_recv()
        dcp(q, 1).wait_recv()
        dn[sl, :, x, 0:HR] += d1[sl, 0]
        dn[sl, y, :, HR:R] += d1[sl, 1]
        dcp(q, 2).start()
        dcp(q, 3).start()

    def rows3(q):
        sl = q % 2
        dcp(q, 2).wait_recv()
        dcp(q, 3).wait_recv()
        for i in range(2):
            d = dn[sl, y, x, i * HR : (i + 1) * HR].astype(f32) + d2[q, i].astype(f32)
            r = pl.ds(al(q * R + i * HR), HR)
            zz, rr = row_norm(n2[r, :].astype(f32))
            g = d * gain1
            pb[r, :] = (
                h_v[r, :]
                + rr
                * (
                    g
                    - jnp.mean(g, axis=-1, keepdims=True)
                    - zz * jnp.mean(g * zz, axis=-1, keepdims=True)
                )
            ).astype(bf16)


    def emit(name):
        for k, u in SCHEDULE.get(name, ()):
            if k == 1:
                step1(u, True)
            elif k == 2:
                if u >= 2 * J:
                    if u == 2 * J:
                        cp5(0).wait_recv()
                    step2(u, False)
                else:
                    step2(u, True)
            else:
                {3: step3, 4: step4, 5: step5, 6: rows1, 7: rows2, 8: rows3}[k](u)

    def emit_when(names):
        for name, cond in names:
            if name in SCHEDULE:
                pl.when(cond)(functools.partial(emit, name))

    def load(i, h, v):
        cp = pltpu.make_async_copy(h, v, lsem.at[i])
        cp.start()
        return cp

    c_a = load(0, a_h, a_v)
    c_wo = load(1, wo_h, wo)
    c_x = load(2, x_h, du)
    c_cot = load(3, cot_h, cot)
    def e_copy(t, slot):
        return pltpu.make_async_copy(e_h.at[t], e_v.at[slot], esem.at[slot])


    gain1, shift1, b_out, gain2, shift2, b_down = (
        row(r) for r in (g1_r, s1_r, bo_r, g2_r, s2_r, bd_r)
    )
    for j in range(J):
        bup[j : j + 1, :] = bu_r[j * D : (j + 1) * D].astype(f32).reshape(1, D)
    sm[...] = jnp.zeros_like(sm)
    for w in (c_a, c_wo, c_x, c_cot):
        w.wait()
    c_w = [
        (
            load(4 + 2 * j, wu_h.at[:, pl.ds(j * D, D)], vv.at[pl.ds(j * D, D)]),
            load(5 + 2 * j, gu_h.at[pl.ds(j * N, N)], kk.at[pl.ds(j * N, N)]),
        )
        for j in range(J)
    ]
    n0 = 4 + 2 * J
    c_q = load(n0, q_h, q_v)
    c_n1 = load(n0 + 1, n1_h, n1)
    c_wk = load(n0 + 2, wk_h, wk)
    c_wv = load(n0 + 3, wv_h, wv)
    e_copy(0, 0).start()
    e_copy(1, 1).start()

    def first(i, _):
        r = pl.ds(al(i * R), R)
        h = du[r, :].astype(f32) + dg(a_v[r, :], wo[...], NN) + b_out
        h_v[r, :] = h
        zn, _r = row_norm(h)
        n2[r, :] = (zn * gain2 + shift2).astype(bf16)
        acc[r, :] = h + b_down
        dn2[r, :] = jnp.zeros((R, D), f32)
        sm[7:8, :] += jnp.sum(cot[r, :].astype(f32), axis=0, keepdims=True)
        return 0

    lax.fori_loop(0, C, first, 0)
    pl.semaphore_wait(bar, len(beside))

    def p_copy(j):
        return pltpu.make_async_copy(
            kk.at[pl.ds(al(j * N), N)], p_h.at[pl.ds(al(j * N), N)], psem.at[j]
        )

    def ffn(j, _):
        jr = pl.ds(al(j * D), D)
        for jj in range(J):

            @pl.when(j == jj)
            def _():
                c_w[jj][0].wait()
                c_w[jj][1].wait()

        bias = bup[pl.ds(j, 1), :]

        def chunk(i, sums):
            emit_when(
                (f"f{jj}{ii}", (j == jj) & (i == ii)) for jj in range(J) for ii in range(C)
            )
            r = pl.ds(al(i * R), R)
            u = dg(n2[r, :], vv[jr, :], NN) + bias
            rj = pl.ds(al(j * N + i * R), R)
            g = kk[rj, :].astype(f32)
            u2 = u * u
            t = jnp.tanh(u * (GC0 + GC1 * u2))
            hu = 0.5 * u
            half = 0.5 + 0.5 * t
            p = (u * half).astype(bf16)
            d = (g * (half + hu * (1.0 - t * t) * (GC0 + 3.0 * GC1 * u2))).astype(bf16)
            kk[rj, :] = p
            du[r, :] = d
            dn2[r, :] += dg(d, vv[jr, :], NT)
            return sums + jnp.sum(d.astype(f32), axis=0, keepdims=True)

        dj = lax.fori_loop(0, C, chunk, jnp.zeros((1, D), f32))
        sm[pl.ds(8 + j, 1), :] = dj
        emit_when((f"u{jj}", j == jj) for jj in range(J))
        gb[j] = dg(n2[...], du[...], TN).astype(bf16).reshape(B // 2, 2, CH, D)
        step1(j, False)
        emit_when((f"w{jj}", j == jj) for jj in range(J))
        per = FF // B
        pt = kk.at[pl.ds(al(j * N), N)]
        for bb in range(D // per):
            gw = dg(pt[:, bb * per : (bb + 1) * per], cot[...], TN).astype(bf16)
            for i in range(per // CH):
                gb[J + i, j, bb] = gw[i * CH : (i + 1) * CH, :]
        p_copy(j).start()
        return 0

    lax.fori_loop(0, J, ffn, 0)

    c_v = load(1, v_h, vv.at[pl.ds(0, t_rows)])

    for j in range(J):
        p_copy(j).wait()
    c_k = load(0, k_h, kk.at[pl.ds(0, t_rows)])

    def second(i, _):
        emit_when((f"s{ii}", i == ii) for ii in range(C))
        r = pl.ds(al(i * R), R)
        zn, rr = row_norm(h_v[r, :])
        dnn = dn2[r, :]
        g = dnn * gain2
        sm[5:6, :] += jnp.sum(dnn * zn, axis=0, keepdims=True)
        sm[6:7, :] += jnp.sum(dnn, axis=0, keepdims=True)
        dh = cot[r, :].astype(f32) + rr * (
            g
            - jnp.mean(g, axis=-1, keepdims=True)
            - zn * jnp.mean(g * zn, axis=-1, keepdims=True)
        )
        h_v[r, :] = dh
        db = dh.astype(bf16)
        n2[r, :] = db
        sm[4:5, :] += jnp.sum(db.astype(f32), axis=0, keepdims=True)
        du[r, :] = dg(db, wo[...], NT).astype(bf16)
        return 0

    lax.fori_loop(0, C, second, 0)
    c_li = load(2, li_h, dn2)
    emit("wo")
    sent(0)
    c_wq = load(3, wq_h, wo)
    gb[slot(2 * J)] = dg(a_v[...], n2[...], TN).astype(bf16).reshape(B // 2, 2, CH, D)

    c_x = load(4, x_h, n2)
    emit("kw")
    for w in (c_x, c_k, c_v, c_li, c_q, c_wk, c_wv, c_wq, c_n1):
        w.wait()
    dq_v, do_v = cot, du
    lane = lax.broadcasted_iota(jnp.int32, (1, 128), 1)
    lo = lane < 64

    def stack(v):
        zero = jnp.zeros_like(v)
        return jnp.concatenate([jnp.where(lo, v, zero), jnp.where(lo, zero, v)], 0)

    def pair(t, _):
        q, p = t // pairs, t % pairs
        slot = t % 2
        emit_when((f"t{tt}", t == tt) for tt in range(C * pairs))
        lanes = pl.ds(al(p * 128, 128), 128)
        rq = pl.ds(al(q * R), R)
        rk = pl.ds(al(q * T), T)
        qs = stack(q_v[rq, lanes])
        dof = do_v[rq, lanes].astype(f32) * dn2[rq, lanes]
        dos = stack(dof.astype(bf16))
        dl = jnp.sum(stack(dof * a_v[rq, lanes].astype(f32)), axis=1, keepdims=True)
        e_copy(t, slot).wait()
        dp = dg(dos, vv[rk, lanes], NT)
        ds = (e_v[slot].astype(f32) * (dp - dl)).astype(bf16)
        dqs = dg(ds, kk[rk, lanes], NN)
        dq_v[rq, lanes] = (jnp.where(lo, dqs[:R], dqs[R:]) * (HEAD_DIM ** (-0.5))).astype(
            bf16
        )
        kk[rk, lanes] = (dg(qs, ds, TN) * (1.0 / LOG2E)).astype(bf16).T
        vv[rk, lanes] = dg(dos, e_v[slot], TN).astype(bf16).T

        @pl.when(t + 2 < C * pairs)
        def _():
            e_copy(t + 2, slot).start()

        @pl.when(p == pairs - 1)
        def _():
            @pl.when(q == 2)
            def _():
                for i in range(4):
                    dcp(0, i).wait_send()

            def put(blk, more):
                rr = pl.ds(al((q * S + blk) * R), R)
                d = dg(kk[rr, :], wk[...], NT) + dg(vv[rr, :], wv[...], NT)
                if more:
                    d += dg(dq_v[rq, :], wo[...], NT)
                n = n1[rr, :].astype(f32)
                sm[0:1, :] += jnp.sum(d * n, axis=0, keepdims=True)
                sm[1:2, :] += jnp.sum(d, axis=0, keepdims=True)
                dn[q % 2, blk // 2, blk % 2] = d.astype(bf16)

            def others(i, _):
                emit_when(
                    (f"d{qq}{ii}", (q == qq) & (i == ii)) for qq in range(C) for ii in range(S - 1)
                )
                put((s + 1 + i) % S, False)
                return 0

            lax.fori_loop(0, S - 1, others, 0)
            emit_when((f"d{qq}{S - 1}", q == qq) for qq in range(C))
            put(s, True)

        return 0

    lax.fori_loop(0, C * pairs, pair, 0)
    for u in (1, 2, 3):
        sent(u)
        cp5(u).wait_recv()
    for i in range(C):
        r = pl.ds(i * R, R)
        a_v[r, :] = n1[pl.ds(al((i * S + s) * R), R), :]
    q_u, k_u, v_u = 2 * J + 1, 2 * J + 2, 2 * J + 3
    emit("q")
    gb[slot(q_u)] = dg(a_v[...], dq_v[...], TN).astype(bf16).reshape(B // 2, 2, CH, D)
    sm[2:3, :] = jnp.sum(dq_v[...].astype(f32), axis=0, keepdims=True)
    sm[3:4, :] = jnp.sum(vv[0:t_rows, :].astype(f32), axis=0, keepdims=True)
    sm[0:1, :] = (sm[0:1, :] - shift1 * sm[1:2, :]) / gain1

    def mcp(i, src, dst, dev):
        return remote(src, dst, ms.at[i], mr.at[i], dev)

    m1 = mcp(0, sm, mc.at[0], (s, sib))
    m1.start()
    emit("k")
    for i in range(2):
        gb[slot(k_u), 2 * i : 2 * i + 2] = (
            dg(n1[:, i * (D // 2) : (i + 1) * (D // 2)], kk[0:t_rows, :], TN)
            .astype(bf16)
            .reshape(2, 2, CH, D)
        )
    m1.wait()
    mz[0] = sm[...] + mc[0]
    m2 = [mcp(k, mz.at[0], mz.at[k], (s, (z + k) % 4 * 2 + c)) for k in (1, 2, 3)]
    for m in m2:
        m.start()
    c_wd = load(0, wd_h, kk)
    emit("v")
    for i in range(2):
        gb[slot(v_u), 2 * i : 2 * i + 2] = (
            dg(n1[:, i * (D // 2) : (i + 1) * (D // 2)], vv[0:t_rows, :], TN)
            .astype(bf16)
            .reshape(2, 2, CH, D)
        )
    c_p = load(1, p_h, n1)
    emit("o0")
    c_wd.wait()
    c_p.wait()

    def last(i):
        r = pl.ds(al(i * R), R)
        o = acc[r, :]
        for j in range(J):
            o += dg(n1[pl.ds(al(j * N + i * R), R), :], kk[j * D : (j + 1) * D, :], NN)
        q_v[r, :] = o.astype(bf16)

    last(0)
    emit("o1")
    for m in m2:
        m.wait()
    mx[0] = (mz[0] + mz[1]) + (mz[2] + mz[3])
    m3 = mcp(4, mx.at[0], mx.at[1], (px, b))
    m3.start()
    last(1)
    emit("o2")
    m3.wait()
    mx[2] = mx[0] + mx[1]
    m4 = mcp(5, mx.at[2], mx.at[3], (py, b))
    m4.start()
    last(2)
    c_o = pltpu.make_async_copy(q_v, out_h, osem.at[0])
    c_o.start()
    emit("end0")
    m4.wait()
    sm[...] = mx[2] + mx[3]
    c_s = pltpu.make_async_copy(sm, sm_h, osem.at[2])
    c_s.start()
    emit("end1")
    c_i = pltpu.make_async_copy(pb, ig_h, osem.at[1])
    c_i.start()
    emit("end2")
    for u in range(U):
        if u > 3:
            cp5(u).wait_recv()
    c_f = pltpu.make_async_copy(f, f_h, osem.at[3])
    c_f.start()
    for u in range(U):
        if u > 3:
            sent(u)
        if u >= 2 * J:
            cp4(u).wait_send()
        cp5(u).wait_send()
    for q in (1, 2):
        for i in range(4):
            dcp(q, i).wait_send()
    for o in (c_o, c_i, c_s, c_f):
        o.wait()


def backward(C, R, D, S, FF, x, cot, a, li, q, k, v, n1, e, gu, vecs, wo, wu, wd, wq, wk, wv):
    N, T = C * R, R * S
    J = FF // D
    U, CH = 2 * J + 4, D // 8
    sd = jax.ShapeDtypeStruct
    dma = pltpu.SemaphoreType.DMA
    vm = pltpu.VMEM
    return pl.pallas_call(
        functools.partial(backward_kernel, C, R, D, S, FF),
        out_shape=(
            sd((N, D), bf16),
            sd((N, D), bf16),
            sd((U, D // 8, D), bf16),
            sd((16, D), f32),
            sd((J * N, D), bf16),
        ),
        in_specs=[ANY] * 10 + [VM] * 7 + [ANY] * 6,
        out_specs=(ANY,) * 5,
        scratch_shapes=[
            vm((N, D), bf16), vm((N, D), bf16), vm((N, D), bf16),
            vm((N, D), bf16), vm((N, D), bf16), vm((N, D), bf16),
            vm((N, D), f32), vm((N, D), f32), vm((N, D), f32),
            vm((FF, D), bf16), vm((FF, D), bf16), vm((C * T, D), bf16),
            vm((D, D), bf16), vm((D, D), bf16), vm((D, D), bf16),
            vm((2 * J, 4, 2, CH, D), bf16), vm((2, 2, 2, R, D), bf16),
            vm((2, 2 * R, T), bf16), vm((16, D), f32),
            vm((4, 4, CH, D), bf16), vm((2 * J, 4, CH // 2, D), bf16), vm((U, 3, CH // 2, D), bf16),
            vm((4, CH // 2, D), bf16), vm((U, CH // 2, D), bf16), vm((U, CH, D), bf16),
            vm((2, 2, 2, R // 2, D), bf16), vm((C, 2, R // 2, D), bf16),
            vm((1, 16, D), f32), vm((4, 16, D), f32), vm((4, 16, D), f32), vm((J, D), f32),
            dma((4 + 2 * J + 4,)), dma((2,)), dma((4,)), dma((J,)),
            dma((4, U)), dma((4, U)), dma((3, U)), dma((3, U)),
            dma((4, C)), dma((4, C)), dma((6,)), dma((6,)),
            pltpu.SemaphoreType.REGULAR((4,)),
        ],
        compiler_params=pltpu.CompilerParams(
            collective_id=2, has_side_effects=True, vmem_limit_bytes=(64 * 2**20) - 2**17
        ),
        cost_estimate=pl.CostEstimate(
            flops=40 * 10**9, bytes_accessed=60 * 10**6, transcendentals=0
        ),
    )(x, cot, a, li, q, k, v, n1, e, gu, *vecs, wo, wu, wd, wq, wk, wv)


def finish_kernel(D, FF, f_h, sm, out_h, ig_h, *rest):
    o_out, o_ig, g1, s1, wq, bq, wk, wv, bv, wo, bo, g2, s2, wu, bu, wd, bd, f, v_out, v_ig, sem = rest
    J, CH = FF // D, D // 8
    c1 = pltpu.make_async_copy(f_h, f, sem.at[0])
    c2 = pltpu.make_async_copy(out_h, v_out, sem.at[1])
    c3 = pltpu.make_async_copy(ig_h, v_ig, sem.at[2])
    for c in (c1, c2, c3):
        c.start()
    b = lax.axis_index("batch")
    c2.wait()
    c4 = pltpu.make_async_copy(v_out, o_out, sem.at[1])
    c4.start()
    c3.wait()
    c5 = pltpu.make_async_copy(v_ig, o_ig, sem.at[2])
    c5.start()
    rolled = pltpu.roll(sm[0:8, :], (8 - b) % 8 * CH, 1)
    for i, o in enumerate((g1, s1, bq, bv, bo, g2, s2, bd)):
        o[...] = rolled[i, :CH]
    per = FF // 8
    half = D // per
    up = sm[8 : 8 + J, :]
    here = lax.broadcasted_iota(jnp.int32, (J, 1), 0) == b // half
    up = jnp.sum(jnp.where(here, up, 0.0), axis=0, keepdims=True)
    up = jnp.where(b % half == 0, up[:, :per], up[:, per:])
    bu[...] = up[0]
    c1.wait()
    for j in range(J):
        wu[:, j * D : (j + 1) * D] = f[j].astype(f32)
        wd[j * CH : (j + 1) * CH, :] = f[J + j].astype(f32)
    for i, o in enumerate((wo, wq, wk, wv)):
        o[...] = f[2 * J + i].astype(f32)
    c4.wait()
    c5.wait()


def finish(D, FF, f, sm, out, ig):
    sd = jax.ShapeDtypeStruct
    CH = D // 8
    row, mat = sd((CH,), f32), sd((CH, D), f32)
    return pl.pallas_call(
        functools.partial(finish_kernel, D, FF),
        out_shape=(
            sd(out.shape, bf16), sd(ig.shape, bf16), row, row, mat, row, mat, mat, row, mat,
            row, row, row, sd((CH, FF), f32), sd((FF // 8,), f32), sd((FF // 8, D), f32), row,
        ),
        in_specs=[ANY, VM, ANY, ANY],
        out_specs=(ANY, ANY) + (VM,) * 15,
        scratch_shapes=[pltpu.VMEM(v.shape, bf16) for v in (f, out, ig)] + [pltpu.SemaphoreType.DMA((3,))],
        compiler_params=pltpu.CompilerParams(vmem_limit_bytes=62 * 2**20),
    )(f, sm, out, ig)


def fast_body(
    inputs, lengths, gain_one, shift_one, w_query, b_query, w_key, w_value, b_value, w_out, b_out,
    gain_two, shift_two, w_up, b_up, w_down, b_down, cotangent,
):
    C, R, D = inputs.shape
    S = lax.axis_size("seq")
    FF = w_up.shape[1]
    N = C * R
    x = inputs.reshape(N, D)
    cot = cotangent.reshape(N, D)
    n1, q, k, v, a, li, e, gu = attend(
        C, R, D, S, FF, x, cot, lengths, (gain_one, shift_one, b_query, b_value),
        w_query, w_key, w_value, w_down,
    )
    out, input_grad, g, sm, _ = backward(
        C, R, D, S, FF, x, cot, a, li, q, k, v, n1, e, gu,
        (gain_one, shift_one, b_out, gain_two, shift_two, b_down, b_up),
        w_out, w_up, w_down, w_query, w_key, w_value,
    )
    out, input_grad, *grads = finish(D, FF, g, sm, out, input_grad)
    return (out.reshape(inputs.shape), input_grad.reshape(inputs.shape), *grads)


def from_behind(x, axis, by):
    length = lax.axis_size(axis)
    return lax.ppermute(x, axis, [(i, (i + by) % length) for i in range(length)])


def normed(values, gain, offset):
    average = jnp.mean(values, axis=-1, keepdims=True)
    centred = values - average
    spread = jnp.mean(centred * centred, axis=-1, keepdims=True)
    return centred * lax.rsqrt(spread + norm_eps) * gain + offset


def outer_sum(left, right):
    return lax.dot_general(
        left, right, (((0,), (0,)), ((), ())), preferred_element_type=jnp.float32
    )


def back_dot(grad_rows, weight):
    return lax.dot_general(
        grad_rows, weight, (((1,), (1,)), ((), ())), preferred_element_type=jnp.float32
    )


def front_dot(rows_low, weight, bias):
    return jnp.dot(rows_low, weight, preferred_element_type=jnp.float32) + bias.astype(jnp.float32)


def column_sums(values):
    return jnp.sum(values.astype(jnp.float32), axis=0)


def key_valid(lengths, source, block_rows):
    positions = source * block_rows + jnp.arange(block_rows, dtype=jnp.int32)
    return (positions[None, :] < lengths[:, None])[:, None, None, :]


def block_scores(queries, key_block, valid):
    scores = jnp.einsum(
        "srhd,sthd->srht", queries, key_block, preferred_element_type=jnp.float32
    ) * HEAD_DIM ** (-0.5)
    return jnp.where(valid, scores, masked_score)


def ring_body(
    inputs,
    lengths,
    gain_one,
    shift_one,
    w_query,
    b_query,
    w_key,
    w_value,
    b_value,
    w_out,
    b_out,
    gain_two,
    shift_two,
    w_up,
    b_up,
    w_down,
    b_down,
    cotangent,
):
    cycle_size = lax.axis_size("seq")
    position = lax.axis_index("seq")
    count, block_rows, width = inputs.shape
    heads = width // HEAD_DIM
    total_rows = count * block_rows
    split_shape = (count, block_rows, heads, HEAD_DIM)
    scale = HEAD_DIM ** (-0.5)
    rows_in = inputs.astype(jnp.float32).reshape(total_rows, width)
    first_full, norm_one_pull = jax.vjp(
        normed, rows_in, gain_one.astype(jnp.float32), shift_one.astype(jnp.float32)
    )
    first = first_full.astype(jnp.bfloat16)
    queries = front_dot(first, w_query, b_query).astype(jnp.bfloat16).reshape(split_shape)
    key_rows = jnp.dot(first, w_key, preferred_element_type=jnp.float32).astype(jnp.bfloat16)
    value_rows = front_dot(first, w_value, b_value).astype(jnp.bfloat16)
    own_block = jnp.stack((key_rows, value_rows)).reshape((2,) + split_shape)
    running_max = jnp.full((count, block_rows, heads), masked_score, jnp.float32)
    running_total = jnp.zeros((count, block_rows, heads), jnp.float32)
    running_sum = jnp.zeros(split_shape, jnp.float32)
    moving = own_block
    for rotation in range(cycle_size):
        source = (position - rotation) % cycle_size
        valid = key_valid(lengths, source, block_rows)
        scores = block_scores(queries, moving[0], valid)
        new_max = jnp.maximum(running_max, jnp.max(scores, axis=-1))
        decay = jnp.exp(running_max - new_max)
        weights_exp = jnp.where(valid, jnp.exp(scores - new_max[..., None]), 0.0)
        running_total = running_total * decay + jnp.sum(weights_exp, axis=-1)
        running_sum = running_sum * decay[..., None] + jnp.einsum(
            "srht,sthd->srhd",
            weights_exp.astype(jnp.bfloat16),
            moving[1],
            preferred_element_type=jnp.float32,
        )
        running_max = new_max
        if rotation + 1 < cycle_size:
            moving = from_behind(moving, "seq", 1)
    attended = running_sum / running_total[..., None]
    log_total = running_max + jnp.log(running_total)
    attended_low = attended.reshape(total_rows, width).astype(jnp.bfloat16)
    middle = rows_in + front_dot(attended_low, w_out, b_out)
    second_full, norm_two_pull = jax.vjp(
        normed, middle, gain_two.astype(jnp.float32), shift_two.astype(jnp.float32)
    )
    second = second_full.astype(jnp.bfloat16)
    hidden = front_dot(second, w_up, b_up)
    gelu_value, gelu_pull = jax.vjp(jax.nn.gelu, hidden)
    active = gelu_value.astype(jnp.bfloat16)
    outputs = middle + front_dot(active, w_down, b_down)
    grad_rows_out = cotangent.astype(jnp.float32).reshape(total_rows, width)
    grad_ffn = cotangent.reshape(total_rows, width)
    grad_w_down = outer_sum(active, grad_ffn)
    grad_b_down = column_sums(grad_ffn)
    grad_hidden = gelu_pull(back_dot(grad_ffn, w_down))[0].astype(jnp.bfloat16)
    grad_w_up = outer_sum(second, grad_hidden)
    grad_b_up = column_sums(grad_hidden)
    grad_middle_part, grad_gain_two, grad_shift_two = norm_two_pull(back_dot(grad_hidden, w_up))
    grad_middle = grad_rows_out + grad_middle_part
    grad_branch = grad_middle.astype(jnp.bfloat16)
    grad_w_out = outer_sum(attended_low, grad_branch)
    grad_b_out = column_sums(grad_branch)
    grad_attended = back_dot(grad_branch, w_out).astype(jnp.bfloat16).reshape(split_shape)
    row_delta = jnp.sum(grad_attended.astype(jnp.float32) * attended, axis=-1)
    grad_queries = jnp.zeros(split_shape, jnp.float32)
    carried = jnp.zeros((2,) + split_shape, jnp.float32)
    moving = own_block
    for rotation in range(cycle_size):
        source = (position - rotation) % cycle_size
        valid = key_valid(lengths, source, block_rows)
        scores = block_scores(queries, moving[0], valid)
        probs = jnp.where(valid, jnp.exp(scores - log_total[..., None]), 0.0)
        grad_probs = jnp.einsum(
            "srhd,sthd->srht", grad_attended, moving[1], preferred_element_type=jnp.float32
        )
        grad_scores = (probs * (grad_probs - row_delta[..., None])).astype(jnp.bfloat16)
        grad_queries = (
            grad_queries
            + jnp.einsum(
                "srht,sthd->srhd", grad_scores, moving[0], preferred_element_type=jnp.float32
            )
            * scale
        )
        grad_keys_part = (
            jnp.einsum("srht,srhd->sthd", grad_scores, queries, preferred_element_type=jnp.float32)
            * scale
        )
        grad_values_part = jnp.einsum(
            "srht,srhd->sthd",
            probs.astype(jnp.bfloat16),
            grad_attended,
            preferred_element_type=jnp.float32,
        )
        carried = from_behind(
            (carried + jnp.stack((grad_keys_part, grad_values_part))).astype(jnp.bfloat16), "seq", 1
        ).astype(jnp.float32)
        if rotation + 1 < cycle_size:
            moving = from_behind(moving, "seq", 1)
    grad_keys = carried[0].reshape(total_rows, width).astype(jnp.bfloat16)
    grad_values = carried[1].reshape(total_rows, width).astype(jnp.bfloat16)
    grad_query_rows = grad_queries.reshape(total_rows, width).astype(jnp.bfloat16)
    grad_w_query = outer_sum(first, grad_query_rows)
    grad_b_query = column_sums(grad_query_rows)
    grad_w_key = outer_sum(first, grad_keys)
    grad_w_value = outer_sum(first, grad_values)
    grad_b_value = column_sums(grad_values)
    grad_first = (
        back_dot(grad_query_rows, w_query)
        + back_dot(grad_keys, w_key)
        + back_dot(grad_values, w_value)
    )
    grad_rows_part, grad_gain_one, grad_shift_one = norm_one_pull(grad_first)
    input_grad = grad_middle + grad_rows_part
    scattered = (
        lax.psum_scatter(
            grad_gain_one.astype(jnp.bfloat16), "batch", scatter_dimension=0, tiled=True
        ).astype(jnp.float32),
        lax.psum_scatter(
            grad_shift_one.astype(jnp.bfloat16), "batch", scatter_dimension=0, tiled=True
        ).astype(jnp.float32),
        lax.psum_scatter(
            grad_w_query.astype(jnp.bfloat16), "batch", scatter_dimension=0, tiled=True
        ).astype(jnp.float32),
        lax.psum_scatter(
            grad_b_query.astype(jnp.bfloat16), "batch", scatter_dimension=0, tiled=True
        ).astype(jnp.float32),
        lax.psum_scatter(
            grad_w_key.astype(jnp.bfloat16), "batch", scatter_dimension=0, tiled=True
        ).astype(jnp.float32),
        lax.psum_scatter(
            grad_w_value.astype(jnp.bfloat16), "batch", scatter_dimension=0, tiled=True
        ).astype(jnp.float32),
        lax.psum_scatter(
            grad_b_value.astype(jnp.bfloat16), "batch", scatter_dimension=0, tiled=True
        ).astype(jnp.float32),
        lax.psum_scatter(
            grad_w_out.astype(jnp.bfloat16), "batch", scatter_dimension=0, tiled=True
        ).astype(jnp.float32),
        lax.psum_scatter(
            grad_b_out.astype(jnp.bfloat16), "batch", scatter_dimension=0, tiled=True
        ).astype(jnp.float32),
        lax.psum_scatter(
            grad_gain_two.astype(jnp.bfloat16), "batch", scatter_dimension=0, tiled=True
        ).astype(jnp.float32),
        lax.psum_scatter(
            grad_shift_two.astype(jnp.bfloat16), "batch", scatter_dimension=0, tiled=True
        ).astype(jnp.float32),
        lax.psum_scatter(
            grad_w_up.astype(jnp.bfloat16), "batch", scatter_dimension=0, tiled=True
        ).astype(jnp.float32),
        lax.psum_scatter(
            grad_b_up.astype(jnp.bfloat16), "batch", scatter_dimension=0, tiled=True
        ).astype(jnp.float32),
        lax.psum_scatter(
            grad_w_down.astype(jnp.bfloat16), "batch", scatter_dimension=0, tiled=True
        ).astype(jnp.float32),
        lax.psum_scatter(
            grad_b_down.astype(jnp.bfloat16), "batch", scatter_dimension=0, tiled=True
        ).astype(jnp.float32),
    )
    summed = (
        lax.psum(scattered[0].astype(jnp.bfloat16), "seq").astype(jnp.float32),
        lax.psum(scattered[1].astype(jnp.bfloat16), "seq").astype(jnp.float32),
        lax.psum(scattered[2].astype(jnp.bfloat16), "seq").astype(jnp.float32),
        lax.psum(scattered[3].astype(jnp.bfloat16), "seq").astype(jnp.float32),
        lax.psum(scattered[4].astype(jnp.bfloat16), "seq").astype(jnp.float32),
        lax.psum(scattered[5].astype(jnp.bfloat16), "seq").astype(jnp.float32),
        lax.psum(scattered[6].astype(jnp.bfloat16), "seq").astype(jnp.float32),
        lax.psum(scattered[7].astype(jnp.bfloat16), "seq").astype(jnp.float32),
        lax.psum(scattered[8].astype(jnp.bfloat16), "seq").astype(jnp.float32),
        lax.psum(scattered[9].astype(jnp.bfloat16), "seq").astype(jnp.float32),
        lax.psum(scattered[10].astype(jnp.bfloat16), "seq").astype(jnp.float32),
        lax.psum(scattered[11].astype(jnp.bfloat16), "seq").astype(jnp.float32),
        lax.psum(scattered[12].astype(jnp.bfloat16), "seq").astype(jnp.float32),
        lax.psum(scattered[13].astype(jnp.bfloat16), "seq").astype(jnp.float32),
        lax.psum(scattered[14].astype(jnp.bfloat16), "seq").astype(jnp.float32),
    )
    return (
        outputs.astype(jnp.bfloat16).reshape(inputs.shape),
        input_grad.astype(jnp.bfloat16).reshape(inputs.shape),
        summed[0],
        summed[1],
        summed[2],
        summed[3],
        summed[4],
        summed[5],
        summed[6],
        summed[7],
        summed[8],
        summed[9],
        summed[10],
        summed[11],
        summed[12],
        summed[13],
        summed[14],
    )


def solution(mesh):
    placed = (
        P("batch", "seq", None),
        P("batch"),
        P(),
        P(),
        P(),
        P(),
        P(),
        P(),
        P(),
        P(),
        P(),
        P(),
        P(),
        P(),
        P(),
        P(),
        P(),
        P("batch", "seq", None),
    )
    small = mesh.shape["seq"] == 4 and mesh.shape["batch"] == 8
    body = fast_body if small else ring_body
    return jax.shard_map(
        body,
        mesh=mesh,
        in_specs=placed,
        out_specs=(
            P("batch", "seq", None),
            P("batch", "seq", None),
            P("batch"),
            P("batch"),
            P("batch", None),
            P("batch"),
            P("batch", None),
            P("batch", None),
            P("batch"),
            P("batch", None),
            P("batch"),
            P("batch"),
            P("batch"),
            P("batch", None),
            P("batch"),
            P("batch", None),
            P("batch"),
        ),
        check_vma=False,
    )
```

```python
import functools
import math

import jax
import jax.numpy as jnp
from jax import lax
from jax.experimental import pallas as pl
from jax.experimental.pallas import tpu as pltpu
from jax.sharding import PartitionSpec as P

HEAD_DIM = 64
norm_eps = 1e-05
masked_score = -1e30

bf16 = jnp.bfloat16
f32 = jnp.float32
MESH = pl.DeviceIdType.MESH
ANY = pl.BlockSpec(memory_space=pl.ANY)
VM = pl.BlockSpec(memory_space=pltpu.VMEM)
SM = pl.BlockSpec(memory_space=pltpu.SMEM)
NN = (((1,), (0,)), ((), ()))
NT = (((1,), (1,)), ((), ()))
TN = (((0,), (0,)), ((), ()))
LOG2E = math.log2(math.e)
GC0 = math.sqrt(2.0 / math.pi)
GC1 = GC0 * 0.044715


def dg(a, b, dims):
    return lax.dot_general(a, b, dims, preferred_element_type=f32)


def row(ref):
    return ref[...].astype(f32).reshape(1, ref.shape[0])


def al(i, m=16):
    return pl.multiple_of(i, m)


def places():
    s = lax.axis_index("seq")
    b = lax.axis_index("batch")
    y, x = s // 2, s % 2
    return s, b, y * 2 + (1 - x), (1 - y) * 2 + x, (1 - y) * 2 + (1 - x)


def row_norm(x):
    mean = jnp.mean(x, axis=-1, keepdims=True)
    c = x - mean
    r = lax.rsqrt(jnp.mean(c * c, axis=-1, keepdims=True) + norm_eps)
    return c * r, r


def attend_kernel(
    C, R, D, S,
    x_h, cot_h, len_s, g_r, s_r, bq_r, bv_r, wq_h, wk_h, wv_h, wd_h,
    n1_h, q_h, k_h, v_h, a_h, li_h, e_h, gu_h,
    x_v, n1, wq, wk, wv, q_v, k_v, v_v, a_v, li_v, e_v, s_v, cot, wd, gu,
    lsem, osem, esem, gsem, os, orr, rs, rr,
):
    T = R * S
    HR = R // 2
    pairs = D // 128
    s, b, px, py, pd = places()
    bar = pltpu.get_barrier_semaphore()
    for o in (px, py):
        pl.semaphore_signal(bar, 1, device_id=(o, b), device_id_type=MESH)
    xc = [
        pltpu.make_async_copy(
            x_h.at[pl.ds(i * R, R)], x_v.at[pl.ds(i * R, R)], lsem.at[i]
        )
        for i in range(C)
    ]
    for c in xc:
        c.start()
    wc = [
        pltpu.make_async_copy(h, v, lsem.at[C + i])
        for i, (h, v) in enumerate(((wk_h, wk), (wv_h, wv), (wq_h, wq), (cot_h, cot), (wd_h, wd)))
    ]
    for c in wc:
        c.start()

    def rows(q, blk, off, n):
        return pl.ds(al((q * S + blk) * R + off), n)

    def copy(q, peer, blk, off, ss, rs):
        ref = n1.at[rows(q, blk, off, HR)]
        return pltpu.make_async_remote_copy(
            ref, ref, ss, rs, device_id=(peer, b), device_id_type=MESH
        )

    own = [
        [
            copy(q, peer, s, off, os.at[i, q], orr.at[i, q])
            for i, (peer, off) in enumerate(((px, 0), (py, HR), (px, HR), (py, 0)))
        ]
        for q in range(C)
    ]
    rel = [
        [
            copy(q, peer, blk, off, rs.at[i, q], rr.at[i, q])
            for i, (peer, blk, off) in enumerate(((py, px, 0), (px, py, HR)))
        ]
        for q in range(C)
    ]

    gain, shift, bq, bv = (row(r) for r in (g_r, s_r, bq_r, bv_r))
    for q in range(C):
        xc[q].wait()
        z, _ = row_norm(x_v[q * R : (q + 1) * R, :].astype(f32))
        n1[rows(q, s, 0, R), :] = (z * gain + shift).astype(bf16)
        if q == 0:
            pl.semaphore_wait(bar, 2)
        if q < 2:
            for c in own[q]:
                c.start()
    for c in wc[:3]:
        c.wait()

    def kv(q, blk):
        rs = rows(q, blk, 0, R)
        v = n1[rs, :]
        k_v[rs, :] = dg(v, wk[...], NN).astype(bf16)
        v_v[rs, :] = (dg(v, wv[...], NN) + bv).astype(bf16)

    def own_rows(q, _):
        v = n1[rows(q, s, 0, R), :]
        q_v[pl.ds(al(q * R), R), :] = (
            (dg(v, wq[...], NN) + bq) * (HEAD_DIM ** (-0.5) * LOG2E)
        ).astype(bf16)
        kv(q, s)
        return 0

    lax.fori_loop(0, C, own_rows, 0)
    qc = pltpu.make_async_copy(q_v, q_h, osem.at[0])
    qc.start()

    def onward(q):
        for c in own[q][:2]:
            c.wait_recv()
        for c in rel[q]:
            c.start()

    def near(q):
        for c in own[q][2:]:
            c.wait_recv()
        lax.fori_loop(0, 2, lambda i, c: (kv(q, jnp.where(i == 0, px, py)), c)[1], 0)

    def gu_copy(j):
        return pltpu.make_async_copy(
            gu.at[pl.ds(al(j * C * R), C * R)], gu_h.at[pl.ds(al(j * C * R), C * R)], gsem.at[j]
        )

    def hidden(j, _):
        gu[pl.ds(al(j * C * R), C * R), :] = dg(
            cot[...], wd[pl.ds(al(j * D), D), :], NT
        ).astype(bf16)
        gu_copy(j).start()
        return 0

    J = wd.shape[0] // D

    def far(q):
        for c in rel[q]:
            c.wait_recv()
        kv(q, pd)
        for i, (v, h) in enumerate(((n1, n1_h), (k_v, k_h), (v_v, v_h))):
            pltpu.make_async_copy(
                v.at[pl.ds(q * T, T)], h.at[pl.ds(q * T, T)], osem.at[3 + 3 * q + i]
            ).start()

    onward(0)
    for c in wc[3:]:
        c.wait()
    lax.fori_loop(0, J // 2, hidden, 0)
    near(0)
    lax.fori_loop(J // 2, J, hidden, 0)
    onward(1)
    for c in own[2]:
        c.start()
    near(1)
    far(0)

    lane = lax.broadcasted_iota(jnp.int32, (1, 128), 1)
    lo = lane < 64
    col = lax.broadcasted_iota(jnp.int32, (1, T), 1)

    def e_copy(t, slot):
        return pltpu.make_async_copy(e_v.at[slot], e_h.at[t], esem.at[slot])

    def scores(t):
        q, p = t // pairs, t % pairs
        lanes = pl.ds(al(p * 128, 128), 128)
        qp = q_v[pl.ds(al(q * R), R), lanes]
        zero = jnp.zeros_like(qp)
        qs = jnp.concatenate([jnp.where(lo, qp, zero), jnp.where(lo, zero, qp)], 0)
        bias = jnp.where(col < len_s[q], 0.0, masked_score).astype(f32)
        return dg(qs, k_v[pl.ds(al(q * T), T), lanes], NT) + bias

    def weigh(t, slot):
        q, p = t // pairs, t % pairs
        lanes = pl.ds(al(p * 128, 128), 128)
        rq = pl.ds(al(q * R), R)
        m = jnp.max(s_v[slot], axis=1, keepdims=True)
        e = jnp.exp2(s_v[slot] - m)
        eb = e.astype(bf16)
        tot = jnp.sum(e, axis=1, keepdims=True)
        e_v[slot] = eb
        ol = dg(eb, v_v[pl.ds(al(q * T), T), lanes], NN)
        inv = 1.0 / tot
        inv = jnp.where(lo, inv[:R], inv[R:])
        li_v[rq, lanes] = inv
        a_v[rq, lanes] = (jnp.where(lo, ol[:R], ol[R:]) * inv).astype(bf16)

    def sequence(q, _):
        @pl.when(q == 1)
        def _():
            far(1)
            onward(2)

        @pl.when(q == 2)
        def _():
            near(2)
            far(2)

        s_v[0] = scores(q * pairs)

        def two(h, _):
            t = q * pairs + 2 * h

            @pl.when(t >= 2)
            def _():
                e_copy(t - 2, 0).wait()
                e_copy(t - 1, 1).wait()

            s_v[1] = scores(t + 1)
            weigh(t, 0)
            s_v[0] = scores(q * pairs + lax.rem(2 * h + 2, pairs))
            weigh(t + 1, 1)
            e_copy(t, 0).start()
            e_copy(t + 1, 1).start()
            return 0

        lax.fori_loop(0, pairs // 2, two, 0)
        return 0

    lax.fori_loop(0, C, sequence, 0)
    ac = pltpu.make_async_copy(a_v, a_h, osem.at[1])
    lc = pltpu.make_async_copy(li_v, li_h, osem.at[2])
    ac.start()
    lc.start()
    e_copy(C * pairs - 2, 0).wait()
    e_copy(C * pairs - 1, 1).wait()
    for q in range(C):
        for i, (v, h) in enumerate(((n1, n1_h), (k_v, k_h), (v_v, v_h))):
            pltpu.make_async_copy(
                v.at[pl.ds(q * T, T)], h.at[pl.ds(q * T, T)], osem.at[3 + 3 * q + i]
            ).wait()
        for c in own[q] + rel[q]:
            c.wait_send()
    for j in range(J):
        gu_copy(j).wait()
    qc.wait()
    ac.wait()
    lc.wait()


def attend(C, R, D, S, FF, x, cot, lengths, vecs, wq, wk, wv, wd):
    N, T, pairs = C * R, R * S, D // 128
    sd = jax.ShapeDtypeStruct
    dma = pltpu.SemaphoreType.DMA
    return pl.pallas_call(
        functools.partial(attend_kernel, C, R, D, S),
        out_shape=(
            sd((C * T, D), bf16),
            sd((N, D), bf16),
            sd((C * T, D), bf16),
            sd((C * T, D), bf16),
            sd((N, D), bf16),
            sd((N, D), f32),
            sd((C * pairs, 2 * R, T), bf16),
            sd((FF // D * N, D), bf16),
        ),
        in_specs=[ANY, ANY, SM] + [VM] * 4 + [ANY] * 4,
        out_specs=(ANY,) * 8,
        scratch_shapes=[
            pltpu.VMEM((N, D), bf16),
            pltpu.VMEM((C * T, D), bf16),
            pltpu.VMEM((D, D), bf16),
            pltpu.VMEM((D, D), bf16),
            pltpu.VMEM((D, D), bf16),
            pltpu.VMEM((N, D), bf16),
            pltpu.VMEM((C * T, D), bf16),
            pltpu.VMEM((C * T, D), bf16),
            pltpu.VMEM((N, D), bf16),
            pltpu.VMEM((N, D), f32),
            pltpu.VMEM((2, 2 * R, T), bf16),
            pltpu.VMEM((2, 2 * R, T), f32),
            pltpu.VMEM((N, D), bf16),
            pltpu.VMEM((FF, D), bf16),
            pltpu.VMEM((FF // D * N, D), bf16),
            dma((C + 5,)),
            dma((3 + 3 * C,)),
            dma((2,)),
            dma((FF // D,)),
            dma((4, C)),
            dma((4, C)),
            dma((2, C)),
            dma((2, C)),
        ],
        compiler_params=pltpu.CompilerParams(
            collective_id=1, has_side_effects=True, vmem_limit_bytes=60 * 2**20
        ),
        cost_estimate=pl.CostEstimate(
            flops=20 * 10**9, bytes_accessed=40 * 10**6, transcendentals=0
        ),
    )(x, cot, lengths, *vecs, wq, wk, wv, wd)


SCHEDULE = {
    "f11": ((1, 4),),
    "f12": ((2, 0),),
    "w1": ((2, 4),),
    "f21": ((1, 5),),
    "f22": ((2, 1),),
    "f30": ((3, 0),),
    "u3": ((2, 2),),
    "w3": ((2, 5),),
    "s0": ((3, 1),),
    "s1": ((2, 3),),
    "s2": ((1, 6), (4, 0),),
    "t0": ((2, 6), (3, 2),),
    "t1": ((1, 7),),
    "t3": ((4, 1),),
    "t4": ((3, 3),),
    "t5": ((2, 7),),
    "d00": ((5, 1), (5, 0),),
    "t6": ((6, 0), (10, 3), (10, 1), (10, 0), (10, 2), (3, 4),),
    "t8": ((1, 8),),
    "t11": ((4, 2), (2, 8),),
    "d11": ((4, 4), (3, 5),),
    "d12": ((4, 3), (7, 0),),
    "t12": ((6, 1), (3, 6),),
    "t16": ((5, 3),),
    "q": ((5, 2),),
    "k": ((1, 9), (3, 8), (4, 5), (4, 6), (3, 7), (2, 9),),
    "v": ((1, 10), (7, 1),),
    "d20": ((2, 10), (5, 6), (1, 11), (5, 4), (8, 0), (3, 9), (2, 11),),
    "o0": ((6, 2), (3, 10),),
    "o1": ((3, 11), (4, 8), (5, 5), (4, 7), (4, 10), (4, 9), (7, 2),),
    "o2": ((5, 7), (8, 1), (4, 11), (5, 10), (5, 9), (5, 8),),
    "end0": ((8, 2),),
    "end2": ((5, 11),),
}


def backward_kernel(
    C, R, D, S, FF,
    x_h, cot_h, a_h, li_h, q_h, k_h, v_h, n1_h, e_h, gu_h,
    g1_r, s1_r, bo_r, g2_r, s2_r, bd_r, bu_r, wo_h, wu_h, wd_h, wq_h, wk_h, wv_h,
    out_h, ig_h, f_h, sm_h, p_h,
    cot, a_v, q_v, n2, du, h_v, acc, dn2, kk, vv, n1, wk, wv, wo, gb, dn, e_v, sm,
    rc, r2, r3, s3, r4, f, d1, d2, mc, mz, mx, bup,
    lsem, esem, osem, psem, tsem, trem, sems, rems, zs, zr, ds_s, ds_r, ms, mr, cr,
):
    T, N = R * S, C * R
    pairs = D // 128
    J = FF // D
    B = 8
    CH = D // B
    s, b, px, py, pd = places()
    y, x = s // 2, s % 2
    z, c = b // 2, b % 2
    sib = z * 2 + 1 - c
    t_rows = C * T
    HC, HR = CH // 2, R // 2
    U = 2 * J + 4
    bar = pltpu.get_barrier_semaphore()
    beside = [(px, b), (py, b), (s, sib)] + [(s, (z + k) % 4 * 2 + c) for k in (1, 2, 3)]
    for o in beside:
        pl.semaphore_signal(bar, 1, device_id=o, device_id_type=MESH)

    def remote(src, dst, ss, rs, dev):
        return pltpu.make_async_remote_copy(
            src, dst, ss, rs, device_id=dev, device_id_type=MESH
        )

    def axis(u):
        return (u - J) // (J // 2) if J <= u < 2 * J else u % 2

    def down(u):
        return isinstance(u, int) and J <= u < 2 * J

    def rslot(u):
        if not isinstance(u, int) or u < J:
            return u
        return J if u < 2 * J else u - 2 * J

    def slot(u):
        return u - 2 * J * (u // (2 * J))

    def mine(u):
        return (x, y)[axis(u)]

    def first_peer(u):
        return (px, py)[axis(u)]

    def last_peer(u):
        return (py, px)[axis(u)]

    def half(h):
        return pl.ds(al(h * HC), HC)

    def cp1(u):
        part = gb.at[pl.ds(J, J), u - J, 1 - c] if down(u) else gb.at[slot(u), :, 1 - c]
        return remote(part, rc.at[rslot(u)], sems.at[0, u], rems.at[0, u], (s, sib))

    def tile_copies(j):
        ux, uy = pl.ds(J, J // 2), pl.ds(J + J // 2, J // 2)
        return (
            remote(
                gb.at[ux, j, c, half(1 - x)], r2.at[ux, j], sems.at[1, J + j], rems.at[1, J + j],
                (px, b),
            ),
            remote(gb.at[uy, j, c, half(1 - y)], r2.at[uy, j], tsem.at[j], trem.at[j], (py, b)),
        )

    def tile2(j):
        cp1(J + j).wait_recv()
        gb[J : 2 * J, j, c] += rc[rslot(J + j)]
        if j < J - 1:
            pl.semaphore_signal(cr.at[rslot(J + j)], 1, device_id=(s, sib), device_id_type=MESH)
        for o in tile_copies(j):
            o.start()

    def tile3(j):
        for o in tile_copies(j):
            o.wait_recv()
        mid = J + J // 2
        gb[J:mid, j, c, half(x)] += r2[J:mid, j]
        gb[mid : 2 * J, j, c, half(y)] += r2[mid : 2 * J, j]

    def cp2(u):
        return remote(
            gb.at[slot(u), :, c, half(1 - mine(u))], r2.at[slot(u)], sems.at[1, u], rems.at[1, u],
            (first_peer(u), b),
        )

    def cp3(u, k):
        zz = (z + k) % 4
        return remote(
            gb.at[slot(u), zz, c, half(mine(u))], r3.at[u, k - 1], zs.at[k - 1, u], zr.at[k - 1, u],
            (s, zz * 2 + c),
        )

    def cp4(u):
        return remote(s3.at[u % 4], r4.at[u], sems.at[2, u], rems.at[2, u], (last_peer(u), b))

    def cp5(u):
        ref = f.at[u, half(mine(u))]
        return remote(ref, ref, sems.at[3, u], rems.at[3, u], (first_peer(u), b))

    def sent(u):
        cp1(u).wait_send()
        for o in tile_copies(u - J) if down(u) else (cp2(u),):
            o.wait_send()
        for k in (1, 2, 3):
            cp3(u, k).wait_send()

    def step1(u, again):
        if again:
            pl.semaphore_wait(cr.at[rslot(u)], 1)
        cp1(u).start()

    def step2(u, more):
        cp1(u).wait_recv()
        gb[slot(u), :, c] += rc[rslot(u)]
        if more:
            pl.semaphore_signal(cr.at[rslot(u)], 1, device_id=(s, sib), device_id_type=MESH)
        cp2(u).start()

    def step3(u):
        if not down(u):
            cp2(u).wait_recv()
            gb[slot(u), :, c, half(mine(u))] += r2[slot(u)]
        for k in (1, 2, 3):
            cp3(u, k).start()

    def step4(u):
        for k in (1, 2, 3):
            cp3(u, k).wait_recv()
        if isinstance(u, int):
            if u >= 4:
                cp4(u - 4).wait_send()
        else:

            @pl.when(u >= 4)
            def _():
                cp4(u - 4).wait_send()

        v = gb[slot(u), z, c, half(mine(u))].astype(f32)
        for k in range(3):
            v += r3[u, k].astype(f32)
        s3[u % 4] = v.astype(bf16)
        cp4(u).start()

    def step5(u):
        cp4(u).wait_recv()
        f[u, half(mine(u))] = s3[u % 4] + r4[u]
        cp5(u).start()

    def dcp(q, i):
        sl = q % 2
        if i == 0:
            a, o, dev = dn.at[sl, :, 1 - x, pl.ds(0, HR)], d1.at[sl, 0], px
        elif i == 1:
            a, o, dev = dn.at[sl, 1 - y, :, pl.ds(HR, HR)], d1.at[sl, 1], py
        elif i == 2:
            a, o, dev = dn.at[sl, 1 - y, x, pl.ds(0, HR)], d2.at[sl, 0], py
        else:
            a, o, dev = dn.at[sl, y, 1 - x, pl.ds(HR, HR)], d2.at[sl, 1], px
        return remote(a, o, ds_s.at[i, q], ds_r.at[i, q], (dev, b))

    def rows1(q):
        dcp(q, 0).start()
        dcp(q, 1).start()

    def rows2(q):
        sl = q % 2
        dcp(q, 0).wait_recv()
        dcp(q, 1).wait_recv()
        dn[sl, :, x, 0:HR] += d1[sl, 0]
        dn[sl, y, :, HR:R] += d1[sl, 1]
        dcp(q, 2).start()
        dcp(q, 3).start()

    def rows3(q):
        sl = q % 2
        dcp(q, 2).wait_recv()
        dcp(q, 3).wait_recv()
        for i in range(2):
            d = dn[sl, y, x, i * HR : (i + 1) * HR].astype(f32) + d2[sl, i].astype(f32)
            r = pl.ds(al(q * R + i * HR), HR)
            zz, rr = row_norm(n2[r, :].astype(f32))
            g = d * gain1
            du[r, :] = (
                h_v[r, :]
                + rr
                * (
                    g
                    - jnp.mean(g, axis=-1, keepdims=True)
                    - zz * jnp.mean(g * zz, axis=-1, keepdims=True)
                )
            ).astype(bf16)


    def emit(name):
        for k, u in SCHEDULE.get(name, ()):
            if k == 1:
                step1(u, u > J)
            elif k == 2 and down(u):
                tile2(u - J)
            elif k == 2:
                if u >= 2 * J:
                    if u == 2 * J:
                        cp5(0).wait_recv()
                    step2(u, False)
                else:
                    step2(u, True)
            else:
                {3: step3, 4: step4, 5: step5, 6: rows1, 7: rows2, 8: rows3, 10: tile3}[k](u)

    def emit_when(names):
        for name, cond in names:
            if name in SCHEDULE:
                pl.when(cond)(functools.partial(emit, name))

    def weight(u, left, right):
        def part(i, _):
            lanes = pl.ds(al(i * (D // 2), 128), D // 2)
            gb[slot(u), pl.ds(2 * i, 2)] = (
                dg(left[:, lanes], right[...], TN).astype(bf16).reshape(2, 2, CH, D)
            )
            return 0

        lax.fori_loop(0, 2, part, 0)

    def load(i, h, v):
        cp = pltpu.make_async_copy(h, v, lsem.at[i])
        cp.start()
        return cp

    c_a = load(0, a_h, a_v)
    c_wo = load(1, wo_h, wo)
    c_x = load(2, x_h, du)
    c_cot = load(3, cot_h, cot)
    def e_copy(t, slot):
        return pltpu.make_async_copy(e_h.at[t], e_v.at[slot], esem.at[slot])


    gain1, shift1, b_out, gain2, shift2, b_down = (
        row(r) for r in (g1_r, s1_r, bo_r, g2_r, s2_r, bd_r)
    )
    for j in range(J):
        bup[j : j + 1, :] = bu_r[j * D : (j + 1) * D].astype(f32).reshape(1, D)
    sm[...] = jnp.zeros_like(sm)
    for w in (c_a, c_wo, c_x, c_cot):
        w.wait()
    c_w = [
        (
            load(4 + 2 * j, wu_h.at[:, pl.ds(j * D, D)], vv.at[pl.ds(j * D, D)]),
            load(5 + 2 * j, gu_h.at[pl.ds(j * N, N)], kk.at[pl.ds(j * N, N)]),
        )
        for j in range(J)
    ]
    n0 = 4 + 2 * J
    c_q = load(n0, q_h, q_v)
    c_n1 = load(n0 + 1, n1_h, n1)
    c_wk = load(n0 + 2, wk_h, wk)
    c_wv = load(n0 + 3, wv_h, wv)
    e_copy(0, 0).start()
    e_copy(1, 1).start()

    def first(i, _):
        r = pl.ds(al(i * R), R)
        h = du[r, :].astype(f32) + dg(a_v[r, :], wo[...], NN) + b_out
        h_v[r, :] = h
        zn, _r = row_norm(h)
        n2[r, :] = (zn * gain2 + shift2).astype(bf16)
        acc[r, :] = h + b_down
        dn2[r, :] = jnp.zeros((R, D), f32)
        sm[7:8, :] += jnp.sum(cot[r, :].astype(f32), axis=0, keepdims=True)
        return 0

    lax.fori_loop(0, C, first, 0)
    pl.semaphore_wait(bar, len(beside))

    def p_copy(j):
        return pltpu.make_async_copy(
            kk.at[pl.ds(al(j * N), N)], p_h.at[pl.ds(al(j * N), N)], psem.at[j]
        )

    def ffn(j, _):
        jr = pl.ds(al(j * D), D)
        for jj in range(J):

            @pl.when(j == jj)
            def _():
                c_w[jj][0].wait()
                c_w[jj][1].wait()

        bias = bup[pl.ds(j, 1), :]

        def chunk(i, sums):
            emit_when(
                (f"f{jj}{ii}", (j == jj) & (i == ii)) for jj in range(J) for ii in range(C)
            )
            r = pl.ds(al(i * R), R)
            u = dg(n2[r, :], vv[jr, :], NN) + bias
            rj = pl.ds(al(j * N + i * R), R)
            g = kk[rj, :].astype(f32)
            u2 = u * u
            t = jnp.tanh(u * (GC0 + GC1 * u2))
            hu = 0.5 * u
            half = 0.5 + 0.5 * t
            p = (u * half).astype(bf16)
            d = (g * (half + hu * (1.0 - t * t) * (GC0 + 3.0 * GC1 * u2))).astype(bf16)
            kk[rj, :] = p
            du[r, :] = d
            dn2[r, :] += dg(d, vv[jr, :], NT)
            return sums + jnp.sum(d.astype(f32), axis=0, keepdims=True)

        dj = lax.fori_loop(0, C, chunk, jnp.zeros((1, D), f32))
        sm[pl.ds(8 + j, 1), :] = dj
        emit_when((f"u{jj}", j == jj) for jj in range(J))
        weight(j, n2, du)
        step1(j, False)
        emit_when((f"w{jj}", j == jj) for jj in range(J))
        per = FF // B
        pt = kk.at[pl.ds(al(j * N), N)]

        def rows_of(bb, _):
            gw = dg(pt[:, pl.ds(al(bb * per, 128), per)], cot[...], TN).astype(bf16)
            for i in range(per // CH):
                gb[J + i, j, bb] = gw[i * CH : (i + 1) * CH, :]
            return 0

        lax.fori_loop(0, D // per, rows_of, 0)
        p_copy(j).start()
        return 0

    lax.fori_loop(0, J, ffn, 0)

    c_v = load(1, v_h, vv.at[pl.ds(0, t_rows)])

    for j in range(J):
        p_copy(j).wait()
    c_k = load(0, k_h, kk.at[pl.ds(0, t_rows)])

    def second(i, _):
        emit_when((f"s{ii}", i == ii) for ii in range(C))
        r = pl.ds(al(i * R), R)
        zn, rr = row_norm(h_v[r, :])
        dnn = dn2[r, :]
        g = dnn * gain2
        sm[5:6, :] += jnp.sum(dnn * zn, axis=0, keepdims=True)
        sm[6:7, :] += jnp.sum(dnn, axis=0, keepdims=True)
        dh = cot[r, :].astype(f32) + rr * (
            g
            - jnp.mean(g, axis=-1, keepdims=True)
            - zn * jnp.mean(g * zn, axis=-1, keepdims=True)
        )
        h_v[r, :] = dh
        db = dh.astype(bf16)
        n2[r, :] = db
        sm[4:5, :] += jnp.sum(db.astype(f32), axis=0, keepdims=True)
        du[r, :] = dg(db, wo[...], NT).astype(bf16)
        return 0

    lax.fori_loop(0, C, second, 0)
    c_li = load(2, li_h, dn2)
    emit("wo")
    sent(0)
    c_wq = load(3, wq_h, wo)
    weight(2 * J, a_v, n2)

    c_x = load(4, x_h, n2)
    emit("kw")
    for w in (c_x, c_k, c_v, c_li, c_q, c_wk, c_wv, c_wq, c_n1):
        w.wait()
    dq_v, do_v = cot, du
    lane = lax.broadcasted_iota(jnp.int32, (1, 128), 1)
    lo = lane < 64

    def stack(v):
        zero = jnp.zeros_like(v)
        return jnp.concatenate([jnp.where(lo, v, zero), jnp.where(lo, zero, v)], 0)

    def row_parts(q):
        rq = pl.ds(al(q * R), R)

        def put(blk, more):
            rr = pl.ds(al((q * S + blk) * R), R)
            d = dg(kk[rr, :], wk[...], NT) + dg(vv[rr, :], wv[...], NT)
            if more:
                d += dg(dq_v[rq, :], wo[...], NT)
            n = n1[rr, :].astype(f32)
            sm[0:1, :] += jnp.sum(d * n, axis=0, keepdims=True)
            sm[1:2, :] += jnp.sum(d, axis=0, keepdims=True)
            dn[q % 2, blk // 2, blk % 2] = d.astype(bf16)

        def others(i, _):
            emit_when(
                (f"d{qq}{ii}", (q == qq) & (i == ii))
                for qq in range(C)
                for ii in range(S - 1)
                if qq + 1 < C or ii > 0
            )
            put((s + 1 + i) % S, False)
            return 0

        lax.fori_loop(0, S - 1, others, 0)
        emit_when((f"d{qq}{S - 1}", q == qq) for qq in range(C))
        put(s, True)

    def pair(t, _):
        q, p = t // pairs, t % pairs
        slot = t % 2
        emit_when((f"t{tt}", t == tt) for tt in range(C * pairs))
        lanes = pl.ds(al(p * 128, 128), 128)
        rq = pl.ds(al(q * R), R)
        rk = pl.ds(al(q * T), T)
        qs = stack(q_v[rq, lanes])
        dof = do_v[rq, lanes].astype(f32) * dn2[rq, lanes]
        dos = stack(dof.astype(bf16))
        dl = jnp.sum(stack(dof * a_v[rq, lanes].astype(f32)), axis=1, keepdims=True)
        e_copy(t, slot).wait()
        dp = dg(dos, vv[rk, lanes], NT)
        vv[rk, lanes] = dg(dos, e_v[slot], TN).astype(bf16).T
        ds = (e_v[slot].astype(f32) * (dp - dl)).astype(bf16)
        dks = (dg(qs, ds, TN) * (1.0 / LOG2E)).astype(bf16).T
        dqs = dg(ds, kk[rk, lanes], NN)
        kk[rk, lanes] = dks
        dq_v[rq, lanes] = (jnp.where(lo, dqs[:R], dqs[R:]) * (HEAD_DIM ** (-0.5))).astype(
            bf16
        )

        @pl.when(t + 2 < C * pairs)
        def _():
            e_copy(t + 2, slot).start()

        @pl.when((p == pairs - 1) & (q < C - 1))
        def _():
            row_parts(q)

        return 0

    lax.fori_loop(0, C * pairs, pair, 0)
    emit("q")
    for u in (1, 2, 3):
        sent(u)
        cp5(u).wait_recv()
    for i in range(C):
        r = pl.ds(i * R, R)
        a_v[r, :] = n1[pl.ds(al((i * S + s) * R), R), :]
    q_u, k_u, v_u = 2 * J + 1, 2 * J + 2, 2 * J + 3
    weight(q_u, a_v, dq_v)
    sm[2:3, :] = jnp.sum(dq_v[...].astype(f32), axis=0, keepdims=True)
    sm[3:4, :] = jnp.sum(vv[0:t_rows, :].astype(f32), axis=0, keepdims=True)
    def mcp(i, src, dst, dev):
        return remote(src, dst, ms.at[i], mr.at[i], dev)

    emit("k")
    weight(k_u, n1, kk.at[pl.ds(0, t_rows)])
    h_rows, h_p = J // 2 * D, J // 2 * N
    c_w0 = load(0, wd_h.at[pl.ds(0, h_rows)], kk.at[pl.ds(0, h_rows)])
    emit("v")
    weight(v_u, n1, vv.at[pl.ds(0, t_rows)])
    c_p0 = load(1, p_h.at[pl.ds(0, h_p)], n1.at[pl.ds(0, h_p)])
    emit("d20")
    for i in range(4):
        dcp(0, i).wait_send()
    row_parts(C - 1)
    sm[0:1, :] = (sm[0:1, :] - shift1 * sm[1:2, :]) / gain1

    m1 = mcp(0, sm, mc.at[0], (s, sib))
    m1.start()
    c_w1 = load(2, wd_h.at[pl.ds(h_rows, h_rows)], kk.at[pl.ds(h_rows, h_rows)])
    c_p1 = load(3, p_h.at[pl.ds(h_p, h_p)], n1.at[pl.ds(h_p, h_p)])

    def last(i):
        r = pl.ds(al(i * R), R)
        o = acc[r, :]
        for j in range(J):
            o += dg(n1[pl.ds(al(j * N + i * R), R), :], kk[j * D : (j + 1) * D, :], NN)
        q_v[r, :] = o.astype(bf16)

    emit("o0")
    for w in (c_w0, c_p0, c_w1, c_p1):
        w.wait()
    last(0)
    m1.wait()
    mz[0] = sm[...] + mc[0]
    m2 = [mcp(k, mz.at[0], mz.at[k], (s, (z + k) % 4 * 2 + c)) for k in (1, 2, 3)]
    for m in m2:
        m.start()
    emit("o1")
    last(1)
    for m in m2:
        m.wait()
    mx[0] = (mz[0] + mz[1]) + (mz[2] + mz[3])
    m3 = mcp(4, mx.at[0], mx.at[1], (px, b))
    m3.start()
    emit("o2")
    last(2)
    c_o = pltpu.make_async_copy(q_v, out_h, osem.at[0])
    c_o.start()
    m3.wait()
    mx[2] = mx[0] + mx[1]
    m4 = mcp(5, mx.at[2], mx.at[3], (py, b))
    m4.start()
    emit("end0")
    m4.wait()
    sm[...] = mx[2] + mx[3]
    c_s = pltpu.make_async_copy(sm, sm_h, osem.at[2])
    c_s.start()
    emit("end1")
    c_i = pltpu.make_async_copy(du, ig_h, osem.at[1])
    c_i.start()
    emit("end2")
    for u in range(U):
        if u > 3:
            cp5(u).wait_recv()
    c_f = pltpu.make_async_copy(f, f_h, osem.at[3])
    c_f.start()
    for u in range(U):
        if u > 3:
            sent(u)
        if u >= 2 * J:
            cp4(u).wait_send()
        cp5(u).wait_send()
    for q in (1, 2):
        for i in range(4):
            dcp(q, i).wait_send()
    for o in (c_o, c_i, c_s, c_f):
        o.wait()


def backward(C, R, D, S, FF, x, cot, a, li, q, k, v, n1, e, gu, vecs, wo, wu, wd, wq, wk, wv):
    N, T = C * R, R * S
    J = FF // D
    U, CH = 2 * J + 4, D // 8
    sd = jax.ShapeDtypeStruct
    dma = pltpu.SemaphoreType.DMA
    vm = pltpu.VMEM
    return pl.pallas_call(
        functools.partial(backward_kernel, C, R, D, S, FF),
        out_shape=(
            sd((N, D), bf16),
            sd((N, D), bf16),
            sd((U, D // 8, D), bf16),
            sd((16, D), f32),
            sd((J * N, D), bf16),
        ),
        in_specs=[ANY] * 10 + [VM] * 7 + [ANY] * 6,
        out_specs=(ANY,) * 5,
        scratch_shapes=[
            vm((N, D), bf16), vm((N, D), bf16), vm((N, D), bf16),
            vm((N, D), bf16), vm((N, D), bf16),
            vm((N, D), f32), vm((N, D), f32), vm((N, D), f32),
            vm((FF, D), bf16), vm((FF, D), bf16), vm((C * T, D), bf16),
            vm((D, D), bf16), vm((D, D), bf16), vm((D, D), bf16),
            vm((2 * J, 4, 2, CH, D), bf16), vm((2, 2, 2, R, D), bf16),
            vm((2, 2 * R, T), bf16), vm((16, D), f32),
            vm((5, 4, CH, D), bf16), vm((2 * J, 4, CH // 2, D), bf16), vm((U, 3, CH // 2, D), bf16),
            vm((4, CH // 2, D), bf16), vm((U, CH // 2, D), bf16), vm((U, CH, D), bf16),
            vm((2, 2, 2, R // 2, D), bf16), vm((2, 2, R // 2, D), bf16),
            vm((1, 16, D), f32), vm((4, 16, D), f32), vm((4, 16, D), f32), vm((J, D), f32),
            dma((4 + 2 * J + 4,)), dma((2,)), dma((4,)), dma((J,)), dma((J,)), dma((J,)),
            dma((4, U)), dma((4, U)), dma((3, U)), dma((3, U)),
            dma((4, C)), dma((4, C)), dma((6,)), dma((6,)),
            pltpu.SemaphoreType.REGULAR((5,)),
        ],
        compiler_params=pltpu.CompilerParams(
            collective_id=2, has_side_effects=True, vmem_limit_bytes=(64 * 2**20) - 2**17
        ),
        cost_estimate=pl.CostEstimate(
            flops=40 * 10**9, bytes_accessed=60 * 10**6, transcendentals=0
        ),
    )(x, cot, a, li, q, k, v, n1, e, gu, *vecs, wo, wu, wd, wq, wk, wv)


def finish_kernel(D, FF, f_h, sm, out_h, ig_h, *rest):
    o_out, o_ig, g1, s1, wq, bq, wk, wv, bv, wo, bo, g2, s2, wu, bu, wd, bd, f, v_out, v_ig, sem = rest
    J, CH = FF // D, D // 8
    c1 = pltpu.make_async_copy(f_h, f, sem.at[0])
    c2 = pltpu.make_async_copy(out_h, v_out, sem.at[1])
    c3 = pltpu.make_async_copy(ig_h, v_ig, sem.at[2])
    for c in (c1, c2, c3):
        c.start()
    b = lax.axis_index("batch")
    c2.wait()
    c4 = pltpu.make_async_copy(v_out, o_out, sem.at[1])
    c4.start()
    c3.wait()
    c5 = pltpu.make_async_copy(v_ig, o_ig, sem.at[2])
    c5.start()
    rolled = pltpu.roll(sm[0:8, :], (8 - b) % 8 * CH, 1)
    for i, o in enumerate((g1, s1, bq, bv, bo, g2, s2, bd)):
        o[...] = rolled[i, :CH]
    per = FF // 8
    half = D // per
    up = sm[8 : 8 + J, :]
    here = lax.broadcasted_iota(jnp.int32, (J, 1), 0) == b // half
    up = jnp.sum(jnp.where(here, up, 0.0), axis=0, keepdims=True)
    up = jnp.where(b % half == 0, up[:, :per], up[:, per:])
    bu[...] = up[0]
    c1.wait()
    for j in range(J):
        wu[:, j * D : (j + 1) * D] = f[j].astype(f32)
        wd[j * CH : (j + 1) * CH, :] = f[J + j].astype(f32)
    for i, o in enumerate((wo, wq, wk, wv)):
        o[...] = f[2 * J + i].astype(f32)
    c4.wait()
    c5.wait()


def finish(D, FF, f, sm, out, ig):
    sd = jax.ShapeDtypeStruct
    CH = D // 8
    row, mat = sd((CH,), f32), sd((CH, D), f32)
    return pl.pallas_call(
        functools.partial(finish_kernel, D, FF),
        out_shape=(
            sd(out.shape, bf16), sd(ig.shape, bf16), row, row, mat, row, mat, mat, row, mat,
            row, row, row, sd((CH, FF), f32), sd((FF // 8,), f32), sd((FF // 8, D), f32), row,
        ),
        in_specs=[ANY, VM, ANY, ANY],
        out_specs=(ANY, ANY) + (VM,) * 15,
        scratch_shapes=[pltpu.VMEM(v.shape, bf16) for v in (f, out, ig)] + [pltpu.SemaphoreType.DMA((3,))],
        compiler_params=pltpu.CompilerParams(vmem_limit_bytes=62 * 2**20),
    )(f, sm, out, ig)


def fast_body(
    inputs, lengths, gain_one, shift_one, w_query, b_query, w_key, w_value, b_value, w_out, b_out,
    gain_two, shift_two, w_up, b_up, w_down, b_down, cotangent,
):
    C, R, D = inputs.shape
    S = lax.axis_size("seq")
    FF = w_up.shape[1]
    N = C * R
    x = inputs.reshape(N, D)
    cot = cotangent.reshape(N, D)
    n1, q, k, v, a, li, e, gu = attend(
        C, R, D, S, FF, x, cot, lengths, (gain_one, shift_one, b_query, b_value),
        w_query, w_key, w_value, w_down,
    )
    out, input_grad, g, sm, _ = backward(
        C, R, D, S, FF, x, cot, a, li, q, k, v, n1, e, gu,
        (gain_one, shift_one, b_out, gain_two, shift_two, b_down, b_up),
        w_out, w_up, w_down, w_query, w_key, w_value,
    )
    out, input_grad, *grads = finish(D, FF, g, sm, out, input_grad)
    return (out.reshape(inputs.shape), input_grad.reshape(inputs.shape), *grads)


def from_behind(x, axis, by):
    length = lax.axis_size(axis)
    return lax.ppermute(x, axis, [(i, (i + by) % length) for i in range(length)])


def normed(values, gain, offset):
    average = jnp.mean(values, axis=-1, keepdims=True)
    centred = values - average
    spread = jnp.mean(centred * centred, axis=-1, keepdims=True)
    return centred * lax.rsqrt(spread + norm_eps) * gain + offset


def outer_sum(left, right):
    return lax.dot_general(
        left, right, (((0,), (0,)), ((), ())), preferred_element_type=jnp.float32
    )


def back_dot(grad_rows, weight):
    return lax.dot_general(
        grad_rows, weight, (((1,), (1,)), ((), ())), preferred_element_type=jnp.float32
    )


def front_dot(rows_low, weight, bias):
    return jnp.dot(rows_low, weight, preferred_element_type=jnp.float32) + bias.astype(jnp.float32)


def column_sums(values):
    return jnp.sum(values.astype(jnp.float32), axis=0)


def key_valid(lengths, source, block_rows):
    positions = source * block_rows + jnp.arange(block_rows, dtype=jnp.int32)
    return (positions[None, :] < lengths[:, None])[:, None, None, :]


def block_scores(queries, key_block, valid):
    scores = jnp.einsum(
        "srhd,sthd->srht", queries, key_block, preferred_element_type=jnp.float32
    ) * HEAD_DIM ** (-0.5)
    return jnp.where(valid, scores, masked_score)


def ring_body(
    inputs,
    lengths,
    gain_one,
    shift_one,
    w_query,
    b_query,
    w_key,
    w_value,
    b_value,
    w_out,
    b_out,
    gain_two,
    shift_two,
    w_up,
    b_up,
    w_down,
    b_down,
    cotangent,
):
    cycle_size = lax.axis_size("seq")
    position = lax.axis_index("seq")
    count, block_rows, width = inputs.shape
    heads = width // HEAD_DIM
    total_rows = count * block_rows
    split_shape = (count, block_rows, heads, HEAD_DIM)
    scale = HEAD_DIM ** (-0.5)
    rows_in = inputs.astype(jnp.float32).reshape(total_rows, width)
    first_full, norm_one_pull = jax.vjp(
        normed, rows_in, gain_one.astype(jnp.float32), shift_one.astype(jnp.float32)
    )
    first = first_full.astype(jnp.bfloat16)
    queries = front_dot(first, w_query, b_query).astype(jnp.bfloat16).reshape(split_shape)
    key_rows = jnp.dot(first, w_key, preferred_element_type=jnp.float32).astype(jnp.bfloat16)
    value_rows = front_dot(first, w_value, b_value).astype(jnp.bfloat16)
    own_block = jnp.stack((key_rows, value_rows)).reshape((2,) + split_shape)
    running_max = jnp.full((count, block_rows, heads), masked_score, jnp.float32)
    running_total = jnp.zeros((count, block_rows, heads), jnp.float32)
    running_sum = jnp.zeros(split_shape, jnp.float32)
    moving = own_block
    for rotation in range(cycle_size):
        source = (position - rotation) % cycle_size
        valid = key_valid(lengths, source, block_rows)
        scores = block_scores(queries, moving[0], valid)
        new_max = jnp.maximum(running_max, jnp.max(scores, axis=-1))
        decay = jnp.exp(running_max - new_max)
        weights_exp = jnp.where(valid, jnp.exp(scores - new_max[..., None]), 0.0)
        running_total = running_total * decay + jnp.sum(weights_exp, axis=-1)
        running_sum = running_sum * decay[..., None] + jnp.einsum(
            "srht,sthd->srhd",
            weights_exp.astype(jnp.bfloat16),
            moving[1],
            preferred_element_type=jnp.float32,
        )
        running_max = new_max
        if rotation + 1 < cycle_size:
            moving = from_behind(moving, "seq", 1)
    attended = running_sum / running_total[..., None]
    log_total = running_max + jnp.log(running_total)
    attended_low = attended.reshape(total_rows, width).astype(jnp.bfloat16)
    middle = rows_in + front_dot(attended_low, w_out, b_out)
    second_full, norm_two_pull = jax.vjp(
        normed, middle, gain_two.astype(jnp.float32), shift_two.astype(jnp.float32)
    )
    second = second_full.astype(jnp.bfloat16)
    hidden = front_dot(second, w_up, b_up)
    gelu_value, gelu_pull = jax.vjp(jax.nn.gelu, hidden)
    active = gelu_value.astype(jnp.bfloat16)
    outputs = middle + front_dot(active, w_down, b_down)
    grad_rows_out = cotangent.astype(jnp.float32).reshape(total_rows, width)
    grad_ffn = cotangent.reshape(total_rows, width)
    grad_w_down = outer_sum(active, grad_ffn)
    grad_b_down = column_sums(grad_ffn)
    grad_hidden = gelu_pull(back_dot(grad_ffn, w_down))[0].astype(jnp.bfloat16)
    grad_w_up = outer_sum(second, grad_hidden)
    grad_b_up = column_sums(grad_hidden)
    grad_middle_part, grad_gain_two, grad_shift_two = norm_two_pull(back_dot(grad_hidden, w_up))
    grad_middle = grad_rows_out + grad_middle_part
    grad_branch = grad_middle.astype(jnp.bfloat16)
    grad_w_out = outer_sum(attended_low, grad_branch)
    grad_b_out = column_sums(grad_branch)
    grad_attended = back_dot(grad_branch, w_out).astype(jnp.bfloat16).reshape(split_shape)
    row_delta = jnp.sum(grad_attended.astype(jnp.float32) * attended, axis=-1)
    grad_queries = jnp.zeros(split_shape, jnp.float32)
    carried = jnp.zeros((2,) + split_shape, jnp.float32)
    moving = own_block
    for rotation in range(cycle_size):
        source = (position - rotation) % cycle_size
        valid = key_valid(lengths, source, block_rows)
        scores = block_scores(queries, moving[0], valid)
        probs = jnp.where(valid, jnp.exp(scores - log_total[..., None]), 0.0)
        grad_probs = jnp.einsum(
            "srhd,sthd->srht", grad_attended, moving[1], preferred_element_type=jnp.float32
        )
        grad_scores = (probs * (grad_probs - row_delta[..., None])).astype(jnp.bfloat16)
        grad_queries = (
            grad_queries
            + jnp.einsum(
                "srht,sthd->srhd", grad_scores, moving[0], preferred_element_type=jnp.float32
            )
            * scale
        )
        grad_keys_part = (
            jnp.einsum("srht,srhd->sthd", grad_scores, queries, preferred_element_type=jnp.float32)
            * scale
        )
        grad_values_part = jnp.einsum(
            "srht,srhd->sthd",
            probs.astype(jnp.bfloat16),
            grad_attended,
            preferred_element_type=jnp.float32,
        )
        carried = from_behind(
            (carried + jnp.stack((grad_keys_part, grad_values_part))).astype(jnp.bfloat16), "seq", 1
        ).astype(jnp.float32)
        if rotation + 1 < cycle_size:
            moving = from_behind(moving, "seq", 1)
    grad_keys = carried[0].reshape(total_rows, width).astype(jnp.bfloat16)
    grad_values = carried[1].reshape(total_rows, width).astype(jnp.bfloat16)
    grad_query_rows = grad_queries.reshape(total_rows, width).astype(jnp.bfloat16)
    grad_w_query = outer_sum(first, grad_query_rows)
    grad_b_query = column_sums(grad_query_rows)
    grad_w_key = outer_sum(first, grad_keys)
    grad_w_value = outer_sum(first, grad_values)
    grad_b_value = column_sums(grad_values)
    grad_first = (
        back_dot(grad_query_rows, w_query)
        + back_dot(grad_keys, w_key)
        + back_dot(grad_values, w_value)
    )
    grad_rows_part, grad_gain_one, grad_shift_one = norm_one_pull(grad_first)
    input_grad = grad_middle + grad_rows_part
    scattered = (
        lax.psum_scatter(
            grad_gain_one.astype(jnp.bfloat16), "batch", scatter_dimension=0, tiled=True
        ).astype(jnp.float32),
        lax.psum_scatter(
            grad_shift_one.astype(jnp.bfloat16), "batch", scatter_dimension=0, tiled=True
        ).astype(jnp.float32),
        lax.psum_scatter(
            grad_w_query.astype(jnp.bfloat16), "batch", scatter_dimension=0, tiled=True
        ).astype(jnp.float32),
        lax.psum_scatter(
            grad_b_query.astype(jnp.bfloat16), "batch", scatter_dimension=0, tiled=True
        ).astype(jnp.float32),
        lax.psum_scatter(
            grad_w_key.astype(jnp.bfloat16), "batch", scatter_dimension=0, tiled=True
        ).astype(jnp.float32),
        lax.psum_scatter(
            grad_w_value.astype(jnp.bfloat16), "batch", scatter_dimension=0, tiled=True
        ).astype(jnp.float32),
        lax.psum_scatter(
            grad_b_value.astype(jnp.bfloat16), "batch", scatter_dimension=0, tiled=True
        ).astype(jnp.float32),
        lax.psum_scatter(
            grad_w_out.astype(jnp.bfloat16), "batch", scatter_dimension=0, tiled=True
        ).astype(jnp.float32),
        lax.psum_scatter(
            grad_b_out.astype(jnp.bfloat16), "batch", scatter_dimension=0, tiled=True
        ).astype(jnp.float32),
        lax.psum_scatter(
            grad_gain_two.astype(jnp.bfloat16), "batch", scatter_dimension=0, tiled=True
        ).astype(jnp.float32),
        lax.psum_scatter(
            grad_shift_two.astype(jnp.bfloat16), "batch", scatter_dimension=0, tiled=True
        ).astype(jnp.float32),
        lax.psum_scatter(
            grad_w_up.astype(jnp.bfloat16), "batch", scatter_dimension=0, tiled=True
        ).astype(jnp.float32),
        lax.psum_scatter(
            grad_b_up.astype(jnp.bfloat16), "batch", scatter_dimension=0, tiled=True
        ).astype(jnp.float32),
        lax.psum_scatter(
            grad_w_down.astype(jnp.bfloat16), "batch", scatter_dimension=0, tiled=True
        ).astype(jnp.float32),
        lax.psum_scatter(
            grad_b_down.astype(jnp.bfloat16), "batch", scatter_dimension=0, tiled=True
        ).astype(jnp.float32),
    )
    summed = (
        lax.psum(scattered[0].astype(jnp.bfloat16), "seq").astype(jnp.float32),
        lax.psum(scattered[1].astype(jnp.bfloat16), "seq").astype(jnp.float32),
        lax.psum(scattered[2].astype(jnp.bfloat16), "seq").astype(jnp.float32),
        lax.psum(scattered[3].astype(jnp.bfloat16), "seq").astype(jnp.float32),
        lax.psum(scattered[4].astype(jnp.bfloat16), "seq").astype(jnp.float32),
        lax.psum(scattered[5].astype(jnp.bfloat16), "seq").astype(jnp.float32),
        lax.psum(scattered[6].astype(jnp.bfloat16), "seq").astype(jnp.float32),
        lax.psum(scattered[7].astype(jnp.bfloat16), "seq").astype(jnp.float32),
        lax.psum(scattered[8].astype(jnp.bfloat16), "seq").astype(jnp.float32),
        lax.psum(scattered[9].astype(jnp.bfloat16), "seq").astype(jnp.float32),
        lax.psum(scattered[10].astype(jnp.bfloat16), "seq").astype(jnp.float32),
        lax.psum(scattered[11].astype(jnp.bfloat16), "seq").astype(jnp.float32),
        lax.psum(scattered[12].astype(jnp.bfloat16), "seq").astype(jnp.float32),
        lax.psum(scattered[13].astype(jnp.bfloat16), "seq").astype(jnp.float32),
        lax.psum(scattered[14].astype(jnp.bfloat16), "seq").astype(jnp.float32),
    )
    return (
        outputs.astype(jnp.bfloat16).reshape(inputs.shape),
        input_grad.astype(jnp.bfloat16).reshape(inputs.shape),
        summed[0],
        summed[1],
        summed[2],
        summed[3],
        summed[4],
        summed[5],
        summed[6],
        summed[7],
        summed[8],
        summed[9],
        summed[10],
        summed[11],
        summed[12],
        summed[13],
        summed[14],
    )


def solution(mesh):
    placed = (
        P("batch", "seq", None),
        P("batch"),
        P(),
        P(),
        P(),
        P(),
        P(),
        P(),
        P(),
        P(),
        P(),
        P(),
        P(),
        P(),
        P(),
        P(),
        P(),
        P("batch", "seq", None),
    )
    small = mesh.shape["seq"] == 4 and mesh.shape["batch"] == 8
    body = fast_body if small else ring_body
    return jax.shard_map(
        body,
        mesh=mesh,
        in_specs=placed,
        out_specs=(
            P("batch", "seq", None),
            P("batch", "seq", None),
            P("batch"),
            P("batch"),
            P("batch", None),
            P("batch"),
            P("batch", None),
            P("batch", None),
            P("batch"),
            P("batch", None),
            P("batch"),
            P("batch"),
            P("batch"),
            P("batch", None),
            P("batch"),
            P("batch", None),
            P("batch"),
        ),
        check_vma=False,
    )
```

```python
import functools
import math

import jax
import jax.numpy as jnp
from jax import lax
from jax.experimental import pallas as pl
from jax.experimental.pallas import tpu as pltpu
from jax.sharding import PartitionSpec as P

HEAD_DIM = 64
norm_eps = 1e-05
masked_score = -1e30

bf16 = jnp.bfloat16
f32 = jnp.float32
MESH = pl.DeviceIdType.MESH
ANY = pl.BlockSpec(memory_space=pl.ANY)
VM = pl.BlockSpec(memory_space=pltpu.VMEM)
SM = pl.BlockSpec(memory_space=pltpu.SMEM)
NN = (((1,), (0,)), ((), ()))
NT = (((1,), (1,)), ((), ()))
TN = (((0,), (0,)), ((), ()))
LOG2E = math.log2(math.e)
GC0 = math.sqrt(2.0 / math.pi)
GC1 = GC0 * 0.044715


def dg(a, b, dims):
    return lax.dot_general(a, b, dims, preferred_element_type=f32)


def row(ref):
    return ref[...].astype(f32).reshape(1, ref.shape[0])


def al(i, m=16):
    return pl.multiple_of(i, m)


def places():
    s = lax.axis_index("seq")
    b = lax.axis_index("batch")
    y, x = s // 2, s % 2
    return s, b, y * 2 + (1 - x), (1 - y) * 2 + x, (1 - y) * 2 + (1 - x)


def row_norm(x):
    mean = jnp.mean(x, axis=-1, keepdims=True)
    c = x - mean
    r = lax.rsqrt(jnp.mean(c * c, axis=-1, keepdims=True) + norm_eps)
    return c * r, r


def attend_kernel(
    C, R, D, S,
    x_h, cot_h, len_s, g_r, s_r, bq_r, bv_r, bo_r, g2_r, s2_r, wq_h, wk_h, wv_h, wd_h, wo_h,
    n1_h, q_h, k_h, v_h, a_h, li_h, e_h, gu_h, h_h, n2_h,
    x_v, n1, wq, wk, wv, q_v, k_v, v_v, a_v, li_v, e_v, s_v, cot, wd, gu, wo, h_v, n2,
    lsem, osem, esem, gsem, rsem, os, orr, rs, rr,
):
    T = R * S
    HR = R // 2
    pairs = D // 128
    s, b, px, py, pd = places()
    bar = pltpu.get_barrier_semaphore()
    for o in (px, py):
        pl.semaphore_signal(bar, 1, device_id=(o, b), device_id_type=MESH)
    xc = [
        pltpu.make_async_copy(
            x_h.at[pl.ds(i * R, R)], x_v.at[pl.ds(i * R, R)], lsem.at[i]
        )
        for i in range(C)
    ]
    for c in xc:
        c.start()
    wc = [
        pltpu.make_async_copy(h, v, lsem.at[C + i])
        for i, (h, v) in enumerate(((wk_h, wk), (wv_h, wv), (wq_h, wq), (cot_h, cot), (wd_h, wd), (wo_h, wo)))
    ]
    for c in wc:
        c.start()

    def rows(q, blk, off, n):
        return pl.ds(al((q * S + blk) * R + off), n)

    def copy(q, peer, blk, off, ss, rs):
        ref = n1.at[rows(q, blk, off, HR)]
        return pltpu.make_async_remote_copy(
            ref, ref, ss, rs, device_id=(peer, b), device_id_type=MESH
        )

    own = [
        [
            copy(q, peer, s, off, os.at[i, q], orr.at[i, q])
            for i, (peer, off) in enumerate(((px, 0), (py, HR), (px, HR), (py, 0)))
        ]
        for q in range(C)
    ]
    rel = [
        [
            copy(q, peer, blk, off, rs.at[i, q], rr.at[i, q])
            for i, (peer, blk, off) in enumerate(((py, px, 0), (px, py, HR)))
        ]
        for q in range(C)
    ]

    gain, shift, bq, bv = (row(r) for r in (g_r, s_r, bq_r, bv_r))
    b_out, gain2, shift2 = (row(r) for r in (bo_r, g2_r, s2_r))
    for q in range(C):
        xc[q].wait()
        z, _ = row_norm(x_v[q * R : (q + 1) * R, :].astype(f32))
        n1[rows(q, s, 0, R), :] = (z * gain + shift).astype(bf16)
        if q == 0:
            pl.semaphore_wait(bar, 2)
        if q < 2:
            for c in own[q]:
                c.start()
    for c in wc[:3]:
        c.wait()

    def kv(q, blk):
        rs = rows(q, blk, 0, R)
        v = n1[rs, :]
        k_v[rs, :] = dg(v, wk[...], NN).astype(bf16)
        v_v[rs, :] = (dg(v, wv[...], NN) + bv).astype(bf16)

    def own_rows(q, _):
        v = n1[rows(q, s, 0, R), :]
        q_v[pl.ds(al(q * R), R), :] = (
            (dg(v, wq[...], NN) + bq) * (HEAD_DIM ** (-0.5) * LOG2E)
        ).astype(bf16)
        kv(q, s)
        return 0

    lax.fori_loop(0, C, own_rows, 0)
    qc = pltpu.make_async_copy(q_v, q_h, osem.at[0])
    qc.start()

    def onward(q):
        for c in own[q][:2]:
            c.wait_recv()
        for c in rel[q]:
            c.start()

    def near(q):
        for c in own[q][2:]:
            c.wait_recv()
        lax.fori_loop(0, 2, lambda i, c: (kv(q, jnp.where(i == 0, px, py)), c)[1], 0)

    def gu_copy(j):
        return pltpu.make_async_copy(
            gu.at[pl.ds(al(j * C * R), C * R)], gu_h.at[pl.ds(al(j * C * R), C * R)], gsem.at[j]
        )

    def hidden(j, _):
        gu[pl.ds(al(j * C * R), C * R), :] = dg(
            cot[...], wd[pl.ds(al(j * D), D), :], NT
        ).astype(bf16)
        gu_copy(j).start()
        return 0

    J = wd.shape[0] // D

    def far(q):
        for c in rel[q]:
            c.wait_recv()
        kv(q, pd)
        for i, (v, h) in enumerate(((n1, n1_h), (k_v, k_h), (v_v, v_h))):
            pltpu.make_async_copy(
                v.at[pl.ds(q * T, T)], h.at[pl.ds(q * T, T)], osem.at[3 + 3 * q + i]
            ).start()

    onward(0)
    for c in wc[3:]:
        c.wait()
    lax.fori_loop(0, J // 2, hidden, 0)
    near(0)
    lax.fori_loop(J // 2, J, hidden, 0)
    onward(1)
    for c in own[2]:
        c.start()
    near(1)
    far(0)

    lane = lax.broadcasted_iota(jnp.int32, (1, 128), 1)
    lo = lane < 64
    col = lax.broadcasted_iota(jnp.int32, (1, T), 1)

    def e_copy(t, slot):
        return pltpu.make_async_copy(e_v.at[slot], e_h.at[t], esem.at[slot])

    def scores(t):
        q, p = t // pairs, t % pairs
        lanes = pl.ds(al(p * 128, 128), 128)
        qp = q_v[pl.ds(al(q * R), R), lanes]
        zero = jnp.zeros_like(qp)
        qs = jnp.concatenate([jnp.where(lo, qp, zero), jnp.where(lo, zero, qp)], 0)
        bias = jnp.where(col < len_s[q], 0.0, masked_score).astype(f32)
        return dg(qs, k_v[pl.ds(al(q * T), T), lanes], NT) + bias

    def weigh(t, slot):
        q, p = t // pairs, t % pairs
        lanes = pl.ds(al(p * 128, 128), 128)
        rq = pl.ds(al(q * R), R)
        m = jnp.max(s_v[slot], axis=1, keepdims=True)
        e = jnp.exp2(s_v[slot] - m)
        eb = e.astype(bf16)
        tot = jnp.sum(e, axis=1, keepdims=True)
        e_v[slot] = eb
        ol = dg(eb, v_v[pl.ds(al(q * T), T), lanes], NN)
        inv = 1.0 / tot
        inv = jnp.where(lo, inv[:R], inv[R:])
        li_v[rq, lanes] = inv
        a_v[rq, lanes] = (jnp.where(lo, ol[:R], ol[R:]) * inv).astype(bf16)

    def row_copies(q):
        own_r = pl.ds(al(q * R), R)
        return [
            pltpu.make_async_copy(v.at[own_r], h.at[own_r], rsem.at[i, q])
            for i, (v, h) in enumerate(((n2, n2_h), (a_v, a_h), (h_v, h_h), (li_v, li_h)))
        ]

    def sequence(q, _):
        @pl.when(q == 1)
        def _():
            far(1)
            onward(2)

        @pl.when(q == 2)
        def _():
            near(2)
            far(2)

        s_v[0] = scores(q * pairs)

        def two(h, _):
            t = q * pairs + 2 * h

            @pl.when(t >= 2)
            def _():
                e_copy(t - 2, 0).wait()
                e_copy(t - 1, 1).wait()

            s_v[1] = scores(t + 1)
            weigh(t, 0)
            s_v[0] = scores(q * pairs + lax.rem(2 * h + 2, pairs))
            weigh(t + 1, 1)
            e_copy(t, 0).start()
            e_copy(t + 1, 1).start()
            return 0

        lax.fori_loop(0, pairs // 2, two, 0)
        own_r = pl.ds(al(q * R), R)
        h = x_v[own_r, :].astype(f32) + dg(a_v[own_r, :], wo[...], NN) + b_out
        h_v[own_r, :] = h
        zn, _r = row_norm(h)
        n2[own_r, :] = (zn * gain2 + shift2).astype(bf16)
        for o in row_copies(q):
            o.start()
        return 0

    lax.fori_loop(0, C, sequence, 0)
    e_copy(C * pairs - 2, 0).wait()
    e_copy(C * pairs - 1, 1).wait()
    for q in range(C):
        for i, (v, h) in enumerate(((n1, n1_h), (k_v, k_h), (v_v, v_h))):
            pltpu.make_async_copy(
                v.at[pl.ds(q * T, T)], h.at[pl.ds(q * T, T)], osem.at[3 + 3 * q + i]
            ).wait()
        for c in own[q] + rel[q]:
            c.wait_send()
    for j in range(J):
        gu_copy(j).wait()
    qc.wait()
    for q in range(C):
        for o in row_copies(q):
            o.wait()


def attend(C, R, D, S, FF, x, cot, lengths, vecs, wq, wk, wv, wd, wo):
    N, T, pairs = C * R, R * S, D // 128
    sd = jax.ShapeDtypeStruct
    dma = pltpu.SemaphoreType.DMA
    return pl.pallas_call(
        functools.partial(attend_kernel, C, R, D, S),
        out_shape=(
            sd((C * T, D), bf16),
            sd((N, D), bf16),
            sd((C * T, D), bf16),
            sd((C * T, D), bf16),
            sd((N, D), bf16),
            sd((N, D), f32),
            sd((C * pairs, 2 * R, T), bf16),
            sd((FF // D * N, D), bf16),
            sd((N, D), f32),
            sd((N, D), bf16),
        ),
        in_specs=[ANY, ANY, SM] + [VM] * 7 + [ANY] * 5,
        out_specs=(ANY,) * 10,
        scratch_shapes=[
            pltpu.VMEM((N, D), bf16),
            pltpu.VMEM((C * T, D), bf16),
            pltpu.VMEM((D, D), bf16),
            pltpu.VMEM((D, D), bf16),
            pltpu.VMEM((D, D), bf16),
            pltpu.VMEM((N, D), bf16),
            pltpu.VMEM((C * T, D), bf16),
            pltpu.VMEM((C * T, D), bf16),
            pltpu.VMEM((N, D), bf16),
            pltpu.VMEM((N, D), f32),
            pltpu.VMEM((2, 2 * R, T), bf16),
            pltpu.VMEM((2, 2 * R, T), f32),
            pltpu.VMEM((N, D), bf16),
            pltpu.VMEM((FF, D), bf16),
            pltpu.VMEM((FF // D * N, D), bf16),
            pltpu.VMEM((D, D), bf16),
            pltpu.VMEM((N, D), f32),
            pltpu.VMEM((N, D), bf16),
            dma((C + 6,)),
            dma((5 + 3 * C,)),
            dma((2,)),
            dma((FF // D,)),
            dma((4, C)),
            dma((4, C)),
            dma((4, C)),
            dma((2, C)),
            dma((2, C)),
        ],
        compiler_params=pltpu.CompilerParams(
            collective_id=1, has_side_effects=True, vmem_limit_bytes=60 * 2**20
        ),
        cost_estimate=pl.CostEstimate(
            flops=20 * 10**9, bytes_accessed=40 * 10**6, transcendentals=0
        ),
    )(x, cot, lengths, *vecs, wq, wk, wv, wd, wo)


SCHEDULE = {
    "f10": ((1, 4),),
    "f12": ((2, 0),),
    "u1": ((2, 4),),
    "f22": ((2, 1), (1, 5),),
    "f30": ((3, 0),),
    "f31": ((2, 5),),
    "u3": ((2, 2), (1, 6),),
    "s1": ((3, 1), (2, 6),),
    "wo": ((2, 3), (4, 0), (1, 7),),
    "t1": ((3, 2),),
    "t2": ((2, 7),),
    "d01": ((3, 3), (4, 1),),
    "d02": ((5, 0),),
    "t6": ((6, 0),),
    "t8": ((10, 3), (10, 1), (1, 8), (10, 2), (4, 2), (10, 0), (3, 4), (3, 5), (5, 1),),
    "t10": ((2, 8),),
    "d10": ((3, 6),),
    "d12": ((4, 3), (3, 7), (7, 0),),
    "t12": ((5, 2), (4, 4), (6, 1),),
    "t17": ((5, 3),),
    "k": ((1, 9),),
    "v": ((2, 9), (8, 0), (1, 10), (3, 8), (5, 4),),
    "d20": ((4, 6), (1, 11), (2, 10), (4, 5), (2, 11),),
    "d21": ((5, 6), (4, 7), (3, 9),),
    "o0": ((6, 2), (5, 5), (4, 8), (3, 10), (4, 9), (3, 11),),
    "o1": ((5, 7), (7, 1), (4, 10), (7, 2), (4, 11),),
    "o2": ((5, 10), (5, 8), (5, 9),),
    "end0": ((5, 11), (8, 1),),
    "end1": ((8, 2),),
}


def backward_kernel(
    C, R, D, S, FF,
    x_h, cot_h, a_h, li_h, q_h, k_h, v_h, n1_h, e_h, gu_h, h_h, n2_h,
    g1_r, s1_r, g2_r, bd_r, bu_r, wo_h, wu_h, wd_h, wq_h, wk_h, wv_h,
    out_h, ig_h, f_h, sm_h, p_h,
    cot, a_v, q_v, n2, du, h_v, acc, dn2, kk, vv, n1, wk, wv, wo, gb, dn, e_v, sm,
    rc, r2, r3, s3, r4, f, d1, d2, mc, mz, mx, bup,
    lsem, esem, osem, psem, tsem, trem, sems, rems, zs, zr, ds_s, ds_r, ms, mr, cr,
):
    T, N = R * S, C * R
    pairs = D // 128
    J = FF // D
    B = 8
    CH = D // B
    s, b, px, py, pd = places()
    y, x = s // 2, s % 2
    z, c = b // 2, b % 2
    sib = z * 2 + 1 - c
    t_rows = C * T
    HC, HR = CH // 2, R // 2
    U = 2 * J + 4
    bar = pltpu.get_barrier_semaphore()
    beside = [(px, b), (py, b), (s, sib)] + [(s, (z + k) % 4 * 2 + c) for k in (1, 2, 3)]
    for o in beside:
        pl.semaphore_signal(bar, 1, device_id=o, device_id_type=MESH)

    def remote(src, dst, ss, rs, dev):
        return pltpu.make_async_remote_copy(
            src, dst, ss, rs, device_id=dev, device_id_type=MESH
        )

    def axis(u):
        return (u - J) // (J // 2) if J <= u < 2 * J else u % 2

    def down(u):
        return isinstance(u, int) and J <= u < 2 * J

    def rslot(u):
        if not isinstance(u, int) or u < J:
            return u
        return J if u < 2 * J else u - 2 * J

    def slot(u):
        return u - 2 * J * (u // (2 * J))

    def mine(u):
        return (x, y)[axis(u)]

    def first_peer(u):
        return (px, py)[axis(u)]

    def last_peer(u):
        return (py, px)[axis(u)]

    def half(h):
        return pl.ds(al(h * HC), HC)

    def cp1(u):
        part = gb.at[pl.ds(J, J), u - J, 1 - c] if down(u) else gb.at[slot(u), :, 1 - c]
        return remote(part, rc.at[rslot(u)], sems.at[0, u], rems.at[0, u], (s, sib))

    def tile_copies(j):
        ux, uy = pl.ds(J, J // 2), pl.ds(J + J // 2, J // 2)
        return (
            remote(
                gb.at[ux, j, c, half(1 - x)], r2.at[ux, j], sems.at[1, J + j], rems.at[1, J + j],
                (px, b),
            ),
            remote(gb.at[uy, j, c, half(1 - y)], r2.at[uy, j], tsem.at[j], trem.at[j], (py, b)),
        )

    def tile2(j):
        cp1(J + j).wait_recv()
        gb[J : 2 * J, j, c] += rc[rslot(J + j)]
        if j < J - 1:
            pl.semaphore_signal(cr.at[rslot(J + j)], 1, device_id=(s, sib), device_id_type=MESH)
        for o in tile_copies(j):
            o.start()

    def tile3(j):
        for o in tile_copies(j):
            o.wait_recv()
        mid = J + J // 2
        gb[J:mid, j, c, half(x)] += r2[J:mid, j]
        gb[mid : 2 * J, j, c, half(y)] += r2[mid : 2 * J, j]

    def cp2(u):
        return remote(
            gb.at[slot(u), :, c, half(1 - mine(u))], r2.at[slot(u)], sems.at[1, u], rems.at[1, u],
            (first_peer(u), b),
        )

    def cp3(u, k):
        zz = (z + k) % 4
        return remote(
            gb.at[slot(u), zz, c, half(mine(u))], r3.at[u, k - 1], zs.at[k - 1, u], zr.at[k - 1, u],
            (s, zz * 2 + c),
        )

    def cp4(u):
        return remote(s3.at[u % 4], r4.at[u], sems.at[2, u], rems.at[2, u], (last_peer(u), b))

    def cp5(u):
        ref = f.at[u, half(mine(u))]
        return remote(ref, ref, sems.at[3, u], rems.at[3, u], (first_peer(u), b))

    def sent(u):
        cp1(u).wait_send()
        for o in tile_copies(u - J) if down(u) else (cp2(u),):
            o.wait_send()
        for k in (1, 2, 3):
            cp3(u, k).wait_send()

    def step1(u, again):
        if again:
            pl.semaphore_wait(cr.at[rslot(u)], 1)
        cp1(u).start()

    def step2(u, more):
        cp1(u).wait_recv()
        gb[slot(u), :, c] += rc[rslot(u)]
        if more:
            pl.semaphore_signal(cr.at[rslot(u)], 1, device_id=(s, sib), device_id_type=MESH)
        cp2(u).start()

    def step3(u):
        if not down(u):
            cp2(u).wait_recv()
            gb[slot(u), :, c, half(mine(u))] += r2[slot(u)]
        for k in (1, 2, 3):
            cp3(u, k).start()

    def step4(u):
        for k in (1, 2, 3):
            cp3(u, k).wait_recv()
        if isinstance(u, int):
            if u >= 4:
                cp4(u - 4).wait_send()
        else:

            @pl.when(u >= 4)
            def _():
                cp4(u - 4).wait_send()

        v = gb[slot(u), z, c, half(mine(u))].astype(f32)
        for k in range(3):
            v += r3[u, k].astype(f32)
        s3[u % 4] = v.astype(bf16)
        cp4(u).start()

    def step5(u):
        cp4(u).wait_recv()
        f[u, half(mine(u))] = s3[u % 4] + r4[u]
        cp5(u).start()

    def dcp(q, i):
        sl = q % 2
        if i == 0:
            a, o, dev = dn.at[sl, :, 1 - x, pl.ds(0, HR)], d1.at[sl, 0], px
        elif i == 1:
            a, o, dev = dn.at[sl, 1 - y, :, pl.ds(HR, HR)], d1.at[sl, 1], py
        elif i == 2:
            a, o, dev = dn.at[sl, 1 - y, x, pl.ds(0, HR)], d2.at[sl, 0], py
        else:
            a, o, dev = dn.at[sl, y, 1 - x, pl.ds(HR, HR)], d2.at[sl, 1], px
        return remote(a, o, ds_s.at[i, q], ds_r.at[i, q], (dev, b))

    def rows1(q):
        dcp(q, 0).start()
        dcp(q, 1).start()

    def rows2(q):
        sl = q % 2
        dcp(q, 0).wait_recv()
        dcp(q, 1).wait_recv()
        dn[sl, :, x, 0:HR] += d1[sl, 0]
        dn[sl, y, :, HR:R] += d1[sl, 1]
        dcp(q, 2).start()
        dcp(q, 3).start()

    def rows3(q):
        sl = q % 2
        dcp(q, 2).wait_recv()
        dcp(q, 3).wait_recv()
        for i in range(2):
            d = dn[sl, y, x, i * HR : (i + 1) * HR].astype(f32) + d2[sl, i].astype(f32)
            r = pl.ds(al(q * R + i * HR), HR)
            zz, rr = row_norm(n2[r, :].astype(f32))
            g = d * gain1
            du[r, :] = (
                h_v[r, :]
                + rr
                * (
                    g
                    - jnp.mean(g, axis=-1, keepdims=True)
                    - zz * jnp.mean(g * zz, axis=-1, keepdims=True)
                )
            ).astype(bf16)


    def emit(name):
        for k, u in SCHEDULE.get(name, ()):
            if k == 1:
                step1(u, u > J)
            elif k == 2 and down(u):
                tile2(u - J)
            elif k == 2:
                if u >= 2 * J:
                    if u == 2 * J:
                        cp5(0).wait_recv()
                    step2(u, False)
                else:
                    step2(u, True)
            else:
                {3: step3, 4: step4, 5: step5, 6: rows1, 7: rows2, 8: rows3, 10: tile3}[k](u)

    def emit_when(names):
        for name, cond in names:
            if name in SCHEDULE:
                pl.when(cond)(functools.partial(emit, name))

    def weight(u, left, right):
        def part(i, _):
            lanes = pl.ds(al(i * (D // 2), 128), D // 2)
            gb[slot(u), pl.ds(2 * i, 2)] = (
                dg(left[:, lanes], right[...], TN).astype(bf16).reshape(2, 2, CH, D)
            )
            return 0

        lax.fori_loop(0, 2, part, 0)

    def load(i, h, v):
        cp = pltpu.make_async_copy(h, v, lsem.at[i])
        cp.start()
        return cp

    def tile(j):
        return (
            load(4 + 2 * j, wu_h.at[:, pl.ds(j * D, D)], vv.at[pl.ds(j * D, D)]),
            load(5 + 2 * j, gu_h.at[pl.ds(j * N, N)], kk.at[pl.ds(j * N, N)]),
        )

    c_n2 = load(0, n2_h, n2)
    c_w = [tile(0)]
    c_cot = load(1, cot_h, cot)

    def e_copy(t, slot):
        return pltpu.make_async_copy(e_h.at[t], e_v.at[slot], esem.at[slot])


    gain1, shift1, gain2, b_down = (row(r) for r in (g1_r, s1_r, g2_r, bd_r))
    for j in range(J):
        bup[j : j + 1, :] = bu_r[j * D : (j + 1) * D].astype(f32).reshape(1, D)
    sm[...] = jnp.zeros_like(sm)
    dn2[...] = jnp.zeros_like(dn2)
    c_n2.wait()
    c_w += [tile(j) for j in range(1, J)]
    n0 = 4 + 2 * J
    c_a = load(0, a_h, a_v)
    c_wo = load(2, wo_h, wo)
    c_h = load(3, h_h, h_v)
    c_q = load(n0, q_h, q_v)
    c_n1 = load(n0 + 1, n1_h, n1)
    c_wk = load(n0 + 2, wk_h, wk)
    c_wv = load(n0 + 3, wv_h, wv)
    e_copy(0, 0).start()
    e_copy(1, 1).start()
    pl.semaphore_wait(bar, len(beside))
    c_cot.wait()

    def p_copy(j):
        return pltpu.make_async_copy(
            kk.at[pl.ds(al(j * N), N)], p_h.at[pl.ds(al(j * N), N)], psem.at[j]
        )

    def ffn(j, _):
        jr = pl.ds(al(j * D), D)
        for jj in range(J):

            @pl.when(j == jj)
            def _():
                c_w[jj][0].wait()
                c_w[jj][1].wait()

        bias = bup[pl.ds(j, 1), :]

        def chunk(i, sums):
            emit_when(
                (f"f{jj}{ii}", (j == jj) & (i == ii)) for jj in range(J) for ii in range(C)
            )
            r = pl.ds(al(i * R), R)
            u = dg(n2[r, :], vv[jr, :], NN) + bias
            rj = pl.ds(al(j * N + i * R), R)
            g = kk[rj, :].astype(f32)
            u2 = u * u
            t = jnp.tanh(u * (GC0 + GC1 * u2))
            hu = 0.5 * u
            half = 0.5 + 0.5 * t
            p = (u * half).astype(bf16)
            d = (g * (half + hu * (1.0 - t * t) * (GC0 + 3.0 * GC1 * u2))).astype(bf16)
            kk[rj, :] = p
            du[r, :] = d
            dn2[r, :] += dg(d, vv[jr, :], NT)
            return sums + jnp.sum(d.astype(f32), axis=0, keepdims=True)

        dj = lax.fori_loop(0, C, chunk, jnp.zeros((1, D), f32))
        sm[pl.ds(8 + j, 1), :] = dj
        emit_when((f"u{jj}", j == jj) for jj in range(J))
        weight(j, n2, du)
        step1(j, False)
        emit_when((f"w{jj}", j == jj) for jj in range(J))
        per = FF // B
        pt = kk.at[pl.ds(al(j * N), N)]

        def rows_of(bb, _):
            gw = dg(pt[:, pl.ds(al(bb * per, 128), per)], cot[...], TN).astype(bf16)
            for i in range(per // CH):
                gb[J + i, j, bb] = gw[i * CH : (i + 1) * CH, :]
            return 0

        lax.fori_loop(0, D // per, rows_of, 0)
        p_copy(j).start()
        return 0

    lax.fori_loop(0, J, ffn, 0)

    c_v = load(1, v_h, vv.at[pl.ds(0, t_rows)])

    for w in (c_a, c_wo, c_h):
        w.wait()


    c_k = pltpu.make_async_copy(k_h, kk.at[pl.ds(0, t_rows)], lsem.at[0])

    def second(i, _):
        emit_when((f"s{ii}", i == ii) for ii in range(C))

        @pl.when(i == 1)
        def _():
            for j in range(J):
                p_copy(j).wait()
            c_k.start()

        r = pl.ds(al(i * R), R)
        acc[r, :] = h_v[r, :] + b_down
        sm[7:8, :] += jnp.sum(cot[r, :].astype(f32), axis=0, keepdims=True)
        zn, rr = row_norm(h_v[r, :])
        dnn = dn2[r, :]
        g = dnn * gain2
        sm[5:6, :] += jnp.sum(dnn * zn, axis=0, keepdims=True)
        sm[6:7, :] += jnp.sum(dnn, axis=0, keepdims=True)
        dh = cot[r, :].astype(f32) + rr * (
            g
            - jnp.mean(g, axis=-1, keepdims=True)
            - zn * jnp.mean(g * zn, axis=-1, keepdims=True)
        )
        h_v[r, :] = dh
        db = dh.astype(bf16)
        n2[r, :] = db
        sm[4:5, :] += jnp.sum(db.astype(f32), axis=0, keepdims=True)
        du[r, :] = dg(db, wo[...], NT).astype(bf16)
        return 0

    lax.fori_loop(0, C, second, 0)
    c_li = load(2, li_h, dn2)
    emit("wo")
    sent(0)
    c_wq = load(3, wq_h, wo)
    weight(2 * J, a_v, n2)

    c_x = load(4, x_h, n2)
    emit("kw")
    for w in (c_x, c_k, c_v, c_li, c_q, c_wk, c_wv, c_wq, c_n1):
        w.wait()
    dq_v, do_v = cot, du
    lane = lax.broadcasted_iota(jnp.int32, (1, 128), 1)
    lo = lane < 64

    def stack(v):
        zero = jnp.zeros_like(v)
        return jnp.concatenate([jnp.where(lo, v, zero), jnp.where(lo, zero, v)], 0)

    def row_parts(q):
        rq = pl.ds(al(q * R), R)

        def put(blk, more):
            rr = pl.ds(al((q * S + blk) * R), R)
            d = dg(kk[rr, :], wk[...], NT) + dg(vv[rr, :], wv[...], NT)
            if more:
                d += dg(dq_v[rq, :], wo[...], NT)
            n = n1[rr, :].astype(f32)
            sm[0:1, :] += jnp.sum(d * n, axis=0, keepdims=True)
            sm[1:2, :] += jnp.sum(d, axis=0, keepdims=True)
            dn[q % 2, blk // 2, blk % 2] = d.astype(bf16)

        def others(i, _):
            emit_when(
                (f"d{qq}{ii}", (q == qq) & (i == ii))
                for qq in range(C)
                for ii in range(S - 1)
                if qq + 1 < C or ii > 0
            )
            put((s + 1 + i) % S, False)
            return 0

        lax.fori_loop(0, S - 1, others, 0)
        emit_when((f"d{qq}{S - 1}", q == qq) for qq in range(C))
        put(s, True)

    def pair(t, _):
        q, p = t // pairs, t % pairs
        slot = t % 2
        emit_when((f"t{tt}", t == tt) for tt in range(C * pairs))
        lanes = pl.ds(al(p * 128, 128), 128)
        rq = pl.ds(al(q * R), R)
        rk = pl.ds(al(q * T), T)
        qs = stack(q_v[rq, lanes])
        dof = do_v[rq, lanes].astype(f32) * dn2[rq, lanes]
        dos = stack(dof.astype(bf16))
        dl = jnp.sum(stack(dof * a_v[rq, lanes].astype(f32)), axis=1, keepdims=True)
        e_copy(t, slot).wait()
        dp = dg(dos, vv[rk, lanes], NT)
        vv[rk, lanes] = dg(dos, e_v[slot], TN).astype(bf16).T
        ds = (e_v[slot].astype(f32) * (dp - dl)).astype(bf16)
        dks = (dg(qs, ds, TN) * (1.0 / LOG2E)).astype(bf16).T
        dqs = dg(ds, kk[rk, lanes], NN)
        kk[rk, lanes] = dks
        dq_v[rq, lanes] = (jnp.where(lo, dqs[:R], dqs[R:]) * (HEAD_DIM ** (-0.5))).astype(
            bf16
        )

        @pl.when(t + 2 < C * pairs)
        def _():
            e_copy(t + 2, slot).start()

        @pl.when((p == pairs - 1) & (q < C - 1))
        def _():
            row_parts(q)

        return 0

    lax.fori_loop(0, C * pairs, pair, 0)
    emit("q")
    for u in (1, 2, 3):
        sent(u)
        cp5(u).wait_recv()
    for i in range(C):
        r = pl.ds(i * R, R)
        a_v[r, :] = n1[pl.ds(al((i * S + s) * R), R), :]
    q_u, k_u, v_u = 2 * J + 1, 2 * J + 2, 2 * J + 3
    weight(q_u, a_v, dq_v)
    def mcp(i, src, dst, dev):
        return remote(src, dst, ms.at[i], mr.at[i], dev)

    emit("k")
    weight(k_u, n1, kk.at[pl.ds(0, t_rows)])
    h_rows, h_p = J // 2 * D, J // 2 * N
    c_w0 = load(0, wd_h.at[pl.ds(0, h_rows)], kk.at[pl.ds(0, h_rows)])
    emit("v")
    weight(v_u, n1, vv.at[pl.ds(0, t_rows)])
    c_p0 = load(1, p_h.at[pl.ds(0, h_p)], n1.at[pl.ds(0, h_p)])
    emit("d20")
    for i in range(4):
        dcp(0, i).wait_send()
    row_parts(C - 1)
    sm[2:3, :] = jnp.sum(dq_v[...].astype(f32), axis=0, keepdims=True)
    sm[3:4, :] = jnp.sum(vv[0:t_rows, :].astype(f32), axis=0, keepdims=True)
    sm[0:1, :] = (sm[0:1, :] - shift1 * sm[1:2, :]) / gain1

    m1 = mcp(0, sm, mc.at[0], (s, sib))
    m1.start()
    c_w1 = load(2, wd_h.at[pl.ds(h_rows, h_rows)], kk.at[pl.ds(h_rows, h_rows)])
    c_p1 = load(3, p_h.at[pl.ds(h_p, h_p)], n1.at[pl.ds(h_p, h_p)])

    def last(i):
        r = pl.ds(al(i * R), R)
        o = acc[r, :]
        for j in range(J):
            o += dg(n1[pl.ds(al(j * N + i * R), R), :], kk[j * D : (j + 1) * D, :], NN)
        q_v[r, :] = o.astype(bf16)

    emit("o0")
    for w in (c_w0, c_p0, c_w1, c_p1):
        w.wait()
    last(0)
    m1.wait()
    mz[0] = sm[...] + mc[0]
    m2 = [mcp(k, mz.at[0], mz.at[k], (s, (z + k) % 4 * 2 + c)) for k in (1, 2, 3)]
    for m in m2:
        m.start()
    emit("o1")
    last(1)
    for m in m2:
        m.wait()
    mx[0] = (mz[0] + mz[1]) + (mz[2] + mz[3])
    m3 = mcp(4, mx.at[0], mx.at[1], (px, b))
    m3.start()
    emit("o2")
    last(2)
    c_o = pltpu.make_async_copy(q_v, out_h, osem.at[0])
    c_o.start()
    m3.wait()
    mx[2] = mx[0] + mx[1]
    m4 = mcp(5, mx.at[2], mx.at[3], (py, b))
    m4.start()
    emit("end0")
    m4.wait()
    sm[...] = mx[2] + mx[3]
    c_s = pltpu.make_async_copy(sm, sm_h, osem.at[2])
    c_s.start()
    emit("end1")
    c_i = pltpu.make_async_copy(du, ig_h, osem.at[1])
    c_i.start()
    emit("end2")
    for u in range(U):
        if u > 3:
            cp5(u).wait_recv()
    c_f = pltpu.make_async_copy(f, f_h, osem.at[3])
    c_f.start()
    for u in range(U):
        if u > 3:
            sent(u)
        if u >= 2 * J:
            cp4(u).wait_send()
        cp5(u).wait_send()
    for q in (1, 2):
        for i in range(4):
            dcp(q, i).wait_send()
    for o in (c_o, c_i, c_s, c_f):
        o.wait()


def backward(C, R, D, S, FF, x, cot, a, li, q, k, v, n1, e, gu, h, n2, vecs, wo, wu, wd, wq, wk, wv):
    N, T = C * R, R * S
    J = FF // D
    U, CH = 2 * J + 4, D // 8
    sd = jax.ShapeDtypeStruct
    dma = pltpu.SemaphoreType.DMA
    vm = pltpu.VMEM
    return pl.pallas_call(
        functools.partial(backward_kernel, C, R, D, S, FF),
        out_shape=(
            sd((N, D), bf16),
            sd((N, D), bf16),
            sd((U, D // 8, D), bf16),
            sd((16, D), f32),
            sd((J * N, D), bf16),
        ),
        in_specs=[ANY] * 12 + [VM] * 5 + [ANY] * 6,
        out_specs=(ANY,) * 5,
        scratch_shapes=[
            vm((N, D), bf16), vm((N, D), bf16), vm((N, D), bf16),
            vm((N, D), bf16), vm((N, D), bf16),
            vm((N, D), f32), vm((N, D), f32), vm((N, D), f32),
            vm((FF, D), bf16), vm((FF, D), bf16), vm((C * T, D), bf16),
            vm((D, D), bf16), vm((D, D), bf16), vm((D, D), bf16),
            vm((2 * J, 4, 2, CH, D), bf16), vm((2, 2, 2, R, D), bf16),
            vm((2, 2 * R, T), bf16), vm((16, D), f32),
            vm((5, 4, CH, D), bf16), vm((2 * J, 4, CH // 2, D), bf16), vm((U, 3, CH // 2, D), bf16),
            vm((4, CH // 2, D), bf16), vm((U, CH // 2, D), bf16), vm((U, CH, D), bf16),
            vm((2, 2, 2, R // 2, D), bf16), vm((2, 2, R // 2, D), bf16),
            vm((1, 16, D), f32), vm((4, 16, D), f32), vm((4, 16, D), f32), vm((J, D), f32),
            dma((4 + 2 * J + 4,)), dma((2,)), dma((4,)), dma((J,)), dma((J,)), dma((J,)),
            dma((4, U)), dma((4, U)), dma((3, U)), dma((3, U)),
            dma((4, C)), dma((4, C)), dma((6,)), dma((6,)),
            pltpu.SemaphoreType.REGULAR((5,)),
        ],
        compiler_params=pltpu.CompilerParams(
            collective_id=2, has_side_effects=True, vmem_limit_bytes=(64 * 2**20) - 2**17
        ),
        cost_estimate=pl.CostEstimate(
            flops=40 * 10**9, bytes_accessed=60 * 10**6, transcendentals=0
        ),
    )(x, cot, a, li, q, k, v, n1, e, gu, h, n2, *vecs, wo, wu, wd, wq, wk, wv)


def finish_kernel(D, FF, f_h, sm, out_h, ig_h, *rest):
    (
        o_out, o_ig, g1, s1, wq_o, bq, wk_o, wv_o, bv, wo_o, bo, g2, s2, wu_o, bu, wd_o, bd,
        f, v_out, v_ig, up, low, sq, sem, osem,
    ) = rest
    J, CH = FF // D, D // 8
    parts = [
        pltpu.make_async_copy(f_h.at[pl.ds(i * J, J)], f.at[pl.ds(i * J, J)], sem.at[i])
        for i in range(3)
    ]
    c2 = pltpu.make_async_copy(out_h, v_out, sem.at[3])
    c3 = pltpu.make_async_copy(ig_h, v_ig, sem.at[4])
    for c in (*parts, c2, c3):
        c.start()
    started = []

    def write(v, o):
        started.append(pltpu.make_async_copy(v, o, osem.at[len(started)]))
        started[-1].start()

    b = lax.axis_index("batch")
    rolled = pltpu.roll(sm[0:8, :], (8 - b) % 8 * CH, 1)
    for i, o in enumerate((g1, s1, bq, bv, bo, g2, s2, bd)):
        o[...] = rolled[i, :CH]
    per = FF // 8
    half = D // per
    ub = sm[8 : 8 + J, :]
    here = lax.broadcasted_iota(jnp.int32, (J, 1), 0) == b // half
    ub = jnp.sum(jnp.where(here, ub, 0.0), axis=0, keepdims=True)
    ub = jnp.where(b % half == 0, ub[:, :per], ub[:, per:])
    bu[...] = ub[0]
    parts[0].wait()
    for j in range(J):
        up[:, j * D : (j + 1) * D] = f[j].astype(f32)
    write(up, wu_o)
    parts[1].wait()
    for j in range(J):
        low[j * CH : (j + 1) * CH, :] = f[J + j].astype(f32)
    write(low, wd_o)
    parts[2].wait()
    for i, o in enumerate((wo_o, wq_o, wk_o, wv_o)):
        sq[i] = f[2 * J + i].astype(f32)
        write(sq.at[i], o)
    c2.wait()
    write(v_out, o_out)
    c3.wait()
    write(v_ig, o_ig)
    for c in started:
        c.wait()


def finish(D, FF, f, sm, out, ig):
    sd = jax.ShapeDtypeStruct
    CH = D // 8
    row, mat = sd((CH,), f32), sd((CH, D), f32)
    return pl.pallas_call(
        functools.partial(finish_kernel, D, FF),
        out_shape=(
            sd(out.shape, bf16), sd(ig.shape, bf16), row, row, mat, row, mat, mat, row, mat,
            row, row, row, sd((CH, FF), f32), sd((FF // 8,), f32), sd((FF // 8, D), f32), row,
        ),
        in_specs=[ANY, VM, ANY, ANY],
        out_specs=(ANY, ANY, VM, VM, ANY, VM, ANY, ANY, VM, ANY, VM, VM, VM, ANY, VM, ANY, VM),
        scratch_shapes=[pltpu.VMEM(v.shape, bf16) for v in (f, out, ig)]
        + [pltpu.VMEM((CH, FF), f32), pltpu.VMEM((FF // 8, D), f32), pltpu.VMEM((4, CH, D), f32)]
        + [pltpu.SemaphoreType.DMA((5,)), pltpu.SemaphoreType.DMA((8,))],
        compiler_params=pltpu.CompilerParams(vmem_limit_bytes=62 * 2**20),
    )(f, sm, out, ig)


def fast_body(
    inputs, lengths, gain_one, shift_one, w_query, b_query, w_key, w_value, b_value, w_out, b_out,
    gain_two, shift_two, w_up, b_up, w_down, b_down, cotangent,
):
    C, R, D = inputs.shape
    S = lax.axis_size("seq")
    FF = w_up.shape[1]
    N = C * R
    x = inputs.reshape(N, D)
    cot = cotangent.reshape(N, D)
    n1, q, k, v, a, li, e, gu, h, n2 = attend(
        C, R, D, S, FF, x, cot, lengths,
        (gain_one, shift_one, b_query, b_value, b_out, gain_two, shift_two),
        w_query, w_key, w_value, w_down, w_out,
    )
    out, input_grad, g, sm, _ = backward(
        C, R, D, S, FF, x, cot, a, li, q, k, v, n1, e, gu, h, n2,
        (gain_one, shift_one, gain_two, b_down, b_up),
        w_out, w_up, w_down, w_query, w_key, w_value,
    )
    out, input_grad, *grads = finish(D, FF, g, sm, out, input_grad)
    return (out.reshape(inputs.shape), input_grad.reshape(inputs.shape), *grads)


def from_behind(x, axis, by):
    length = lax.axis_size(axis)
    return lax.ppermute(x, axis, [(i, (i + by) % length) for i in range(length)])


def normed(values, gain, offset):
    average = jnp.mean(values, axis=-1, keepdims=True)
    centred = values - average
    spread = jnp.mean(centred * centred, axis=-1, keepdims=True)
    return centred * lax.rsqrt(spread + norm_eps) * gain + offset


def outer_sum(left, right):
    return lax.dot_general(
        left, right, (((0,), (0,)), ((), ())), preferred_element_type=jnp.float32
    )


def back_dot(grad_rows, weight):
    return lax.dot_general(
        grad_rows, weight, (((1,), (1,)), ((), ())), preferred_element_type=jnp.float32
    )


def front_dot(rows_low, weight, bias):
    return jnp.dot(rows_low, weight, preferred_element_type=jnp.float32) + bias.astype(jnp.float32)


def column_sums(values):
    return jnp.sum(values.astype(jnp.float32), axis=0)


def key_valid(lengths, source, block_rows):
    positions = source * block_rows + jnp.arange(block_rows, dtype=jnp.int32)
    return (positions[None, :] < lengths[:, None])[:, None, None, :]


def block_scores(queries, key_block, valid):
    scores = jnp.einsum(
        "srhd,sthd->srht", queries, key_block, preferred_element_type=jnp.float32
    ) * HEAD_DIM ** (-0.5)
    return jnp.where(valid, scores, masked_score)


def ring_body(
    inputs,
    lengths,
    gain_one,
    shift_one,
    w_query,
    b_query,
    w_key,
    w_value,
    b_value,
    w_out,
    b_out,
    gain_two,
    shift_two,
    w_up,
    b_up,
    w_down,
    b_down,
    cotangent,
):
    cycle_size = lax.axis_size("seq")
    position = lax.axis_index("seq")
    count, block_rows, width = inputs.shape
    heads = width // HEAD_DIM
    total_rows = count * block_rows
    split_shape = (count, block_rows, heads, HEAD_DIM)
    scale = HEAD_DIM ** (-0.5)
    rows_in = inputs.astype(jnp.float32).reshape(total_rows, width)
    first_full, norm_one_pull = jax.vjp(
        normed, rows_in, gain_one.astype(jnp.float32), shift_one.astype(jnp.float32)
    )
    first = first_full.astype(jnp.bfloat16)
    queries = front_dot(first, w_query, b_query).astype(jnp.bfloat16).reshape(split_shape)
    key_rows = jnp.dot(first, w_key, preferred_element_type=jnp.float32).astype(jnp.bfloat16)
    value_rows = front_dot(first, w_value, b_value).astype(jnp.bfloat16)
    own_block = jnp.stack((key_rows, value_rows)).reshape((2,) + split_shape)
    running_max = jnp.full((count, block_rows, heads), masked_score, jnp.float32)
    running_total = jnp.zeros((count, block_rows, heads), jnp.float32)
    running_sum = jnp.zeros(split_shape, jnp.float32)
    moving = own_block
    for rotation in range(cycle_size):
        source = (position - rotation) % cycle_size
        valid = key_valid(lengths, source, block_rows)
        scores = block_scores(queries, moving[0], valid)
        new_max = jnp.maximum(running_max, jnp.max(scores, axis=-1))
        decay = jnp.exp(running_max - new_max)
        weights_exp = jnp.where(valid, jnp.exp(scores - new_max[..., None]), 0.0)
        running_total = running_total * decay + jnp.sum(weights_exp, axis=-1)
        running_sum = running_sum * decay[..., None] + jnp.einsum(
            "srht,sthd->srhd",
            weights_exp.astype(jnp.bfloat16),
            moving[1],
            preferred_element_type=jnp.float32,
        )
        running_max = new_max
        if rotation + 1 < cycle_size:
            moving = from_behind(moving, "seq", 1)
    attended = running_sum / running_total[..., None]
    log_total = running_max + jnp.log(running_total)
    attended_low = attended.reshape(total_rows, width).astype(jnp.bfloat16)
    middle = rows_in + front_dot(attended_low, w_out, b_out)
    second_full, norm_two_pull = jax.vjp(
        normed, middle, gain_two.astype(jnp.float32), shift_two.astype(jnp.float32)
    )
    second = second_full.astype(jnp.bfloat16)
    hidden = front_dot(second, w_up, b_up)
    gelu_value, gelu_pull = jax.vjp(jax.nn.gelu, hidden)
    active = gelu_value.astype(jnp.bfloat16)
    outputs = middle + front_dot(active, w_down, b_down)
    grad_rows_out = cotangent.astype(jnp.float32).reshape(total_rows, width)
    grad_ffn = cotangent.reshape(total_rows, width)
    grad_w_down = outer_sum(active, grad_ffn)
    grad_b_down = column_sums(grad_ffn)
    grad_hidden = gelu_pull(back_dot(grad_ffn, w_down))[0].astype(jnp.bfloat16)
    grad_w_up = outer_sum(second, grad_hidden)
    grad_b_up = column_sums(grad_hidden)
    grad_middle_part, grad_gain_two, grad_shift_two = norm_two_pull(back_dot(grad_hidden, w_up))
    grad_middle = grad_rows_out + grad_middle_part
    grad_branch = grad_middle.astype(jnp.bfloat16)
    grad_w_out = outer_sum(attended_low, grad_branch)
    grad_b_out = column_sums(grad_branch)
    grad_attended = back_dot(grad_branch, w_out).astype(jnp.bfloat16).reshape(split_shape)
    row_delta = jnp.sum(grad_attended.astype(jnp.float32) * attended, axis=-1)
    grad_queries = jnp.zeros(split_shape, jnp.float32)
    carried = jnp.zeros((2,) + split_shape, jnp.float32)
    moving = own_block
    for rotation in range(cycle_size):
        source = (position - rotation) % cycle_size
        valid = key_valid(lengths, source, block_rows)
        scores = block_scores(queries, moving[0], valid)
        probs = jnp.where(valid, jnp.exp(scores - log_total[..., None]), 0.0)
        grad_probs = jnp.einsum(
            "srhd,sthd->srht", grad_attended, moving[1], preferred_element_type=jnp.float32
        )
        grad_scores = (probs * (grad_probs - row_delta[..., None])).astype(jnp.bfloat16)
        grad_queries = (
            grad_queries
            + jnp.einsum(
                "srht,sthd->srhd", grad_scores, moving[0], preferred_element_type=jnp.float32
            )
            * scale
        )
        grad_keys_part = (
            jnp.einsum("srht,srhd->sthd", grad_scores, queries, preferred_element_type=jnp.float32)
            * scale
        )
        grad_values_part = jnp.einsum(
            "srht,srhd->sthd",
            probs.astype(jnp.bfloat16),
            grad_attended,
            preferred_element_type=jnp.float32,
        )
        carried = from_behind(
            (carried + jnp.stack((grad_keys_part, grad_values_part))).astype(jnp.bfloat16), "seq", 1
        ).astype(jnp.float32)
        if rotation + 1 < cycle_size:
            moving = from_behind(moving, "seq", 1)
    grad_keys = carried[0].reshape(total_rows, width).astype(jnp.bfloat16)
    grad_values = carried[1].reshape(total_rows, width).astype(jnp.bfloat16)
    grad_query_rows = grad_queries.reshape(total_rows, width).astype(jnp.bfloat16)
    grad_w_query = outer_sum(first, grad_query_rows)
    grad_b_query = column_sums(grad_query_rows)
    grad_w_key = outer_sum(first, grad_keys)
    grad_w_value = outer_sum(first, grad_values)
    grad_b_value = column_sums(grad_values)
    grad_first = (
        back_dot(grad_query_rows, w_query)
        + back_dot(grad_keys, w_key)
        + back_dot(grad_values, w_value)
    )
    grad_rows_part, grad_gain_one, grad_shift_one = norm_one_pull(grad_first)
    input_grad = grad_middle + grad_rows_part
    scattered = (
        lax.psum_scatter(
            grad_gain_one.astype(jnp.bfloat16), "batch", scatter_dimension=0, tiled=True
        ).astype(jnp.float32),
        lax.psum_scatter(
            grad_shift_one.astype(jnp.bfloat16), "batch", scatter_dimension=0, tiled=True
        ).astype(jnp.float32),
        lax.psum_scatter(
            grad_w_query.astype(jnp.bfloat16), "batch", scatter_dimension=0, tiled=True
        ).astype(jnp.float32),
        lax.psum_scatter(
            grad_b_query.astype(jnp.bfloat16), "batch", scatter_dimension=0, tiled=True
        ).astype(jnp.float32),
        lax.psum_scatter(
            grad_w_key.astype(jnp.bfloat16), "batch", scatter_dimension=0, tiled=True
        ).astype(jnp.float32),
        lax.psum_scatter(
            grad_w_value.astype(jnp.bfloat16), "batch", scatter_dimension=0, tiled=True
        ).astype(jnp.float32),
        lax.psum_scatter(
            grad_b_value.astype(jnp.bfloat16), "batch", scatter_dimension=0, tiled=True
        ).astype(jnp.float32),
        lax.psum_scatter(
            grad_w_out.astype(jnp.bfloat16), "batch", scatter_dimension=0, tiled=True
        ).astype(jnp.float32),
        lax.psum_scatter(
            grad_b_out.astype(jnp.bfloat16), "batch", scatter_dimension=0, tiled=True
        ).astype(jnp.float32),
        lax.psum_scatter(
            grad_gain_two.astype(jnp.bfloat16), "batch", scatter_dimension=0, tiled=True
        ).astype(jnp.float32),
        lax.psum_scatter(
            grad_shift_two.astype(jnp.bfloat16), "batch", scatter_dimension=0, tiled=True
        ).astype(jnp.float32),
        lax.psum_scatter(
            grad_w_up.astype(jnp.bfloat16), "batch", scatter_dimension=0, tiled=True
        ).astype(jnp.float32),
        lax.psum_scatter(
            grad_b_up.astype(jnp.bfloat16), "batch", scatter_dimension=0, tiled=True
        ).astype(jnp.float32),
        lax.psum_scatter(
            grad_w_down.astype(jnp.bfloat16), "batch", scatter_dimension=0, tiled=True
        ).astype(jnp.float32),
        lax.psum_scatter(
            grad_b_down.astype(jnp.bfloat16), "batch", scatter_dimension=0, tiled=True
        ).astype(jnp.float32),
    )
    summed = (
        lax.psum(scattered[0].astype(jnp.bfloat16), "seq").astype(jnp.float32),
        lax.psum(scattered[1].astype(jnp.bfloat16), "seq").astype(jnp.float32),
        lax.psum(scattered[2].astype(jnp.bfloat16), "seq").astype(jnp.float32),
        lax.psum(scattered[3].astype(jnp.bfloat16), "seq").astype(jnp.float32),
        lax.psum(scattered[4].astype(jnp.bfloat16), "seq").astype(jnp.float32),
        lax.psum(scattered[5].astype(jnp.bfloat16), "seq").astype(jnp.float32),
        lax.psum(scattered[6].astype(jnp.bfloat16), "seq").astype(jnp.float32),
        lax.psum(scattered[7].astype(jnp.bfloat16), "seq").astype(jnp.float32),
        lax.psum(scattered[8].astype(jnp.bfloat16), "seq").astype(jnp.float32),
        lax.psum(scattered[9].astype(jnp.bfloat16), "seq").astype(jnp.float32),
        lax.psum(scattered[10].astype(jnp.bfloat16), "seq").astype(jnp.float32),
        lax.psum(scattered[11].astype(jnp.bfloat16), "seq").astype(jnp.float32),
        lax.psum(scattered[12].astype(jnp.bfloat16), "seq").astype(jnp.float32),
        lax.psum(scattered[13].astype(jnp.bfloat16), "seq").astype(jnp.float32),
        lax.psum(scattered[14].astype(jnp.bfloat16), "seq").astype(jnp.float32),
    )
    return (
        outputs.astype(jnp.bfloat16).reshape(inputs.shape),
        input_grad.astype(jnp.bfloat16).reshape(inputs.shape),
        summed[0],
        summed[1],
        summed[2],
        summed[3],
        summed[4],
        summed[5],
        summed[6],
        summed[7],
        summed[8],
        summed[9],
        summed[10],
        summed[11],
        summed[12],
        summed[13],
        summed[14],
    )


def solution(mesh):
    placed = (
        P("batch", "seq", None),
        P("batch"),
        P(),
        P(),
        P(),
        P(),
        P(),
        P(),
        P(),
        P(),
        P(),
        P(),
        P(),
        P(),
        P(),
        P(),
        P(),
        P("batch", "seq", None),
    )
    small = mesh.shape["seq"] == 4 and mesh.shape["batch"] == 8
    body = fast_body if small else ring_body
    return jax.shard_map(
        body,
        mesh=mesh,
        in_specs=placed,
        out_specs=(
            P("batch", "seq", None),
            P("batch", "seq", None),
            P("batch"),
            P("batch"),
            P("batch", None),
            P("batch"),
            P("batch", None),
            P("batch", None),
            P("batch"),
            P("batch", None),
            P("batch"),
            P("batch"),
            P("batch"),
            P("batch", None),
            P("batch"),
            P("batch", None),
            P("batch"),
        ),
        check_vma=False,
    )
```
